128 devices in a mesh: dp: 16 (over y_hi, z, core), ctx: 8 (over x, y_lo).
Axes of the slice: x: 4, y: 4 (y_hi: 2, y_lo: 2; y = y_hi * 2 + y_lo), z: 4, core: 2. Of those that a mesh axis runs over, the one named last changes fastest.
Arguments:
- tokens: bfloat16 [32, 1024, 1280], P('dp', 'ctx'), may hold values from -6 to 6
- segments: int32 [32, 1024], P('dp', 'ctx'), may hold values from 0 to 3, as said below
- cotangent: bfloat16 [32, 1024, 1280], P('dp', 'ctx'), may hold values from -6 to 6
- w_qkv: bfloat16 [1280, 3840], P('ctx', 'dp'), may hold values from -0.15625 to 0.15625
- w_out: bfloat16 [1280, 1280], P('ctx', 'dp'), may hold values from -1.25 to 1.25
- w_fc: bfloat16 [1280, 5120], P('ctx', 'dp'), may hold values from -0.15625 to 0.15625
- w_proj: bfloat16 [5120, 1280], P('dp', 'ctx'), may hold values from -0.078125 to 0.078125
- pre_gain: bfloat16 [1280], P(('dp', 'ctx')), may hold values from 0.5 to 1.5
- pre_shift: bfloat16 [1280], P(('dp', 'ctx')), may hold values from -4 to 4
- bias_qv: bfloat16 [2560], P(('dp', 'ctx')), may hold values from -1.5 to 1.5
- bias_out: bfloat16 [1280], P(('dp', 'ctx')), may hold values from -4 to 4
- mid_gain: bfloat16 [1280], P(('dp', 'ctx')), may hold values from 0.5 to 1.5
- mid_shift: bfloat16 [1280], P(('dp', 'ctx')), may hold values from -4 to 4
- bias_fc: bfloat16 [5120], P(('dp', 'ctx')), may hold values from -4 to 4
- bias_proj: bfloat16 [1280], P(('dp', 'ctx')), may hold values from -4 to 4
Outputs:
- block_out: bfloat16 [32, 1024, 1280], P('dp', 'ctx')
- input_grad: float32 [32, 1024, 1280], P('dp', 'ctx')
- grad_w_qkv: float32 [1280, 3840], P('ctx', 'dp')
- grad_w_out: float32 [1280, 1280], P('ctx', 'dp')
- grad_w_fc: float32 [1280, 5120], P('ctx', 'dp')
- grad_w_proj: float32 [5120, 1280], P('dp', 'ctx')
- grad_pre_gain: float32 [1280], P(('dp', 'ctx'))
- grad_pre_shift: float32 [1280], P(('dp', 'ctx'))
- grad_bias_qv: float32 [2560], P(('dp', 'ctx'))
- grad_bias_out: float32 [1280], P(('dp', 'ctx'))
- grad_mid_gain: float32 [1280], P(('dp', 'ctx'))
- grad_mid_shift: float32 [1280], P(('dp', 'ctx'))
- grad_bias_fc: float32 [5120], P(('dp', 'ctx'))
- grad_bias_proj: float32 [1280], P(('dp', 'ctx'))
The draws below stay inside these ranges and needn't reach their ends.
Inputs may be any that keep to these rules, and one draw needn't show every extreme that they name: `segments`: segment numbers never fall along a sequence; of the 2 sequences of each dp index, one, drawn from the seed, is a single segment.
All inputs are finite; a program needn't handle non-finite values.
Results may differ from the reference program's by a relative error of at most 0.014.
Values may be sent and summed in bfloat16 or wider, within the bound.
A program may use at most 320 MiB of HBM per device.

```python
import jax
import jax.numpy as jnp
from jax import lax

D = 1280
HEADS = 20
HD = 64
FF = 5120
LEN = 1024
SEQ_DEV = 2
SEQS = 32


def draw_segments(key, part):
    key = jax.random.fold_in(key, 11)
    pick_key, cut_key = jax.random.split(key)
    cut_points = jax.random.randint(cut_key, (SEQS, 1, 3), 1, LEN)
    positions = jnp.arange(LEN, dtype=jnp.int32)[None, :, None]
    seg_numbers = jnp.sum((positions >= cut_points).astype(jnp.int32), axis=-1)
    group_count = SEQS // SEQ_DEV
    whole_pick = jax.random.randint(pick_key, (group_count, 1), 0, SEQ_DEV)
    slot_index = (jnp.arange(SEQS, dtype=jnp.int32) % SEQ_DEV).reshape(group_count, SEQ_DEV)
    single = (slot_index == whole_pick).reshape(SEQS, 1)
    return jnp.where(single, 0, seg_numbers).astype(jnp.int32)


def level_of(own_key, shape, cuts, least, largest):
    def one(axis_at, parts):
        draws = jax.random.uniform(jax.random.fold_in(jax.random.fold_in(own_key, 6), axis_at), (parts,), jnp.float32, least / len(cuts), largest / len(cuts))
        return jnp.repeat(jnp.exp(draws), shape[axis_at] // parts).reshape((-1,) + (1,) * (len(shape) - axis_at - 1))

    level = one(*cuts[0])
    for cut in cuts[1:]:
        level = level * one(*cut)
    return level


def gaussian(rng, dims, deviation, limit, cuts=(), kind=jnp.bfloat16):
    entries = deviation * jax.random.normal(rng, dims, jnp.float32)
    if cuts:
        entries = entries * level_of(rng, dims, cuts, -0.22, 0.18)
    return jnp.clip(entries, -limit, limit).astype(kind)


def setup_inputs(seed: int = 0) -> dict:
    streams_of = jax.random.split(jax.random.key(seed), 16)
    tokens = gaussian(streams_of[0], (SEQS, LEN, D), 1.0, 6.0, ((0, 16), (1, 8)))
    segments = draw_segments(jax.random.fold_in(streams_of[15], 71), 0)
    cotangent = gaussian(streams_of[2], (SEQS, LEN, D), 1.0, 6.0, ((0, 16), (1, 8)))
    w_qkv = gaussian(streams_of[3], (D, 3 * D), D ** -0.5, 0.15625, ((0, 8), (1, 16)))
    w_out = gaussian(streams_of[4], (D, D), (D // 64) ** -0.5, 1.25, ((0, 8), (1, 16)))
    w_fc = gaussian(streams_of[5], (D, FF), D ** -0.5, 0.15625, ((0, 8), (1, 16)))
    w_proj = gaussian(streams_of[6], (FF, D), FF ** -0.5, 0.078125, ((0, 16), (1, 8)))
    pre_gain = jnp.clip(1.0 + 0.1 * jax.random.normal(streams_of[7], (D,), jnp.float32), 0.5, 1.5).astype(jnp.bfloat16)
    pre_shift = gaussian(streams_of[8], (D,), 0.3, 4.0, ((0, 128),))
    bias_qv = gaussian(streams_of[9], (2 * D,), 0.1, 1.5, ((0, 128),))
    bias_out = gaussian(streams_of[10], (D,), 0.3, 4.0, ((0, 128),))
    mid_gain = jnp.clip(1.0 + 0.1 * jax.random.normal(streams_of[11], (D,), jnp.float32), 0.5, 1.5).astype(jnp.bfloat16)
    mid_shift = gaussian(streams_of[12], (D,), 0.3, 4.0, ((0, 128),))
    bias_fc = gaussian(streams_of[13], (FF,), 0.3, 4.0, ((0, 128),))
    bias_proj = gaussian(streams_of[14], (D,), 0.3, 4.0, ((0, 128),))
    return dict(tokens=tokens, segments=segments, cotangent=cotangent, w_qkv=w_qkv, w_out=w_out, w_fc=w_fc, w_proj=w_proj, pre_gain=pre_gain, pre_shift=pre_shift, bias_qv=bias_qv, bias_out=bias_out, mid_gain=mid_gain, mid_shift=mid_shift, bias_fc=bias_fc, bias_proj=bias_proj)


EPSILON = 1e-05
SCORE_SCALE = 0.125
MASKED_VALUE = -1e+30
PRECISE = lax.Precision.HIGHEST

@jax.custom_vjp
def low(v):
    return lax.optimization_barrier(v.astype(jnp.bfloat16)).astype(jnp.float32)

@jax.custom_vjp
def low_back(v):
    return v

def low_keep(v):
    return (low(v), None)

def low_pass(kept, grad):
    return (grad,)

def back_keep(v):
    return (v, None)

def back_low(kept, grad):
    return (low(grad),)
low.defvjp(low_keep, low_pass)
low_back.defvjp(back_keep, back_low)

def norm_rows(values, gain, shift):
    center = values - lax.optimization_barrier(jnp.mean(values, axis=-1, keepdims=True))
    spread = lax.optimization_barrier(jnp.mean(center * center, axis=-1, keepdims=True))
    return center * lax.rsqrt(spread + EPSILON) * gain + shift

def matmul(left, right):
    return jnp.dot(left, right, precision=PRECISE)

def block_forward(inputs, segment_row, weights):
    w_qkv, w_out, w_fc, w_proj, pre_gain, pre_shift, bias_qv, bias_out, mid_gain, mid_shift, bias_fc, bias_proj = weights
    row_count = inputs.shape[0]
    model_width = inputs.shape[1]
    normed = low(norm_rows(inputs, pre_gain, pre_shift))
    bias_full = jnp.concatenate([bias_qv[:model_width], jnp.zeros((model_width,), jnp.float32), bias_qv[model_width:]])
    packed = low(low_back(matmul(normed, w_qkv) + bias_full))
    query = packed[:, :model_width].reshape(row_count, HEADS, HD)
    key_rows = packed[:, model_width:2 * model_width].reshape(row_count, HEADS, HD)
    value_rows = packed[:, 2 * model_width:].reshape(row_count, HEADS, HD)
    scores = low_back(jnp.einsum('qhd,khd->hqk', query, key_rows, precision=PRECISE) * SCORE_SCALE)
    positions = jnp.arange(row_count, dtype=jnp.int32)
    allowed = (positions[None, :] <= positions[:, None]) & (segment_row[None, :] == segment_row[:, None])
    masked = jnp.where(allowed[None], scores, MASKED_VALUE)
    row_max = lax.optimization_barrier(jnp.max(masked, axis=-1, keepdims=True))
    exponent = jnp.exp(masked - row_max)
    soft_low = low(exponent / lax.optimization_barrier(jnp.sum(exponent, axis=-1, keepdims=True)))
    mixed = jnp.einsum('hqk,khd->qhd', soft_low, value_rows, precision=PRECISE).reshape(row_count, model_width)
    mixed = low(low_back(mixed))
    middle = inputs + low_back(matmul(mixed, w_out) + bias_out)
    normed_mid = low(norm_rows(middle, mid_gain, mid_shift))
    pre_gelu = low_back(matmul(normed_mid, w_fc) + bias_fc)
    activated = low(jax.nn.gelu(pre_gelu, approximate=True))
    return middle + low_back(matmul(activated, w_proj) + bias_proj)

def reference(tokens, segments, cotangent, w_qkv, w_out, w_fc, w_proj, pre_gain, pre_shift, bias_qv, bias_out, mid_gain, mid_shift, bias_fc, bias_proj):
    weights = tuple((entry.astype(jnp.float32) for entry in (w_qkv, w_out, w_fc, w_proj, pre_gain, pre_shift, bias_qv, bias_out, mid_gain, mid_shift, bias_fc, bias_proj)))

    def one_sequence(summed, element):
        inputs, segment_row, out_grad = element
        result, pull = jax.vjp(lambda values, params: block_forward(values, segment_row, params), inputs.astype(jnp.float32), weights)
        input_part, weight_grads = pull(out_grad.astype(jnp.float32))
        summed = jax.tree.map(jnp.add, summed, weight_grads)
        return (summed, (result.astype(jnp.bfloat16), input_part))
    start = jax.tree.map(jnp.zeros_like, weights)
    summed, (outputs, input_grads) = lax.scan(one_sequence, start, (tokens, segments, cotangent))
    return (outputs, input_grads, summed[0], summed[1], summed[2], summed[3], summed[4], summed[5], summed[6], summed[7], summed[8], summed[9], summed[10], summed[11])
```

```python
import numpy as np
import jax
import jax.numpy as jnp
from jax import lax
from jax.experimental import pallas as pl
from jax.experimental.pallas import tpu as pltpu
from jax.sharding import PartitionSpec as P

MESH = pl.DeviceIdType.MESH


def coords():
    dp = lax.axis_index("dp")
    ctx = lax.axis_index("ctx")
    core = lax.rem(dp, 2)
    z = lax.rem(lax.div(dp, 2), 4)
    y = lax.div(dp, 8) * 2 + lax.rem(ctx, 2)
    x = lax.div(ctx, 2)
    return dict(x=x, y=y, z=z), core


def device_of(pos, core):
    dp = (lax.div(pos["y"], 2) * 4 + pos["z"]) * 2 + core
    ctx = pos["x"] * 2 + lax.rem(pos["y"], 2)
    return (dp, ctx)


def shifted(pos, axis, by):
    return {**pos, axis: lax.rem(pos[axis] + by + 4, 4)}


def greet(pos, core):
    barrier = pltpu.get_barrier_semaphore()
    for axis in "xyz":
        for by in (1, -1):
            pl.semaphore_signal(barrier, inc=1, device_id=device_of(shifted(pos, axis, by), core), device_id_type=MESH)
    pl.semaphore_signal(barrier, inc=1, device_id=device_of(pos, 1 - core), device_id_type=MESH)
    pl.semaphore_wait(barrier, 7)


def block_index(where, core, lanes):
    out = {}
    for axis in "xz":
        value = where[axis]
        if value is None:
            out[axis] = slice(None)
        elif isinstance(value, tuple):
            out[axis] = pl.ds(value[1] * 2, 2)
        else:
            out[axis] = value
    value = where["y"]
    if value is None:
        hi, lo = slice(None), slice(None)
    elif isinstance(value, tuple):
        hi, lo = value[1], slice(None)
    else:
        hi, lo = lax.div(value, 2), lax.rem(value, 2)
    return (hi, out["z"], out["x"], lo, core, slice(None), pl.ds(lanes[0], lanes[1] - lanes[0]))


ORDERS = {"A": "xyz", "B": "yzx", "C": "zxy"}
PARTS = [
    (0, "A", (0, 256)), (0, "B", (256, 512)), (1, "C", (0, 256)),
    (2, "A", (0, 256)), (2, "B", (256, 512)), (2, "C", (512, 640)),
    (3, "A", (0, 256)), (3, "B", (256, 384)), (3, "C", (384, 640)),
]
LANES = (512, 256, 640, 640)
ROUNDS = [PARTS[0:3], PARTS[3:6], PARTS[6:9]]
SENDS = 16 * len(PARTS)


def gather_kernel(*refs):
    ins, outs = refs[:4], refs[4:8]
    send_sem, recv_sem, local_sem = refs[8:11]
    pos, core = coords()
    greet(pos, core)
    count = [0]
    started = []

    def send(src, dst, dev):
        i = count[0]
        count[0] += 1
        copy = pltpu.make_async_remote_copy(src_ref=src, dst_ref=dst, send_sem=send_sem.at[i], recv_sem=recv_sem.at[i],
                                            device_id=dev, device_id_type=MESH)
        copy.start()
        started.append(copy)
        return copy

    local = []
    for t in range(4):
        where = dict(pos)
        c = pltpu.make_async_copy(ins[t], outs[t].at[block_index(where, core, (0, LANES[t]))], local_sem.at[t])
        c.start()
        local.append(c)

    first, second, pushes = {}, {}, []

    def where_of(part, k, value, half=None):
        order = ORDERS[part[1]]
        where = {}
        for j, axis in enumerate(order):
            where[axis] = None if j < k else (value if j == k else pos[axis])
        if half is not None:
            where[order[k - 1]] = ("half", half)
        return where

    def put(part, where, dev, src=None):
        t, _, lanes = part
        ref = outs[t].at[block_index(where, core, lanes)]
        return send(ref if src is None else src, ref, dev)

    def step1(part, k):
        axis = ORDERS[part[1]][k]
        where = where_of(part, k, pos[axis])
        src = ins[part[0]].at[:, pl.ds(part[2][0], part[2][1] - part[2][0])] if k == 0 else None
        right = put(part, where, device_of(shifted(pos, axis, 1), core), src)
        left = put(part, where, device_of(shifted(pos, axis, -1), core), src)
        first[part, k] = (right, left)
        if k == 2:
            pushes.append(put(part, where, device_of(pos, 1 - core)))

    def step2(part, k):
        axis = ORDERS[part[1]][k]
        right, left = first[part, k]
        right.wait_recv()
        below = shifted(pos, axis, -1)[axis]
        above = shifted(pos, axis, 1)[axis]
        if k == 0:
            fr = put(part, where_of(part, k, below), device_of(shifted(pos, axis, 1), core))
            left.wait_recv()
            second[part, k] = (fr,)
        else:
            fr = put(part, where_of(part, k, below, 0), device_of(shifted(pos, axis, 1), core))
            left.wait_recv()
            fl = put(part, where_of(part, k, above, 1), device_of(shifted(pos, axis, -1), core))
            second[part, k] = (fr, fl)
        if k == 2:
            pushes.append(put(part, where_of(part, k, below), device_of(pos, 1 - core)))
            pushes.append(put(part, where_of(part, k, above), device_of(pos, 1 - core)))

    def step3(part, k):
        axis = ORDERS[part[1]][k]
        for c in second[part, k]:
            c.wait_recv()
        if k == 2:
            across = shifted(pos, axis, 2)[axis]
            pushes.append(put(part, where_of(part, k, across), device_of(pos, 1 - core)))

    def all_of(step, k, r):
        for part in ROUNDS[r]:
            step(part, k)

    for r in range(3):
        all_of(step1, 0, r)
    for c in local:
        c.wait()
    for r in range(3):
        all_of(step2, 0, r)
    for r in range(3):
        all_of(step3, 0, r)
        all_of(step1, 1, r)
    for r in range(3):
        all_of(step2, 1, r)
    for r in range(3):
        all_of(step3, 1, r)
        all_of(step1, 2, r)
    for r in range(3):
        all_of(step2, 2, r)
    for r in range(3):
        all_of(step3, 2, r)
    for c in pushes:
        c.wait_recv()
    for c in started:
        c.wait_send()


def gather(blocks):
    outs = [jax.ShapeDtypeStruct((2, 4, 4, 2, 2, 80, n), jnp.bfloat16) for n in LANES]
    return pl.pallas_call(
        gather_kernel,
        out_shape=outs,
        in_specs=[pl.BlockSpec(memory_space=pl.ANY)] * 4,
        out_specs=[pl.BlockSpec(memory_space=pl.ANY)] * 4,
        scratch_shapes=[
            pltpu.SemaphoreType.DMA((SENDS,)),
            pltpu.SemaphoreType.DMA((SENDS,)),
            pltpu.SemaphoreType.DMA((4,)),
        ],
        compiler_params=pltpu.CompilerParams(collective_id=0, has_side_effects=True),
        name="gather_weights",
    )(*blocks)


def scatter_kernel(*refs):
    grads, outs = refs[:4], refs[4:8]
    sums, slots = refs[8:12], refs[12:16]
    stages = dict(zip("ABC", refs[16:19]))
    send_sem, recv_sem, stage_sem = refs[19:22]
    pos, core = coords()
    greet(pos, core)
    count = [0]
    started = []

    def send(src, dst, dev):
        i = count[0]
        count[0] += 1
        copy = pltpu.make_async_remote_copy(src_ref=src, dst_ref=dst, send_sem=send_sem.at[i], recv_sem=recv_sem.at[i],
                                            device_id=dev, device_id_type=MESH)
        copy.start()
        started.append(copy)
        return copy

    def lanes_of(part):
        return pl.ds(part[2][0], part[2][1] - part[2][0])

    def where_of(part, k, value, half=None):
        order = ORDERS[part[1]]
        where = {}
        for j, axis in enumerate(order):
            where[axis] = None if j < k else (value if j == k else pos[axis])
        if half is not None:
            where[order[k - 1]] = ("half", half)
        return where

    def slot_of(part, k, slot, half=None):
        order = ORDERS[part[1]]
        where = {}
        for j, axis in enumerate(order):
            where[axis] = None if j < k else (slot if j == k else 3)
        if half is not None:
            where[order[k - 1]] = ("half", half)
        return where

    def ranges(where):
        out = {}
        for axis in "xz":
            v = where[axis]
            out[axis] = (0, 4) if v is None else ((v[1] * 2, 2) if isinstance(v, tuple) else (v, 1))
        v = where["y"]
        if v is None:
            hi, lo = (0, 2), (0, 2)
        elif isinstance(v, tuple):
            hi, lo = (v[1], 1), (0, 2)
        elif isinstance(v, int):
            hi, lo = (v // 2, 1), (v % 2, 1)
        else:
            hi, lo = (lax.div(v, 2), 1), (lax.rem(v, 2), 1)
        return (hi, out["z"], out["x"], lo)

    def view(ref, part, where):
        idx = tuple(s if n == 1 else pl.ds(s, n) for s, n in ranges(where))
        return ref.at[idx + (slice(None), lanes_of(part))]

    def each_block(where_to, where_from, body):
        to, frm = ranges(where_to), ranges(where_from)
        total = 1
        for _, n in to:
            total *= n

        def step(i, carry):
            a, b = [], []
            left = i
            for (s, n), (t, m) in zip(reversed(to), reversed(frm)):
                if n == 1:
                    a.append(s)
                    b.append(t)
                else:
                    d = lax.rem(left, n)
                    left = lax.div(left, n)
                    a.append(s + d)
                    b.append(t + d)
            body(tuple(reversed(a)), tuple(reversed(b)), i)
            return carry

        if total == 1:
            step(0, 0)
        else:
            lax.fori_loop(0, total, step, 0)

    pushes = {}

    def push(part, which):
        t = part[0]
        value = at(part, which)
        where = where_of(part, 2, value)
        idx = tuple(s if n == 1 else pl.ds(s, n) for s, n in ranges(where))
        src = grads[t].at[idx + (1 - core, slice(None), lanes_of(part))]
        pushes[part, which] = send(src, view(sums[t], part, where), device_of(pos, 1 - core))

    def at(part, which):
        axis = ORDERS[part[1]][2]
        return shifted(pos, axis, which)[axis]

    plan = []
    for r in range(3):
        for which in (2, 1, -1):
            plan.append((r, which))
    for r in range(3):
        plan.append((r, 0))
    order_of_adds = [(0, 2), (0, 1), (0, -1), (1, 2), (1, 1), (1, -1), (2, 2), (2, 1), (2, -1), (0, 0), (1, 0), (2, 0)]
    loads = {}

    def load(n):
        if n >= len(order_of_adds):
            return
        r, which = order_of_adds[n]
        for j, part in enumerate(ROUNDS[r]):
            t, g, lanes = part
            where = where_of(part, 2, at(part, which))
            idx = tuple(s if m == 1 else pl.ds(s, m) for s, m in ranges(where))
            width = lanes[1] - lanes[0]
            src = grads[t].at[idx + (core, slice(None), lanes_of(part))]
            dst = stages[g].at[n % 2]
            if width != 256:
                dst = dst.at[..., pl.ds(0, width)]
            copy = pltpu.make_async_copy(src, dst, stage_sem.at[n % 2, j])
            copy.start()
            loads[n, j] = copy

    def pair_add(n):
        r, which = order_of_adds[n]
        for j, part in enumerate(ROUNDS[r]):
            t, g, lanes = part
            width = lanes[1] - lanes[0]
            loads[n, j].wait()
            pushes[part, which].wait_recv()
            where = where_of(part, 2, at(part, which))
            zero = dict(where)
            for axis in "xyz":
                if not (zero[axis] is None):
                    zero[axis] = 0
            dims = [k for k, (_, m) in enumerate(ranges(where)) if m != 1]

            def body(a, b, i, t=t, g=g, lanes=lanes, width=width, dims=dims):
                own = stages[g][(n % 2,) + tuple(b[k] for k in dims) + (slice(None), pl.ds(0, width))]
                here = a + (slice(None), pl.ds(lanes[0], width))
                sums[t][here] = sums[t][here] + own

            each_block(where, zero, body)
        load(n + 2)

    first, second = {}, {}

    def add_into(part, where, slot):
        t, _, lanes = part
        la = pl.ds(lanes[0], lanes[1] - lanes[0])

        def body(a, b, i):
            here, there = a + (slice(None), la), b + (slice(None), la)
            sums[t][here] = sums[t][here] + slots[t][there]

        each_block(where, slot, body)

    def step1(r, k):
        for part in ROUNDS[r]:
            t = part[0]
            axis = ORDERS[part[1]][k]
            across = shifted(pos, axis, 2)[axis]
            right, left = (device_of(shifted(pos, axis, by), core) for by in (1, -1))
            if k == 0:
                first[part, k] = (send(view(sums[t], part, where_of(part, k, across)),
                                       view(slots[t], part, slot_of(part, k, 0)), right),)
            else:
                a = send(view(sums[t], part, where_of(part, k, across, 0)),
                         view(slots[t], part, slot_of(part, k, 0, 0)), right)
                b = send(view(sums[t], part, where_of(part, k, across, 1)),
                         view(slots[t], part, slot_of(part, k, 0, 1)), left)
                first[part, k] = (a, b)

    def step2(r, k):
        for part in ROUNDS[r]:
            t = part[0]
            axis = ORDERS[part[1]][k]
            above, below = (shifted(pos, axis, by)[axis] for by in (1, -1))
            right, left = (device_of(shifted(pos, axis, by), core) for by in (1, -1))
            first[part, k][0].wait_recv()
            if k == 0:
                add_into(part, where_of(part, k, above), slot_of(part, k, 0))
            else:
                add_into(part, where_of(part, k, above, 0), slot_of(part, k, 0, 0))
            a = send(view(sums[t], part, where_of(part, k, above)), view(slots[t], part, slot_of(part, k, 1)), right)
            if k != 0:
                first[part, k][1].wait_recv()
                add_into(part, where_of(part, k, below, 1), slot_of(part, k, 0, 1))
            b = send(view(sums[t], part, where_of(part, k, below)), view(slots[t], part, slot_of(part, k, 2)), left)
            second[part, k] = (a, b)

    def step3(r, k):
        for part in ROUNDS[r]:
            t, _, lanes = part
            la = pl.ds(lanes[0], lanes[1] - lanes[0])
            axis = ORDERS[part[1]][k]
            for c in second[part, k]:
                c.wait_recv()

            def body(a, b, i):
                here = a + (slice(None), la)
                b2 = tuple(u + v for u, v in zip(b, gap))
                total = (sums[t][here].astype(jnp.float32) + slots[t][b + (slice(None), la)].astype(jnp.float32)
                         + slots[t][b2 + (slice(None), la)].astype(jnp.float32))
                if k == 0:
                    outs[t][:, la] = total
                else:
                    sums[t][here] = total.astype(jnp.bfloat16)

            one, two = ranges(slot_of(part, k, 1)), ranges(slot_of(part, k, 2))
            gap = tuple(v[0] - u[0] for u, v in zip(one, two))
            each_block(where_of(part, k, pos[axis]), slot_of(part, k, 1), body)

    load(0)
    load(1)
    for r, which in order_of_adds:
        for part in ROUNDS[r]:
            push(part, which)
    pair_add(0)
    step1(0, 2)
    pair_add(1)
    pair_add(2)
    pair_add(3)
    step1(1, 2)
    step2(0, 2)
    pair_add(4)
    pair_add(5)
    pair_add(6)
    step1(2, 2)
    step2(1, 2)
    pair_add(7)
    pair_add(8)
    pair_add(9)
    step2(2, 2)
    step3(0, 2)
    step1(0, 1)
    pair_add(10)
    step2(0, 1)
    step3(1, 2)
    step1(1, 1)
    pair_add(11)
    step3(0, 1)
    step1(0, 0)
    step2(1, 1)
    step3(2, 2)
    step1(2, 1)
    step2(0, 0)
    step3(1, 1)
    step1(1, 0)
    step2(2, 1)
    step3(0, 0)
    step2(1, 0)
    step3(2, 1)
    step1(2, 0)
    step3(1, 0)
    step2(2, 0)
    step3(2, 0)
    for c in started:
        c.wait_send()


SCATTER_SENDS = 9 * (4 + 4 + 4 + 3)


def scatter(grads):
    outs = [jax.ShapeDtypeStruct((80, n), jnp.float32) for n in LANES]
    return pl.pallas_call(
        scatter_kernel,
        out_shape=outs,
        in_specs=[pl.BlockSpec(memory_space=pl.ANY)] * 4,
        out_specs=[pl.BlockSpec(memory_space=pltpu.VMEM)] * 4,
        scratch_shapes=[pltpu.VMEM((2, 4, 4, 2, 80, n), jnp.bfloat16) for n in LANES] * 2 + [
            pltpu.VMEM((2, 2, 4, 2, 80, 256), jnp.bfloat16),
            pltpu.VMEM((2, 2, 4, 2, 80, 256), jnp.bfloat16),
            pltpu.VMEM((2, 4, 4, 80, 256), jnp.bfloat16),
            pltpu.SemaphoreType.DMA((SCATTER_SENDS,)),
            pltpu.SemaphoreType.DMA((SCATTER_SENDS,)),
            pltpu.SemaphoreType.DMA((2, 3)),
        ],
        compiler_params=pltpu.CompilerParams(collective_id=1, has_side_effects=True, vmem_limit_bytes=60 * 1024 * 1024),
        name="scatter_grads",
    )(*grads)


EPSILON = 1e-05
MASKED_VALUE = -1e30
BF = jnp.bfloat16
F32 = jnp.float32
MIB = 1024 * 1024
VMEM = pltpu.VMEM


def dot(a, b):
    return jnp.dot(a, b, preferred_element_type=F32)


def dot_nt(a, b):
    return lax.dot_general(a, b, (((1,), (1,)), ((), ())), preferred_element_type=F32)


def dot_tn(a, b):
    return lax.dot_general(a, b, (((0,), (0,)), ((), ())), preferred_element_type=F32)


def turned(a):
    return a.astype(F32).T.astype(a.dtype)


def norm_parts(values):
    center = values - jnp.mean(values, axis=-1, keepdims=True)
    spread = jnp.mean(center * center, axis=-1, keepdims=True)
    r = lax.rsqrt(spread + EPSILON)
    return center * r, r


def norm_back(u, r, gain, e):
    n = e * gain
    dv = r * (n - jnp.mean(n, axis=-1, keepdims=True) - u * jnp.mean(n * u, axis=-1, keepdims=True))
    return dv, jnp.sum(e * u, axis=0, keepdims=True), jnp.sum(e, axis=0, keepdims=True)


def selector():
    out = np.zeros((1024, 1152), np.float32)
    for m in range(3):
        for j in range(320):
            at = 320 * m + j
            out[(at // 240) * 256 + at % 240, 384 * m + j] = 1
    return out


def qkv_kernel(tokens, gain, shift, w, bias, seg, select, normed, blocks, packed):
    p = pl.program_id(0)

    @pl.when(p == 0)
    def _():
        u, _ = norm_parts(tokens[...].astype(F32))
        normed[...] = (u * gain[...] + shift[...]).astype(BF)

    packed[p] = (dot(normed[...], w[0]) + bias[0]).astype(BF)

    @pl.when(p == 7)
    def _():
        for i in range(4):
            wide = jnp.concatenate([packed[2 * i], packed[2 * i + 1]], axis=1)
            chunks = dot(wide, select[...]).astype(BF)
            for m in range(3):
                n = 3 * i + m
                kind, g = n // 4, n % 4
                chunk = chunks[:, 384 * m:384 * m + 384]
                for s in range(2):
                    rows = chunk[s * 128:(s + 1) * 128]
                    blocks[s * 4 + g, kind] = rows
                    if kind == 0:
                        blocks[s * 4 + g, 0, :, 320:384] = seg[s * 128:(s + 1) * 128, :]


def qkv_forward(tokens, gain, shift, w, bias, seg, select):
    full = lambda *shape: pl.BlockSpec(shape, lambda p: (0,) * len(shape))
    return pl.pallas_call(
        qkv_kernel,
        grid=(8,),
        in_specs=[full(256, 1280), full(1, 1280), full(1, 1280), pl.BlockSpec((1, 1280, 512), lambda p: (p, 0, 0)),
                  pl.BlockSpec((1, 1, 512), lambda p: (p, 0, 0)), full(256, 64), full(1024, 1152)],
        out_specs=[full(256, 1280), full(8, 3, 128, 384)],
        out_shape=[jax.ShapeDtypeStruct((256, 1280), BF), jax.ShapeDtypeStruct((8, 3, 128, 384), BF)],
        scratch_shapes=[VMEM((8, 256, 512), BF)],
        compiler_params=pltpu.CompilerParams(vmem_limit_bytes=56 * MIB),
        name="qkv_forward",
    )(tokens, gain, shift, w, bias, seg, select)


def exchange_kernel(src, dst, send_sem, recv_sem, local_sem):
    dp, ctx = lax.axis_index("dp"), lax.axis_index("ctx")
    barrier = pltpu.get_barrier_semaphore()
    others = [lax.rem(ctx + d, 8) for d in range(1, 8)]
    for other in others:
        pl.semaphore_signal(barrier, inc=1, device_id=(dp, other), device_id_type=MESH)
    pl.semaphore_wait(barrier, 7)
    copies = []
    for i, other in enumerate(others):
        copy = pltpu.make_async_remote_copy(src_ref=src.at[other], dst_ref=dst.at[ctx], send_sem=send_sem.at[i],
                                            recv_sem=recv_sem.at[i], device_id=(dp, other), device_id_type=MESH)
        copy.start()
        copies.append(copy)
    local = pltpu.make_async_copy(src.at[ctx], dst.at[ctx], local_sem)
    local.start()
    local.wait()
    for copy in copies:
        copy.wait()


def exchange(blocks, number):
    return pl.pallas_call(
        exchange_kernel,
        out_shape=jax.ShapeDtypeStruct(blocks.shape, blocks.dtype),
        in_specs=[pl.BlockSpec(memory_space=pl.ANY)],
        out_specs=pl.BlockSpec(memory_space=pl.ANY),
        scratch_shapes=[pltpu.SemaphoreType.DMA((7,)), pltpu.SemaphoreType.DMA((7,)), pltpu.SemaphoreType.DMA],
        compiler_params=pltpu.CompilerParams(collective_id=number, has_side_effects=True),
        name="exchange_heads",
    )(blocks)


def head_lanes(rows, half):
    lane = lax.broadcasted_iota(jnp.int32, (rows, 128), 1)
    return (lane < 64) if half == 0 else (lane >= 64)


def only(values, half):
    return jnp.where(head_lanes(values.shape[0], half), values, jnp.zeros_like(values))


def segment_views(data):
    tile = data[:, 0, :, 256:384].reshape(1024, 128).astype(F32)
    return tile[:, 64:65], jnp.transpose(tile)[64:65, :]


def mask_of(column, row, i, wide):
    rows = lax.broadcasted_iota(jnp.int32, (256, wide), 0) + 256 * i
    cols = lax.broadcasted_iota(jnp.int32, (256, wide), 1)
    keep = (cols <= rows) & (column[256 * i:256 * i + 256] == row[:, :wide])
    return jnp.where(keep, 0.0, MASKED_VALUE)


def attend_kernel(data, mixed):
    column, row = segment_views(data)
    for i in range(4):
        wide = 256 * (i + 1)
        hide = mask_of(column, row, i, wide)
        for j in range(3):
            lanes = slice(128 * j, 128 * j + 128)
            q = data[2 * i:2 * i + 2, 0, :, lanes].reshape(256, 128)
            k = data[0:2 * i + 2, 1, :, lanes].reshape(wide, 128)
            v = data[0:2 * i + 2, 2, :, lanes].reshape(wide, 128)
            total = None
            for half in range(2 if j < 2 else 1):
                scores = dot_nt(only(q, half) * jnp.asarray(0.125, BF), k) + hide
                e = jnp.exp(scores - jnp.max(scores, axis=-1, keepdims=True))
                soft = (e / jnp.sum(e, axis=-1, keepdims=True)).astype(BF)
                part = dot(soft, only(v, half))
                total = part if total is None else total + part
            mixed[2 * i:2 * i + 2, :, lanes] = total.astype(BF).reshape(2, 128, 128)


def attend(data):
    return pl.pallas_call(
        attend_kernel,
        out_shape=jax.ShapeDtypeStruct((8, 128, 384), BF),
        in_specs=[pl.BlockSpec(memory_space=VMEM)],
        out_specs=pl.BlockSpec(memory_space=VMEM),
        compiler_params=pltpu.CompilerParams(vmem_limit_bytes=56 * MIB),
        name="attend",
    )(data)


def attend_back_kernel(data, grad, out, dk, dv):
    column, row = segment_views(data)
    dk[...] = jnp.zeros_like(dk)
    dv[...] = jnp.zeros_like(dv)
    for i in range(4):
        wide = 256 * (i + 1)
        hide = mask_of(column, row, i, wide)
        for j in range(3):
            lanes = slice(128 * j, 128 * j + 128)
            q = data[2 * i:2 * i + 2, 0, :, lanes].reshape(256, 128) * jnp.asarray(0.125, BF)
            k = data[0:2 * i + 2, 1, :, lanes].reshape(wide, 128)
            v = data[0:2 * i + 2, 2, :, lanes].reshape(wide, 128)
            g = grad[2 * i:2 * i + 2, :, lanes].reshape(256, 128)
            total = None
            for half in range(2 if j < 2 else 1):
                qh, gh = only(q, half), only(g, half)
                scores = dot_nt(qh, k) + hide
                e = jnp.exp(scores - jnp.max(scores, axis=-1, keepdims=True))
                soft = e / jnp.sum(e, axis=-1, keepdims=True)
                dv[0:wide, lanes] += dot_tn(soft.astype(BF), gh)
                sg = dot_nt(gh, v)
                sg = (soft * (sg - jnp.sum(soft * sg, axis=-1, keepdims=True))).astype(BF)
                dk[0:wide, lanes] += dot_tn(sg, qh)
                part = dot(sg, only(k, half)) * 0.125
                total = part if total is None else total + part
            out[2 * i:2 * i + 2, 0, :, lanes] = total.astype(BF).reshape(2, 128, 128)
    out[:, 1] = dk[...].astype(BF).reshape(8, 128, 384)
    out[:, 2] = dv[...].astype(BF).reshape(8, 128, 384)


def attend_back(data, grad):
    return pl.pallas_call(
        attend_back_kernel,
        out_shape=jax.ShapeDtypeStruct((8, 3, 128, 384), BF),
        in_specs=[pl.BlockSpec(memory_space=VMEM)] * 2,
        out_specs=pl.BlockSpec(memory_space=VMEM),
        scratch_shapes=[VMEM((1024, 384), F32)] * 2,
        compiler_params=pltpu.CompilerParams(vmem_limit_bytes=56 * MIB),
        name="attend_back",
    )(data, grad)


GELU_A = 0.7978845608028654
GELU_B = 0.044715


def feed_kernel(tokens, cotangent, mixed, w_out, bias_out, gain, shift, fc, pj, bias_fc, bias_proj,
                block_out, middle_grad, mixed_grad, d_fc, d_pj, d_out, d_bias_fc, d_vec,
                middle, a2, a2_t, bg_t, out_sum, a2_sum):
    p = pl.program_id(0)

    @pl.when(p == 0)
    def _():
        total = tokens[...].astype(F32) + bias_out[...]
        for g in range(4):
            rows = jnp.concatenate([mixed[g, :, 0:320], mixed[4 + g, :, 0:320]], axis=0)
            total = total + dot(rows, w_out[320 * g:320 * g + 320, :])
        middle[...] = total
        u, _ = norm_parts(total)
        low = (u * gain[...] + shift[...]).astype(BF)
        a2[...] = low
        a2_t[...] = turned(low)
        bg_t[...] = turned(cotangent[...])
        out_sum[...] = jnp.zeros_like(out_sum)
        a2_sum[...] = jnp.zeros_like(a2_sum)

    pre = dot(a2[...], fc[0]) + bias_fc[0]
    square = pre * pre
    t = jnp.tanh(GELU_A * (pre + GELU_B * pre * square))
    act = (0.5 * pre * (1.0 + t)).astype(BF)
    slope = 0.5 * (1.0 + t) + 0.5 * pre * (1.0 - t * t) * (GELU_A * (1.0 + 3.0 * GELU_B * square))
    out_sum[...] += dot_nt(act, pj[0])
    d_pj[0] = dot(bg_t[...], act).astype(BF)
    pre_grad32 = slope * dot(cotangent[...], pj[0])
    pre_grad = pre_grad32.astype(BF)
    d_bias_fc[0] = jnp.sum(pre_grad.astype(F32), axis=0, keepdims=True)
    d_fc[0] = dot(a2_t[...], pre_grad).astype(BF)
    a2_sum[...] += dot_nt(pre_grad, fc[0])

    @pl.when(p == 7)
    def _():
        block_out[...] = (middle[...] + (out_sum[...] + bias_proj[...])).astype(BF)
        u, r = norm_parts(middle[...])
        dv, dg, db = norm_back(u, r, gain[...], a2_sum[...])
        c = cotangent[...].astype(F32)
        total = c + dv
        middle_grad[...] = total
        low = total.astype(BF)
        d_vec[0:1] = jnp.sum(low.astype(F32), axis=0, keepdims=True)
        d_vec[1:2] = dg
        d_vec[2:3] = db
        d_vec[3:4] = jnp.sum(c, axis=0, keepdims=True)
        for g in range(4):
            rows = jnp.concatenate([mixed[g, :, 0:320], mixed[4 + g, :, 0:320]], axis=0)
            d_out[320 * g:320 * g + 320, :] = dot_tn(rows, low).astype(BF)
            back = dot_nt(low, w_out[320 * g:320 * g + 320, :]).astype(BF)
            for s in range(2):
                mixed_grad[s * 4 + g, :, 0:320] = back[s * 128:(s + 1) * 128]
                mixed_grad[s * 4 + g, :, 320:384] = jnp.zeros((128, 64), BF)


def feed(tokens, cotangent, mixed, w_out, bias_out, gain, shift, fc, pj, bias_fc, bias_proj):
    full = lambda *shape: pl.BlockSpec(shape, lambda p: (0,) * len(shape))
    step = lambda *shape: pl.BlockSpec((1,) + shape, lambda p: (p,) + (0,) * len(shape))
    sds = jax.ShapeDtypeStruct
    return pl.pallas_call(
        feed_kernel,
        grid=(8,),
        in_specs=[full(256, 1280), full(256, 1280), full(8, 128, 384), full(1280, 1280), full(1, 1280), full(1, 1280),
                  full(1, 1280), step(1280, 640), step(1280, 640), step(1, 640), full(1, 1280)],
        out_specs=[full(256, 1280), full(256, 1280), full(8, 128, 384), step(1280, 640), step(1280, 640),
                   full(1280, 1280), step(1, 640), full(4, 1280)],
        out_shape=[sds((256, 1280), BF), sds((256, 1280), F32), sds((8, 128, 384), BF), sds((8, 1280, 640), BF),
                   sds((8, 1280, 640), BF), sds((1280, 1280), BF), sds((8, 1, 640), F32), sds((4, 1280), F32)],
        scratch_shapes=[VMEM((256, 1280), F32), VMEM((256, 1280), BF), VMEM((1280, 256), BF), VMEM((1280, 256), BF),
                        VMEM((256, 1280), F32), VMEM((256, 1280), F32)],
        compiler_params=pltpu.CompilerParams(vmem_limit_bytes=60 * MIB),
        name="feed_forward_and_back",
    )(tokens, cotangent, mixed, w_out, bias_out, gain, shift, fc, pj, bias_fc, bias_proj)


def qkv_back_kernel(tokens, middle_grad, gain, normed, grads, w, unselect, input_grad, d_w, d_bias, d_vec,
                    packed, normed_t, total):
    p = pl.program_id(0)

    @pl.when(p == 0)
    def _():
        normed_t[...] = turned(normed[...])
        total[...] = jnp.zeros_like(total)
        for i in range(4):
            chunks = []
            for m in range(3):
                n = 3 * i + m
                kind, g = n // 4, n % 4
                chunks.append(jnp.concatenate([grads[g, kind], grads[4 + g, kind]], axis=0))
            wide = dot(jnp.concatenate(chunks, axis=1), unselect[...]).astype(BF)
            packed[2 * i] = wide[:, 0:512]
            packed[2 * i + 1] = wide[:, 512:1024]

    mine = packed[p]
    d_bias[0] = jnp.sum(mine.astype(F32), axis=0, keepdims=True)
    d_w[0] = dot(normed_t[...], mine).astype(BF)
    total[...] += dot_nt(mine, w[0])

    @pl.when(p == 7)
    def _():
        u, r = norm_parts(tokens[...].astype(F32))
        dv, dg, db = norm_back(u, r, gain[...], total[...])
        input_grad[...] = middle_grad[...] + dv
        d_vec[0:1] = dg
        d_vec[1:2] = db


def qkv_back(tokens, middle_grad, gain, normed, grads, w, unselect):
    full = lambda *shape: pl.BlockSpec(shape, lambda p: (0,) * len(shape))
    step = lambda *shape: pl.BlockSpec((1,) + shape, lambda p: (p,) + (0,) * len(shape))
    sds = jax.ShapeDtypeStruct
    return pl.pallas_call(
        qkv_back_kernel,
        grid=(8,),
        in_specs=[full(256, 1280), full(256, 1280), full(1, 1280), full(256, 1280), full(8, 3, 128, 384),
                  step(1280, 512), full(1152, 1024)],
        out_specs=[full(256, 1280), step(1280, 512), step(1, 512), full(2, 1280)],
        out_shape=[sds((256, 1280), F32), sds((8, 1280, 512), BF), sds((8, 1, 512), F32), sds((2, 1280), F32)],
        scratch_shapes=[VMEM((8, 256, 512), BF), VMEM((1280, 256), BF), VMEM((256, 1280), F32)],
        compiler_params=pltpu.CompilerParams(vmem_limit_bytes=56 * MIB),
        name="qkv_back",
    )(tokens, middle_grad, gain, normed, grads, w, unselect)


VECTOR_SIZES = (10, 10, 20, 10, 10, 10, 40, 10)


def body(tokens, segments, cotangent, w_qkv, w_out, w_fc, w_proj, *vectors):
    core = lax.rem(lax.axis_index("dp"), 2)
    pairs = [(i, i ^ 1) for i in range(16)]
    mine = jnp.concatenate([w_fc, w_proj.T, w_qkv, jnp.zeros((160, 16), BF), w_out, jnp.zeros((160, 48), BF)], axis=1)
    mine = mine.reshape(2, 80, 1024)
    kept = lax.dynamic_index_in_dim(mine, core, 0, False)
    got = lax.ppermute(lax.dynamic_index_in_dim(mine, 1 - core, 0, False), "dp", pairs)
    one, two = jnp.where(core == 0, kept, got), jnp.where(core == 0, got, kept)
    vec = jnp.pad(jnp.concatenate(vectors), (0, 72)).reshape(2, 96)
    vec = jnp.pad(vec, ((0, 78), (0, 0)))
    blocks = (
        jnp.concatenate([one[:, 640:896], two[:, 640:896]], axis=1),
        jnp.concatenate([one[:, 896:976], two[:, 896:976], vec], axis=1),
        jnp.concatenate([one[:, 0:320], two[:, 0:320]], axis=1),
        jnp.concatenate([one[:, 320:640], two[:, 320:640]], axis=1),
    )
    qkv, out, fc, pj = gather(blocks)
    vec = out[..., 0:2, 160:256].transpose(0, 1, 4, 2, 3, 5, 6).reshape(128, 192)
    whole = []
    at = 0
    for n in VECTOR_SIZES:
        whole.append(vec[:, at:at + n].reshape(1, 128 * n).astype(F32))
        at += n
    pre_gain, pre_shift, bias_qv, bias_out, mid_gain, mid_shift, bias_fc, bias_proj = whole
    qkv = qkv.reshape(8, 1280, 512)
    fc = fc.reshape(8, 1280, 640)
    pj = pj.reshape(8, 1280, 640)
    w_out_all = out.reshape(8, 1280, 256)[:, :, 0:160].transpose(1, 0, 2).reshape(1280, 1280)
    bias_all = jnp.concatenate([bias_qv[:, :1280], jnp.zeros((1, 1280), F32), bias_qv[:, 1280:]], axis=1)
    bias_all = jnp.pad(bias_all.reshape(16, 240), ((0, 0), (0, 16))).reshape(8, 1, 512)
    table = selector()
    select = jnp.asarray(table, BF)
    unselect = jnp.asarray(table.T, BF)

    tokens = tokens.reshape(256, 1280)
    cotangent = cotangent.reshape(256, 1280)
    seg = jnp.broadcast_to(segments.reshape(256, 1).astype(BF), (256, 64))
    normed, sent = qkv_forward(tokens, pre_gain, pre_shift, qkv, bias_all, seg, select)
    data = exchange(sent, 2)
    mixed = exchange(attend(data), 3)
    (block_out, middle_grad, mixed_grad, d_fc, d_pj, d_out, d_bias_fc, d_mid) = feed(
        tokens, cotangent, mixed, w_out_all, bias_out, mid_gain, mid_shift, fc, pj, bias_fc.reshape(8, 1, 640), bias_proj)
    grads = exchange(attend_back(data, exchange(mixed_grad, 4)), 5)
    input_grad, d_qkv, d_bias, d_pre = qkv_back(tokens, middle_grad, pre_gain, normed, grads, qkv, unselect)

    d_bias = d_bias.reshape(16, 256)[:, :240].reshape(1, 3840)
    d_bias = jnp.concatenate([d_bias[:, :1280], d_bias[:, 2560:]], axis=1)
    parts = (d_pre[0:1], d_pre[1:2], d_bias, d_mid[0:1], d_mid[1:2], d_mid[2:3], d_bias_fc.reshape(1, 5120), d_mid[3:4])
    vec = jnp.concatenate([v.astype(BF).reshape(128, n) for v, n in zip(parts, VECTOR_SIZES)], axis=1)
    vec = jnp.pad(vec, ((0, 0), (0, 72))).reshape(2, 4, 2, 4, 2, 2, 96).transpose(0, 1, 3, 4, 2, 5, 6)
    vec = jnp.pad(vec, ((0, 0),) * 5 + ((0, 78), (0, 0)))
    d_out = d_out.reshape(1280, 8, 160).transpose(1, 0, 2).reshape(2, 4, 4, 2, 2, 80, 160)
    d_out = jnp.concatenate([d_out, vec], axis=-1)
    shape = (2, 4, 4, 2, 2, 80)
    s_qkv, s_out, s_fc, s_pj = scatter((d_qkv.reshape(shape + (512,)), d_out, d_fc.reshape(shape + (640,)),
                                        d_pj.reshape(shape + (640,))))
    halves = [jnp.concatenate([s_fc[:, 320 * c:320 * c + 320], s_pj[:, 320 * c:320 * c + 320],
                               s_qkv[:, 256 * c:256 * c + 240], s_out[:, 80 * c:80 * c + 80]], axis=1) for c in range(2)]
    kept, sent = jnp.where(core == 0, halves[0], halves[1]), jnp.where(core == 0, halves[1], halves[0])
    got = lax.ppermute(sent, "dp", pairs)
    rows = jnp.concatenate([jnp.where(core == 0, kept, got), jnp.where(core == 0, got, kept)], axis=0)
    small = s_out[0:2, 160:256].reshape(192)
    ends = []
    at = 0
    for n in VECTOR_SIZES:
        ends.append(small[at:at + n])
        at += n
    return (block_out.reshape(2, 128, 1280), input_grad.reshape(2, 128, 1280), rows[:, 640:880], rows[:, 880:960],
            rows[:, 0:320], rows[:, 320:640].T) + tuple(ends)


def solution(mesh):
    weights = (P("ctx", "dp"), P("ctx", "dp"), P("ctx", "dp"), P("dp", "ctx"))
    vectors = (P(("dp", "ctx")),) * 8
    rows = P("dp", "ctx", None)
    return jax.shard_map(
        body,
        mesh=mesh,
        in_specs=(rows, P("dp", "ctx"), rows) + weights + vectors,
        out_specs=(rows, rows) + weights + vectors,
        check_vma=False,
    )
```

```python
import numpy as np
import jax
import jax.numpy as jnp
from jax import lax
from jax.experimental import pallas as pl
from jax.experimental.pallas import tpu as pltpu
from jax.sharding import PartitionSpec as P

MESH = pl.DeviceIdType.MESH
EPSILON = 1e-05
MASKED_VALUE = -1e30
BF = jnp.bfloat16
F32 = jnp.float32
MIB = 1024 * 1024
VMEM = pltpu.VMEM


def coords():
    dp = lax.axis_index("dp")
    ctx = lax.axis_index("ctx")
    core = lax.rem(dp, 2)
    z = lax.rem(lax.div(dp, 2), 4)
    y = lax.div(dp, 8) * 2 + lax.rem(ctx, 2)
    x = lax.div(ctx, 2)
    return dict(x=x, y=y, z=z), core


def device_of(pos, core):
    dp = (lax.div(pos["y"], 2) * 4 + pos["z"]) * 2 + core
    ctx = pos["x"] * 2 + lax.rem(pos["y"], 2)
    return (dp, ctx)


def shifted(pos, axis, by):
    return {**pos, axis: lax.rem(pos[axis] + by + 4, 4)}


def others_in_ctx():
    ctx = lax.axis_index("ctx")
    return [lax.rem(ctx + d, 8) for d in range(1, 8)]


def greet(pos, core, heads=False):
    barrier = pltpu.get_barrier_semaphore()
    devices = [device_of(shifted(pos, axis, by), core) for axis in "xyz" for by in (1, -1)]
    devices.append(device_of(pos, 1 - core))
    if heads:
        dp, ctx = lax.axis_index("dp"), lax.axis_index("ctx")
        lo = lax.rem(ctx, 2)
        across = lax.rem(pos["x"] + 2, 4) * 2
        devices.append((dp, across + lo))
        for by in (1, 2, 3):
            devices.append((dp, lax.rem(pos["x"] + by, 4) * 2 + 1 - lo))
    for device in devices:
        pl.semaphore_signal(barrier, inc=1, device_id=device, device_id_type=MESH)
    pl.semaphore_wait(barrier, len(devices))


class Sender:
    def __init__(self, send_sem, recv_sem):
        self.send_sem, self.recv_sem, self.started = send_sem, recv_sem, []

    def __call__(self, src, dst, device):
        i = len(self.started)
        copy = pltpu.make_async_remote_copy(src_ref=src, dst_ref=dst, send_sem=self.send_sem.at[i],
                                            recv_sem=self.recv_sem.at[i], device_id=device, device_id_type=MESH)
        copy.start()
        self.started.append(copy)
        return copy

    def finish(self):
        for copy in self.started:
            copy.wait_send()


ORDERS = {"A": "xyz", "B": "yzx", "C": "zxy"}
LANES = (512, 256, 640, 640)
ROUNDS = [
    [(0, "A", (0, 80), (0, 128)), (0, "B", (0, 80), (128, 256)), (0, "C", (0, 80), (256, 384)),
     (0, "A", (0, 32), (384, 512)), (0, "B", (32, 64), (384, 512)), (0, "C", (64, 80), (384, 512))],
    [(2, "A", (0, 80), (0, 384)), (2, "B", (0, 80), (384, 512)), (2, "C", (0, 80), (512, 640)),
     (1, "B", (0, 80), (0, 128)), (1, "C", (0, 80), (128, 256))],
    [(3, "A", (0, 80), (0, 256)), (3, "B", (0, 80), (256, 384)), (3, "C", (0, 80), (384, 640))],
]


def spans(where):
    out = {}
    for axis in "xz":
        v = where[axis]
        out[axis] = (0, 4) if v is None else ((v[1] * 2, 2) if isinstance(v, tuple) else (v, 1))
    v = where["y"]
    if v is None:
        hi, lo = (0, 2), (0, 2)
    elif isinstance(v, tuple):
        hi, lo = (v[1], 1), (0, 2)
    elif isinstance(v, int):
        hi, lo = (v // 2, 1), (v % 2, 1)
    else:
        hi, lo = (lax.div(v, 2), 1), (lax.rem(v, 2), 1)
    return (hi, out["z"], out["x"], lo)


def span_index(where):
    return tuple(s if n == 1 else pl.ds(s, n) for s, n in spans(where))


def part_slice(part):
    _, _, rows, lanes = part
    return (pl.ds(rows[0], rows[1] - rows[0]), pl.ds(lanes[0], lanes[1] - lanes[0]))


def where_of(pos, part, k, value, half=None):
    order = ORDERS[part[1]]
    where = {}
    for j, axis in enumerate(order):
        where[axis] = None if j < k else (value if j == k else pos[axis])
    if half is not None:
        where[order[k - 1]] = ("half", half)
    return where


class Gather:
    def __init__(self, pos, core, ins, bufs, send):
        self.pos, self.core, self.ins, self.bufs, self.send = pos, core, ins, bufs, send
        self.first, self.second = {}, {}
        self.pushes = {r: [] for r in range(len(ROUNDS))}

    def put(self, part, where, device, src=None):
        ref = self.bufs[part[0]].at[span_index(where) + (self.core,) + part_slice(part)]
        return self.send(ref if src is None else src, ref, device)

    def near(self, axis, by):
        return device_of(shifted(self.pos, axis, by), self.core)

    def partner(self):
        return device_of(self.pos, 1 - self.core)

    def step1(self, k, r):
        for part in ROUNDS[r]:
            axis = ORDERS[part[1]][k]
            where = where_of(self.pos, part, k, self.pos[axis])
            src = self.ins[part[0]].at[part_slice(part)] if k == 0 else None
            self.first[part, k] = (self.put(part, where, self.near(axis, 1), src),
                                   self.put(part, where, self.near(axis, -1), src))
            if k == 2:
                self.pushes[r].append(self.put(part, where, self.partner()))

    def step2(self, k, r):
        for part in ROUNDS[r]:
            axis = ORDERS[part[1]][k]
            right, left = self.first[part, k]
            below, above = (shifted(self.pos, axis, by)[axis] for by in (-1, 1))
            right.wait_recv()
            if k == 0:
                out = (self.put(part, where_of(self.pos, part, k, below), self.near(axis, 1)),)
                left.wait_recv()
            else:
                a = self.put(part, where_of(self.pos, part, k, below, 0), self.near(axis, 1))
                left.wait_recv()
                out = (a, self.put(part, where_of(self.pos, part, k, above, 1), self.near(axis, -1)))
            self.second[part, k] = out
            if k == 2:
                self.pushes[r].append(self.put(part, where_of(self.pos, part, k, below), self.partner()))
                self.pushes[r].append(self.put(part, where_of(self.pos, part, k, above), self.partner()))

    def step3(self, k, r):
        for part in ROUNDS[r]:
            axis = ORDERS[part[1]][k]
            for copy in self.second[part, k]:
                copy.wait_recv()
            if k == 2:
                across = shifted(self.pos, axis, 2)[axis]
                self.pushes[r].append(self.put(part, where_of(self.pos, part, k, across), self.partner()))

    def finish(self, r):
        for copy in self.pushes[r]:
            copy.wait_recv()


def dot(a, b):
    return jnp.dot(a, b, preferred_element_type=F32)


def dot_nt(a, b):
    return lax.dot_general(a, b, (((1,), (1,)), ((), ())), preferred_element_type=F32)


def dot_tn(a, b):
    return lax.dot_general(a, b, (((0,), (0,)), ((), ())), preferred_element_type=F32)


def turned(a):
    return a.astype(F32).T.astype(a.dtype)


def norm_parts(values):
    center = values - jnp.mean(values, axis=-1, keepdims=True)
    spread = jnp.mean(center * center, axis=-1, keepdims=True)
    r = lax.rsqrt(spread + EPSILON)
    return center * r, r


def norm_back(u, r, gain, e):
    n = e * gain
    dv = r * (n - jnp.mean(n, axis=-1, keepdims=True) - u * jnp.mean(n * u, axis=-1, keepdims=True))
    return dv, jnp.sum(e * u, axis=0, keepdims=True), jnp.sum(e, axis=0, keepdims=True)


VECTOR_ROWS = ((0,), (1,), (2, 3), (4,), (5,), (6,), (8, 9, 10, 11), (7,))


def selector():
    out = np.zeros((1024, 1152), np.float32)
    for m in range(3):
        for j in range(320):
            at = 320 * m + j
            out[(at // 240) * 256 + at % 240, 384 * m + j] = 1
    return out


def place_tables():
    c = np.arange(1280)
    plain = np.stack([c // 10, 0 * c, c % 10])
    c = np.arange(4096)
    off = c % 256
    n = 240 * (c // 256) + off
    e = np.where(n < 1280, n, n - 1280)
    unused = (off >= 240) | ((n >= 1280) & (n < 2560))
    qkv = np.stack([np.where(unused, -1, e // 20), 2 + (e % 20) // 10, e % 10])
    c = np.arange(5120)
    fc = np.stack([c // 40, 8 + (c % 40) // 10, c % 10])
    pad = lambda t: np.concatenate([t, np.zeros((5, t.shape[1]), t.dtype)]).astype(np.int32)
    return pad(plain), pad(qkv), pad(fc)


def row_owner(core):
    v = lax.broadcasted_iota(jnp.int32, (64, 1), 0)
    return (v // 8) * 16 + core * 8 + lax.rem(v, 8)


def row_picker(r):
    v = lax.broadcasted_iota(jnp.int32, (64, 1024), 0)
    c = lax.broadcasted_iota(jnp.int32, (64, 1024), 1)
    return (c == 16 * v + r).astype(F32).astype(BF)


def entry_picker(entry):
    lane = lax.broadcasted_iota(jnp.int32, (128, entry.shape[1]), 0)
    return (lane == 112 + entry).astype(F32).astype(BF)


def unpack_vectors(buf, plain, qkv, fc, vecs, bias_qkv, bias_fc):
    rows = []
    for h in range(2):
        tile = buf[:, :, :, :, h, 0:16, 256 * h + 128:256 * h + 256].reshape(1024, 128)
        rows.append([dot(row_picker(r), tile).astype(BF) for r in range(12)])

    def take(table, row_ids):
        n = table.shape[1]
        owner, row, entry = table[0:1], table[1:2], table[2:3]
        pick = entry_picker(entry)
        total = jnp.zeros((1, n), F32)
        for h in range(2):
            mine = row_owner(h)
            for r in row_ids:
                hit = (mine == owner) if len(row_ids) == 1 else ((mine == owner) & (row == r))
                total += jnp.sum(jnp.where(hit, dot(rows[h][r], pick), 0.0), axis=0, keepdims=True)
        return total

    for r in (0, 1, 4, 5, 6, 7):
        vecs[r:r + 1] = take(plain[...], (r,))
    for p in range(8):
        bias_qkv[p:p + 1] = take(qkv[:, 512 * p:512 * p + 512], (2, 3))
        bias_fc[p:p + 1] = take(fc[:, 640 * p:640 * p + 640], (8, 9, 10, 11))


def head_lanes(rows, half):
    lane = lax.broadcasted_iota(jnp.int32, (rows, 128), 1)
    return (lane < 64) if half == 0 else (lane >= 64)


def only(values, half):
    return jnp.where(head_lanes(values.shape[0], half), values, jnp.zeros_like(values))


def swapped(values):
    return pltpu.roll(values.astype(F32), 64, 1).astype(values.dtype)


def tile_of(data, a, b, t):
    return data[a:b, :, 128 * t:128 * t + 128].reshape(128 * (b - a), 128)


def segment_views(data):
    tile = tile_of(data, 0, 8, 7).astype(F32)
    return tile[:, 64:65], jnp.transpose(tile)[64:65, :]


def mask_of(column, row, i, wide):
    rows = lax.broadcasted_iota(jnp.int32, (256, wide), 0) + 256 * i
    cols = lax.broadcasted_iota(jnp.int32, (256, wide), 1)
    keep = (cols <= rows) & (column[256 * i:256 * i + 256] == row[:, :wide])
    return jnp.where(keep, 0.0, MASKED_VALUE)


def head_tiles(data, i, j):
    n = 2 * i + 2
    if j < 2:
        return tile_of(data, 2 * i, n, j), tile_of(data, 0, n, 2 + j), tile_of(data, 0, n, 4 + j)
    return tile_of(data, 2 * i, n, 6), swapped(tile_of(data, 0, n, 6)), tile_of(data, 0, n, 7)


def attend_block(data, mixed, column, row, i):
    wide = 256 * (i + 1)
    hide = mask_of(column, row, i, wide)
    for j in range(3):
        q, k, v = head_tiles(data, i, j)
        total = None
        for half in range(2 if j < 2 else 1):
            scores = dot_nt(only(q, half) * jnp.asarray(0.125, BF), k) + hide
            e = jnp.exp(scores - jnp.max(scores, axis=-1, keepdims=True))
            soft = (e / jnp.sum(e, axis=-1, keepdims=True)).astype(BF)
            part = dot(soft, only(v, half))
            total = part if total is None else total + part
        mixed[2 * i:2 * i + 2, :, 128 * j:128 * j + 128] = total.astype(BF).reshape(2, 128, 128)


def front_kernel(qkv_in, out_in, fc_in, pj_in, tokens, seg, select, plain, qkv_table, fc_table,
                 qkv_all, out_all, fc_all, pj_all, normed, data_all, mixed_all, vecs, bias_fc,
                 qkv, bias_qkv, packed, sent, data, mixed_sent, mixed, send_sem, recv_sem, local_sem):
    pos, core = coords()
    dp, ctx = lax.axis_index("dp"), lax.axis_index("ctx")
    send = Sender(send_sem, recv_sem)
    here = tuple(s for s, _ in spans(pos)) + (core,)
    local = [pltpu.make_async_copy(src, dst.at[here], local_sem.at[n])
             for n, (src, dst) in enumerate([(qkv_in, qkv), (out_in, out_all), (fc_in, fc_all), (pj_in, pj_all)])]
    for copy in local:
        copy.start()
    greet(pos, core, heads=True)
    g = Gather(pos, core, (qkv_in, out_in, fc_in, pj_in), (qkv, out_all, fc_all, pj_all), send)
    g.step1(0, 0)
    g.step1(0, 1)
    g.step1(0, 2)
    for copy in local:
        copy.wait()
    g.step2(0, 0)
    g.step3(0, 0)
    g.step1(1, 0)
    g.step2(0, 1)
    g.step2(0, 2)
    g.step2(1, 0)
    g.step3(0, 1)
    g.step1(1, 1)
    g.step3(1, 0)
    g.step1(2, 0)
    g.step3(0, 2)
    g.step1(1, 2)
    g.step2(1, 1)
    g.step2(1, 2)
    g.step2(2, 0)
    g.step3(1, 1)
    g.step1(2, 1)
    u, _ = norm_parts(tokens[...].astype(F32))
    g.step3(2, 0)
    g.step3(1, 2)
    g.step1(2, 2)
    g.finish(0)

    keep = pltpu.make_async_copy(qkv, qkv_all, local_sem.at[0])
    keep.start()
    unpack_vectors(qkv, plain, qkv_table, fc_table, vecs, bias_qkv, bias_fc)
    normed[...] = (u * vecs[0:1] + vecs[1:2]).astype(BF)

    def project(p, carry):
        w = qkv[lax.div(p, 4), lax.rem(p, 4)].reshape(1280, 512)
        packed[p] = (dot(normed[...], w) + bias_qkv[pl.ds(p, 1)]).astype(BF)
        return carry

    lax.fori_loop(0, 8, project, 0)
    for i in range(4):
        wide = jnp.concatenate([packed[2 * i], packed[2 * i + 1]], axis=1)
        chunks = dot(wide, select[...])
        for m in range(3):
            n = 3 * i + m
            kind, group = n // 4, n % 4
            low = chunks[:, 384 * m:384 * m + 256].astype(BF)
            last = chunks[:, 384 * m + 256:384 * m + 384]
            if kind == 1:
                last = pltpu.roll(last, 64, 1)
            last = last.astype(BF)
            for s in range(2):
                at = s * 4 + group
                rows = slice(128 * s, 128 * s + 128)
                sent[at, :, 256 * kind:256 * kind + 256] = low[rows]
                if kind == 0:
                    sent[at, :, 768:896] = last[rows]
                elif kind == 1:
                    sent[at, :, 768:896] = sent[at, :, 768:896] + last[rows]
                else:
                    sent[at, :, 896:1024] = last[rows] + seg[rows]
    others = others_in_ctx()
    first = [send(sent.at[o], data.at[ctx], (dp, o)) for o in others]
    own = pltpu.make_async_copy(sent.at[ctx], data.at[ctx], local_sem.at[1])
    own.start()
    g.step2(2, 1)
    own.wait()
    for copy in first:
        copy.wait_recv()
    keep_data = pltpu.make_async_copy(data, data_all, local_sem.at[1])
    keep_data.start()
    column, row = segment_views(data)
    for i in range(4):
        attend_block(data, mixed_sent, column, row, i)
        if i == 1:
            g.step2(2, 2)
    second = [send(mixed_sent.at[o], mixed.at[ctx], (dp, o)) for o in others]
    own = pltpu.make_async_copy(mixed_sent.at[ctx], mixed.at[ctx], local_sem.at[2])
    own.start()
    g.step3(2, 1)
    g.step3(2, 2)
    own.wait()
    for copy in second:
        copy.wait_recv()
    keep_mixed = pltpu.make_async_copy(mixed, mixed_all, local_sem.at[2])
    keep_mixed.start()
    g.finish(1)
    g.finish(2)
    keep.wait()
    keep_data.wait()
    keep_mixed.wait()
    send.finish()


FRONT_SENDS = 16 * sum(len(r) for r in ROUNDS) + 14


def front(blocks, tokens, seg, select, plain, qkv_table, fc_table):
    sds = jax.ShapeDtypeStruct
    whole = pl.BlockSpec(memory_space=pl.ANY)
    near = pl.BlockSpec(memory_space=VMEM)
    return pl.pallas_call(
        front_kernel,
        out_shape=[sds((2, 4, 4, 2, 2, 80, n), BF) for n in LANES] + [
            sds((256, 1280), BF), sds((8, 128, 1024), BF), sds((8, 128, 384), BF), sds((8, 1280), F32), sds((8, 640), F32)],
        in_specs=[near, whole, whole, whole] + [near] * 6,
        out_specs=[whole] * 4 + [near, whole, whole, near, near],
        scratch_shapes=[
            VMEM((2, 4, 4, 2, 2, 80, 512), BF), VMEM((8, 512), F32), VMEM((8, 256, 512), BF), VMEM((8, 128, 1024), BF),
            VMEM((8, 128, 1024), BF), VMEM((8, 128, 384), BF), VMEM((8, 128, 384), BF),
            pltpu.SemaphoreType.DMA((FRONT_SENDS,)), pltpu.SemaphoreType.DMA((FRONT_SENDS,)), pltpu.SemaphoreType.DMA((4,)),
        ],
        compiler_params=pltpu.CompilerParams(collective_id=0, has_side_effects=True, vmem_limit_bytes=60 * MIB),
        name="fetch_and_attend",
    )(*blocks, tokens, seg, select, plain, qkv_table, fc_table)


def attend_back_block(data, grad, out, dk, dv, column, row, i):
    wide = 256 * (i + 1)
    hide = mask_of(column, row, i, wide)
    for j in range(3):
        q, k, v = head_tiles(data, i, j)
        q = q * jnp.asarray(0.125, BF)
        lanes = slice(128 * j, 128 * j + 128)
        g = grad[2 * i:2 * i + 2, :, lanes].reshape(256, 128)
        total = None
        for half in range(2 if j < 2 else 1):
            qh, gh = only(q, half), only(g, half)
            scores = dot_nt(qh, k) + hide
            e = jnp.exp(scores - jnp.max(scores, axis=-1, keepdims=True))
            soft = e / jnp.sum(e, axis=-1, keepdims=True)
            dv[0:wide, lanes] += dot_tn(soft.astype(BF), gh)
            sg = dot_nt(gh, v)
            sg = (soft * (sg - jnp.sum(soft * sg, axis=-1, keepdims=True))).astype(BF)
            dk[0:wide, lanes] += dot_tn(sg, qh)
            part = dot(sg, only(k, half)) * 0.125
            total = part if total is None else total + part
        t = j if j < 2 else 6
        out[2 * i:2 * i + 2, :, 128 * t:128 * t + 128] = total.astype(BF).reshape(2, 128, 128)


def attend_back_end(out, dk, dv):
    for j in range(2):
        lanes = slice(128 * j, 128 * j + 128)
        out[:, :, 256 + 128 * j:384 + 128 * j] = dk[:, lanes].astype(BF).reshape(8, 128, 128)
        out[:, :, 512 + 128 * j:640 + 128 * j] = dv[:, lanes].astype(BF).reshape(8, 128, 128)
    last = pltpu.roll(dk[:, 256:384], 64, 1).astype(BF).reshape(8, 128, 128)
    out[:, :, 768:896] = out[:, :, 768:896] + last
    out[:, :, 896:1024] = dv[:, 256:384].astype(BF).reshape(8, 128, 128)


class Scatter:
    def __init__(self, pos, core, sums, slots, outs, send, rounds):
        self.pos, self.core, self.sums, self.slots, self.outs, self.send = pos, core, sums, slots, outs, send
        self.rounds, self.first, self.second = rounds, {}, {}

    def near(self, axis, by):
        return device_of(shifted(self.pos, axis, by), self.core)

    def slot_of(self, part, k, slot, half=None):
        order = ORDERS[part[1]]
        where = {}
        for j, axis in enumerate(order):
            where[axis] = None if j < k else (slot if j == k else 3)
        if half is not None:
            where[order[k - 1]] = ("half", half)
        return where

    def sum_at(self, t, idx):
        ref, halves = self.sums[t]
        return ref, (idx + (self.core,) if halves else idx)

    def sum_view(self, part, where):
        ref, idx = self.sum_at(part[0], span_index(where))
        return ref.at[idx + part_slice(part)]

    def slot_view(self, part, where):
        return self.slots[part[0]].at[span_index(where) + part_slice(part)]

    def each(self, where_to, where_from, body):
        to, frm = spans(where_to), spans(where_from)
        total = 1
        for _, n in to:
            total *= n

        def step(i, carry):
            a, b = [], []
            left = i
            for (s, n), (t, m) in zip(reversed(to), reversed(frm)):
                if n == 1:
                    a.append(s)
                    b.append(t)
                else:
                    d = lax.rem(left, n)
                    left = lax.div(left, n)
                    a.append(s + d)
                    b.append(t + d)
            body(tuple(reversed(a)), tuple(reversed(b)))
            return carry

        if total == 1:
            step(0, 0)
        else:
            lax.fori_loop(0, total, step, 0)

    def add_slot(self, part, where, slot):
        def body(a, b):
            ref, idx = self.sum_at(part[0], a)
            here = idx + part_slice(part)
            ref[here] = ref[here] + self.slots[part[0]][b + part_slice(part)]

        self.each(where, slot, body)

    def step1(self, k, r):
        for part in self.rounds[r]:
            axis = ORDERS[part[1]][k]
            across = shifted(self.pos, axis, 2)[axis]

            def out(half, by):
                return self.send(self.sum_view(part, where_of(self.pos, part, k, across, half)),
                                 self.slot_view(part, self.slot_of(part, k, 0, half)), self.near(axis, by))

            self.first[part, k] = (out(None, 1),) if k == 0 else (out(0, 1), out(1, -1))

    def step2(self, k, r):
        for part in self.rounds[r]:
            axis = ORDERS[part[1]][k]
            above, below = (shifted(self.pos, axis, by)[axis] for by in (1, -1))
            first = self.first[part, k]
            half = (None, None) if k == 0 else (0, 1)
            first[0].wait_recv()
            self.add_slot(part, where_of(self.pos, part, k, above, half[0]), self.slot_of(part, k, 0, half[0]))
            a = self.send(self.sum_view(part, where_of(self.pos, part, k, above)),
                          self.slot_view(part, self.slot_of(part, k, 1)), self.near(axis, 1))
            if k != 0:
                first[1].wait_recv()
                self.add_slot(part, where_of(self.pos, part, k, below, 1), self.slot_of(part, k, 0, 1))
            b = self.send(self.sum_view(part, where_of(self.pos, part, k, below)),
                          self.slot_view(part, self.slot_of(part, k, 2)), self.near(axis, -1))
            self.second[part, k] = (a, b)

    def step3(self, k, r):
        for part in self.rounds[r]:
            t = part[0]
            axis = ORDERS[part[1]][k]
            for copy in self.second[part, k]:
                copy.wait_recv()
            one, two = spans(self.slot_of(part, k, 1)), spans(self.slot_of(part, k, 2))
            gap = tuple(v[0] - u[0] for u, v in zip(one, two))
            cut = part_slice(part)

            def body(a, b):
                ref, idx = self.sum_at(t, a)
                b2 = tuple(u + v for u, v in zip(b, gap))
                total = (ref[idx + cut].astype(F32) + self.slots[t][b + cut].astype(F32)
                         + self.slots[t][b2 + cut].astype(F32))
                if k == 0:
                    self.outs[t][cut] = total
                else:
                    ref[idx + cut] = total.astype(BF)

            self.each(where_of(self.pos, part, k, self.pos[axis]), self.slot_of(part, k, 1), body)


class Pairs:
    def __init__(self, scatter, grads, stages, stage_sem, order):
        self.s, self.grads, self.stages, self.stage_sem, self.order = scatter, grads, stages, stage_sem, order
        self.pushed, self.loads = {}, {}

    def where(self, part, which):
        axis = ORDERS[part[1]][2]
        return where_of(self.s.pos, part, 2, shifted(self.s.pos, axis, which)[axis])

    def stage_names(self, r):
        seen = {}
        for part in self.s.rounds[r]:
            n = seen.get(part[1], 0)
            seen[part[1]] = n + 1
            yield part, part[1] + str(n)

    def push_all(self):
        s = self.s
        for r, which in self.order:
            for part in s.rounds[r]:
                where = self.where(part, which)
                src = self.grads[part[0]].at[span_index(where) + (1 - s.core,) + part_slice(part)]
                self.pushed[part, which] = s.send(src, s.sum_view(part, where), device_of(s.pos, 1 - s.core))

    def load(self, n):
        if n >= len(self.order):
            return
        r, which = self.order[n]
        for j, (part, name) in enumerate(self.stage_names(r)):
            src = self.grads[part[0]].at[span_index(self.where(part, which)) + (self.s.core,) + part_slice(part)]
            dst = self.stages[name].at[n % 2].at[..., pl.ds(0, part[3][1] - part[3][0])]
            copy = pltpu.make_async_copy(src, dst, self.stage_sem.at[n % 2, j])
            copy.start()
            self.loads[n, part] = copy

    def add(self, n):
        r, which = self.order[n]
        s = self.s
        for part, name in self.stage_names(r):
            self.loads[n, part].wait()
            self.pushed[part, which].wait_recv()
            where = self.where(part, which)
            zero = {axis: (None if v is None else 0) for axis, v in where.items()}
            dims = [d for d, (_, m) in enumerate(spans(where)) if m != 1]
            stage = self.stages[name]
            width = part[3][1] - part[3][0]

            def body(a, b):
                ref, idx = s.sum_at(part[0], a)
                here = idx + part_slice(part)
                ref[here] = ref[here] + stage[(n % 2,) + tuple(b[d] for d in dims) + (slice(None), pl.ds(0, width))]

            s.each(where, zero, body)
        self.load(n + 2)


BACK_ROUNDS = {1: ROUNDS[1], 2: ROUNDS[2]}
BACK_ORDER = [(1, 2), (1, 1), (1, -1), (2, 2), (2, 1), (2, -1), (1, 0), (2, 0)]
STAGES = {"A0": (2, 4, 2, 80, 384), "B0": (2, 4, 2, 80, 128), "B1": (2, 4, 2, 80, 128),
          "C0": (4, 4, 80, 256), "C1": (4, 4, 80, 128)}


def back_kernel(d_out, d_fc, d_pj, mixed_grad, data, s_out, s_fc, s_pj, grads_all,
                sum_out, sum_fc, sum_pj, slot_out, slot_fc, slot_pj, *rest):
    stages = dict(zip(sorted(STAGES), rest[:5]))
    grad, sent, grads, dk, dv, send_sem, recv_sem, stage_sem, local_sem = rest[5:]
    pos, core = coords()
    dp, ctx = lax.axis_index("dp"), lax.axis_index("ctx")
    send = Sender(send_sem, recv_sem)
    s = Scatter(pos, core, {1: (sum_out, False), 2: (sum_fc, False), 3: (sum_pj, False)},
                {1: slot_out, 2: slot_fc, 3: slot_pj}, {1: s_out, 2: s_fc, 3: s_pj}, send, BACK_ROUNDS)
    pairs = Pairs(s, {1: d_out, 2: d_fc, 3: d_pj}, stages, stage_sem, BACK_ORDER)
    pairs.load(0)
    pairs.load(1)
    own = pltpu.make_async_copy(mixed_grad.at[ctx], grad.at[ctx], local_sem.at[0])
    own.start()
    greet(pos, core, heads=True)
    others = others_in_ctx()
    first = [send(mixed_grad.at[o], grad.at[ctx], (dp, o)) for o in others]
    pairs.push_all()
    dk[...] = jnp.zeros_like(dk)
    dv[...] = jnp.zeros_like(dv)
    column, row = segment_views(data)
    pairs.add(0)
    s.step1(2, 1)
    pairs.add(1)
    pairs.add(2)
    own.wait()
    for copy in first:
        copy.wait_recv()
    attend_back_block(data, grad, sent, dk, dv, column, row, 0)
    pairs.add(3)
    s.step1(2, 2)
    attend_back_block(data, grad, sent, dk, dv, column, row, 1)
    s.step2(2, 1)
    pairs.add(4)
    pairs.add(5)
    attend_back_block(data, grad, sent, dk, dv, column, row, 2)
    s.step2(2, 2)
    pairs.add(6)
    attend_back_block(data, grad, sent, dk, dv, column, row, 3)
    attend_back_end(sent, dk, dv)
    second = [send(sent.at[o], grads.at[ctx], (dp, o)) for o in others]
    own = pltpu.make_async_copy(sent.at[ctx], grads.at[ctx], local_sem.at[0])
    own.start()
    s.step3(2, 1)
    s.step1(1, 1)
    pairs.add(7)
    s.step2(1, 1)
    s.step3(2, 2)
    s.step1(1, 2)
    s.step3(1, 1)
    s.step1(0, 1)
    s.step2(1, 2)
    s.step2(0, 1)
    s.step3(1, 2)
    s.step1(0, 2)
    s.step3(0, 1)
    s.step2(0, 2)
    s.step3(0, 2)
    own.wait()
    for copy in second:
        copy.wait_recv()
    keep = pltpu.make_async_copy(grads, grads_all, local_sem.at[0])
    keep.start()
    keep.wait()
    send.finish()


BACK_SENDS = 14 + sum(15 * len(r) for r in BACK_ROUNDS.values())


def back(d_out, d_fc, d_pj, mixed_grad, data):
    sds = jax.ShapeDtypeStruct
    whole = pl.BlockSpec(memory_space=pl.ANY)
    near = pl.BlockSpec(memory_space=VMEM)
    big = [VMEM((2, 4, 4, 2, 80, n), BF) for n in LANES[1:]]
    return pl.pallas_call(
        back_kernel,
        out_shape=[sds((80, n), F32) for n in LANES[1:]] + [sds((8, 128, 1024), BF)],
        in_specs=[whole] * 4 + [near],
        out_specs=[near] * 3 + [whole],
        scratch_shapes=big + big + [VMEM((2,) + STAGES[n], BF) for n in sorted(STAGES)] + [
            VMEM((8, 128, 384), BF), VMEM((8, 128, 1024), BF), VMEM((8, 128, 1024), BF),
            VMEM((1024, 384), F32), VMEM((1024, 384), F32),
            pltpu.SemaphoreType.DMA((BACK_SENDS,)), pltpu.SemaphoreType.DMA((BACK_SENDS,)),
            pltpu.SemaphoreType.DMA((2, 5)), pltpu.SemaphoreType.DMA((1,)),
        ],
        compiler_params=pltpu.CompilerParams(collective_id=1, has_side_effects=True, vmem_limit_bytes=62 * MIB),
        name="attend_back_and_scatter",
    )(d_out, d_fc, d_pj, mixed_grad, data)


def pack_vectors(plain, qkv, fc, d_pre, d_bias_qkv, d_mid, d_bias_fc):
    out = []
    for h in range(2):
        mine = row_owner(h)
        rows = {}

        def give(table, values, row_ids):
            owner, row, entry = table[0:1], table[1:2], table[2:3]
            pick = entry_picker(entry)
            low = values.astype(BF).astype(F32)
            for r in row_ids:
                hit = (mine == owner) if len(row_ids) == 1 else ((mine == owner) & (row == r))
                part = dot_nt(jnp.where(hit, low, 0.0).astype(BF), pick)
                rows[r] = rows[r] + part if r in rows else part

        for r, values in ((0, d_pre[0]), (1, d_pre[1]), (4, d_mid[0:1]), (5, d_mid[1:2]), (6, d_mid[2:3]), (7, d_mid[3:4])):
            give(plain[...], values, (r,))
        for p in range(8):
            give(qkv[:, 512 * p:512 * p + 512], d_bias_qkv[p:p + 1], (2, 3))
            give(fc[:, 640 * p:640 * p + 640], d_bias_fc[p:p + 1], (8, 9, 10, 11))
        total = jnp.zeros((1024, 128), F32)
        for r in range(12):
            total += dot_tn(row_picker(r), rows[r].astype(BF))
        out.append(total.astype(BF))
    return out


def end_kernel(tokens, middle_grad, vecs, normed, grads, w_all, unselect, plain, qkv_table, fc_table, d_mid, d_bias_fc,
               input_grad, s_qkv, packed, normed_t, d_bias, extra, w, d_w, got, slot, send_sem, recv_sem, w_sem):
    pos, core = coords()
    send = Sender(send_sem, recv_sem)
    s = Scatter(pos, core, {0: (d_w, True)}, {0: slot}, {0: s_qkv}, send, {0: ROUNDS[0]})

    def fetch(p):
        copy = pltpu.make_async_copy(w_all.at[p // 4, p % 4], w.at[p % 2], w_sem.at[p % 2])
        copy.start()
        return copy

    loads = {0: fetch(0), 1: fetch(1)}
    greet(pos, core)
    normed_t[...] = turned(normed[...])
    for i in range(4):
        chunks = []
        for m in range(3):
            n = 3 * i + m
            kind, group = n // 4, n % 4

            def tile(t):
                return jnp.concatenate([grads[group, :, 128 * t:128 * t + 128], grads[4 + group, :, 128 * t:128 * t + 128]],
                                       axis=0)

            chunks += [tile(2 * kind), tile(2 * kind + 1), swapped(tile(6)) if kind == 1 else tile(6 if kind == 0 else 7)]
        wide = dot(jnp.concatenate(chunks, axis=1), unselect[...]).astype(BF)
        packed[2 * i] = wide[:, 0:512]
        packed[2 * i + 1] = wide[:, 512:1024]
    total = jnp.zeros((256, 1280), F32)
    for p in range(8):
        loads[p].wait()
        total += dot_nt(packed[p], w[p % 2].reshape(1280, 512))
        if p + 2 < 8:
            loads[p + 2] = fetch(p + 2)
        d_bias[p:p + 1] = jnp.sum(packed[p].astype(F32), axis=0, keepdims=True)
    u, r = norm_parts(tokens[...].astype(F32))
    dv, dg, db = norm_back(u, r, vecs[0:1], total)
    input_grad[...] = middle_grad[...] + dv
    for h, part in enumerate(pack_vectors(plain, qkv_table, fc_table, (dg, db), d_bias, d_mid, d_bias_fc)):
        extra[h] = part
    pushed = []
    for p in range(8):
        hi, z = p // 4, p % 4
        d_w[hi, z] = dot(normed_t[...], packed[p]).astype(BF).reshape(4, 2, 2, 80, 512)
        for h in range(2):
            lanes = slice(256 * h + 128, 256 * h + 256)
            d_w[hi, z, :, :, h, 0:16, lanes] = (d_w[hi, z, :, :, h, 0:16, lanes]
                                               + extra[h, 128 * p:128 * p + 128].reshape(4, 2, 16, 128))
        pushed.append(send(d_w.at[hi, z, :, :, 1 - core], got.at[hi, z], device_of(pos, 1 - core)))
    for p in range(8):
        hi, z = p // 4, p % 4
        pushed[p].wait_recv()

        def add(i, carry):
            x, lo = lax.div(i, 2), lax.rem(i, 2)
            d_w[hi, z, x, lo, core] = d_w[hi, z, x, lo, core] + got[hi, z, x, lo]
            return carry

        lax.fori_loop(0, 8, add, 0)
    for k in (2, 1, 0):
        s.step1(k, 0)
        s.step2(k, 0)
        s.step3(k, 0)
    send.finish()


END_SENDS = 8 + 11 * len(ROUNDS[0])


def end(tokens, middle_grad, vecs, normed, grads, w_all, unselect, plain, qkv_table, fc_table, d_mid, d_bias_fc):
    sds = jax.ShapeDtypeStruct
    whole = pl.BlockSpec(memory_space=pl.ANY)
    near = pl.BlockSpec(memory_space=VMEM)
    return pl.pallas_call(
        end_kernel,
        out_shape=[sds((256, 1280), F32), sds((80, 512), F32)],
        in_specs=[near] * 5 + [whole] + [near] * 6,
        out_specs=[near] * 2,
        scratch_shapes=[
            VMEM((8, 256, 512), BF), VMEM((1280, 256), BF), VMEM((8, 512), F32), VMEM((2, 1024, 128), BF),
            VMEM((2, 4, 2, 2, 80, 512), BF), VMEM((2, 4, 4, 2, 2, 80, 512), BF), VMEM((2, 4, 4, 2, 80, 512), BF),
            VMEM((2, 4, 4, 2, 80, 512), BF),
            pltpu.SemaphoreType.DMA((END_SENDS,)), pltpu.SemaphoreType.DMA((END_SENDS,)), pltpu.SemaphoreType.DMA((2,)),
        ],
        compiler_params=pltpu.CompilerParams(collective_id=2, has_side_effects=True, vmem_limit_bytes=60 * MIB),
        name="qkv_back_and_scatter",
    )(tokens, middle_grad, vecs, normed, grads, w_all, unselect, plain, qkv_table, fc_table, d_mid, d_bias_fc)


GELU_A = 0.7978845608028654
GELU_B = 0.044715


def joined(mixed, s):
    return jnp.concatenate([mixed[4 * s + g, :, 0:320] for g in range(4)], axis=1)


def feed_kernel(tokens, cotangent, mixed, w_out, vecs, fc, pj, bias_fc,
                block_out, middle_grad, mixed_grad, d_fc, d_pj, d_out, d_bias_fc, d_vec,
                middle, a2, a2_t, bg_t, mixed_t, out_sum, a2_sum):
    p = pl.program_id(0)

    @pl.when(p == 0)
    def _():
        rows = jnp.concatenate([joined(mixed, 0), joined(mixed, 1)], axis=0)
        mixed_t[...] = turned(rows)
        parts = [dot(rows, w_out[n])[:, 0:160] for n in range(8)]
        total = tokens[...].astype(F32) + (jnp.concatenate(parts, axis=1) + vecs[4:5])
        middle[...] = total
        u, _ = norm_parts(total)
        low = (u * vecs[5:6] + vecs[6:7]).astype(BF)
        a2[...] = low
        a2_t[...] = turned(low)
        bg_t[...] = turned(cotangent[...])
        out_sum[...] = jnp.zeros_like(out_sum)
        a2_sum[...] = jnp.zeros_like(a2_sum)

    pre = dot(a2[...], fc[0]) + bias_fc[pl.ds(p, 1)]
    square = pre * pre
    t = jnp.tanh(GELU_A * (pre + GELU_B * pre * square))
    act = (0.5 * pre * (1.0 + t)).astype(BF)
    slope = 0.5 * (1.0 + t) + 0.5 * pre * (1.0 - t * t) * (GELU_A * (1.0 + 3.0 * GELU_B * square))
    out_sum[...] += dot_nt(act, pj[0])
    d_pj[0] = dot(bg_t[...], act).astype(BF)
    pre_grad = (slope * dot(cotangent[...], pj[0])).astype(BF)
    d_bias_fc[pl.ds(p, 1)] = jnp.sum(pre_grad.astype(F32), axis=0, keepdims=True)
    d_fc[0] = dot(a2_t[...], pre_grad).astype(BF)
    a2_sum[...] += dot_nt(pre_grad, fc[0])

    @pl.when(p == 7)
    def _():
        block_out[...] = (middle[...] + (out_sum[...] + vecs[7:8])).astype(BF)
        u, r = norm_parts(middle[...])
        dv, dg, db = norm_back(u, r, vecs[5:6], a2_sum[...])
        c = cotangent[...].astype(F32)
        total = c + dv
        middle_grad[...] = total
        low = total.astype(BF)
        d_vec[0:1] = jnp.sum(low.astype(F32), axis=0, keepdims=True)
        d_vec[1:2] = dg
        d_vec[2:3] = db
        d_vec[3:4] = jnp.sum(c, axis=0, keepdims=True)
        back_sum = jnp.zeros((256, 1280), F32)
        for n in range(8):
            mine = jnp.concatenate([low[:, 160 * n:160 * n + 160], jnp.zeros((256, 96), BF)], axis=1)
            d_out[n] = dot(mixed_t[...], mine).astype(BF)
            back_sum += dot_nt(mine, w_out[n])
        back_low = back_sum.astype(BF)
        for g in range(4):
            rows = jnp.concatenate([back_low[:, 320 * g:320 * g + 320], jnp.zeros((256, 64), BF)], axis=1)
            for s in range(2):
                mixed_grad[s * 4 + g] = rows[s * 128:(s + 1) * 128]


def feed(tokens, cotangent, mixed, w_out, vecs, fc, pj, bias_fc):
    full = lambda *shape: pl.BlockSpec(shape, lambda p: (0,) * len(shape))
    step = lambda *shape: pl.BlockSpec((1,) + shape, lambda p: (p,) + (0,) * len(shape))
    sds = jax.ShapeDtypeStruct
    return pl.pallas_call(
        feed_kernel,
        grid=(8,),
        in_specs=[full(256, 1280), full(256, 1280), full(8, 128, 384), full(8, 1280, 256), full(8, 1280),
                  step(1280, 640), step(1280, 640), full(8, 640)],
        out_specs=[full(256, 1280), full(256, 1280), full(8, 128, 384), step(1280, 640), step(1280, 640),
                   full(8, 1280, 256), full(8, 640), full(4, 1280)],
        out_shape=[sds((256, 1280), BF), sds((256, 1280), F32), sds((8, 128, 384), BF), sds((8, 1280, 640), BF),
                   sds((8, 1280, 640), BF), sds((8, 1280, 256), BF), sds((8, 640), F32), sds((4, 1280), F32)],
        scratch_shapes=[VMEM((256, 1280), F32), VMEM((256, 1280), BF), VMEM((1280, 256), BF), VMEM((1280, 256), BF),
                        VMEM((1280, 256), BF), VMEM((256, 1280), F32), VMEM((256, 1280), F32)],
        compiler_params=pltpu.CompilerParams(vmem_limit_bytes=60 * MIB),
        name="feed_forward_and_back",
    )(tokens, cotangent, mixed, w_out, vecs, fc, pj, bias_fc)


def body(tokens, segments, cotangent, w_qkv, w_out, w_fc, w_proj, *vectors):
    core = lax.rem(lax.axis_index("dp"), 2)
    pairs = [(i, i ^ 1) for i in range(16)]
    rows = jnp.concatenate(
        [vectors[n].reshape(-1, 10) for n in (0, 1, 2, 3, 4, 5, 7, 6)] + [jnp.zeros((4, 10), BF)], axis=0)
    rows = jnp.pad(rows, ((0, 64), (0, 6)))
    rows = jnp.where(core == 0, jnp.concatenate([rows, jnp.zeros_like(rows)], axis=0),
                     jnp.concatenate([jnp.zeros_like(rows), rows], axis=0))
    mine = jnp.concatenate([w_fc, w_proj.T, w_qkv, rows, w_out, jnp.zeros((160, 48), BF)], axis=1)
    mine = mine.reshape(2, 80, 1024)
    kept = lax.dynamic_index_in_dim(mine, core, 0, False)
    got = lax.ppermute(lax.dynamic_index_in_dim(mine, 1 - core, 0, False), "dp", pairs)
    one, two = jnp.where(core == 0, kept, got), jnp.where(core == 0, got, kept)
    blocks = (
        jnp.concatenate([one[:, 640:896], two[:, 640:896]], axis=1),
        jnp.concatenate([one[:, 896:976], two[:, 896:976], jnp.zeros((80, 96), BF)], axis=1),
        jnp.concatenate([one[:, 0:320], two[:, 0:320]], axis=1),
        jnp.concatenate([one[:, 320:640], two[:, 320:640]], axis=1),
    )
    table = selector()
    select = jnp.asarray(table, BF)
    unselect = jnp.asarray(table.T, BF)
    plain, qkv_table, fc_table = (jnp.asarray(t) for t in place_tables())
    tokens = tokens.reshape(256, 1280)
    cotangent = cotangent.reshape(256, 1280)
    seg = jnp.pad(jnp.broadcast_to(segments.reshape(256, 1).astype(BF), (256, 64)), ((0, 0), (64, 0)))
    qkv, out, fc, pj, normed, data, mixed, vecs, bias_fc = front(blocks, tokens, seg, select, plain, qkv_table, fc_table)
    (block_out, middle_grad, mixed_grad, d_fc, d_pj, d_out, d_bias_fc, d_mid) = feed(
        tokens, cotangent, mixed, out.reshape(8, 1280, 256), vecs, fc.reshape(8, 1280, 640), pj.reshape(8, 1280, 640), bias_fc)
    shape = (2, 4, 4, 2, 2, 80)
    s_out, s_fc, s_pj, grads = back(d_out.reshape(shape + (256,)), d_fc.reshape(shape + (640,)), d_pj.reshape(shape + (640,)),
                                    mixed_grad, data)
    input_grad, s_qkv = end(tokens, middle_grad, vecs, normed, grads, qkv, unselect, plain, qkv_table, fc_table, d_mid,
                            d_bias_fc)
    halves = [jnp.concatenate([s_fc[:, 320 * c:320 * c + 320], s_pj[:, 320 * c:320 * c + 320],
                               s_qkv[:, 256 * c:256 * c + 240], s_out[:, 80 * c:80 * c + 80]], axis=1) for c in range(2)]
    kept, sent = jnp.where(core == 0, halves[0], halves[1]), jnp.where(core == 0, halves[1], halves[0])
    got = lax.ppermute(sent, "dp", pairs)
    rows = jnp.concatenate([jnp.where(core == 0, kept, got), jnp.where(core == 0, got, kept)], axis=0)
    small = jnp.where(core == 0, s_qkv[0:16, 240:250], s_qkv[0:16, 496:506])
    ends = tuple(small[ids[0]:ids[-1] + 1].reshape(-1) for ids in VECTOR_ROWS)
    return (block_out.reshape(2, 128, 1280), input_grad.reshape(2, 128, 1280), rows[:, 640:880], rows[:, 880:960],
            rows[:, 0:320], rows[:, 320:640].T) + ends


def solution(mesh):
    weights = (P("ctx", "dp"), P("ctx", "dp"), P("ctx", "dp"), P("dp", "ctx"))
    vectors = (P(("dp", "ctx")),) * 8
    rows = P("dp", "ctx", None)
    return jax.shard_map(
        body,
        mesh=mesh,
        in_specs=(rows, P("dp", "ctx"), rows) + weights + vectors,
        out_specs=(rows, rows) + weights + vectors,
        check_vma=False,
    )
```

```python
import numpy as np
import jax
import jax.numpy as jnp
from jax import lax
from jax.experimental import pallas as pl
from jax.experimental.pallas import tpu as pltpu
from jax.sharding import PartitionSpec as P

MESH = pl.DeviceIdType.MESH
EPSILON = 1e-05
MASKED_VALUE = -1e30
BF = jnp.bfloat16
F32 = jnp.float32
MIB = 1024 * 1024
VMEM = pltpu.VMEM


def coords():
    dp = lax.axis_index("dp")
    ctx = lax.axis_index("ctx")
    core = lax.rem(dp, 2)
    z = lax.rem(lax.div(dp, 2), 4)
    y = lax.div(dp, 8) * 2 + lax.rem(ctx, 2)
    x = lax.div(ctx, 2)
    return dict(x=x, y=y, z=z), core


def device_of(pos, core):
    dp = (lax.div(pos["y"], 2) * 4 + pos["z"]) * 2 + core
    ctx = pos["x"] * 2 + lax.rem(pos["y"], 2)
    return (dp, ctx)


def shifted(pos, axis, by):
    return {**pos, axis: lax.rem(pos[axis] + by + 4, 4)}


def greet(pos, core, heads=False):
    barrier = pltpu.get_barrier_semaphore()
    devices = [device_of(shifted(pos, axis, by), core) for axis in "xyz" for by in (1, -1)]
    devices.append(device_of(pos, 1 - core))
    if heads:
        dp, ctx = lax.axis_index("dp"), lax.axis_index("ctx")
        lo = lax.rem(ctx, 2)
        across = lax.rem(pos["x"] + 2, 4) * 2
        devices.append((dp, across + lo))
        for by in (1, 2, 3):
            devices.append((dp, lax.rem(pos["x"] + by, 4) * 2 + 1 - lo))
    for device in devices:
        pl.semaphore_signal(barrier, inc=1, device_id=device, device_id_type=MESH)
    return lambda: pl.semaphore_wait(barrier, len(devices))


class Sender:
    def __init__(self, send_sem, recv_sem):
        self.send_sem, self.recv_sem, self.started = send_sem, recv_sem, []

    def __call__(self, src, dst, device):
        i = len(self.started)
        copy = pltpu.make_async_remote_copy(src_ref=src, dst_ref=dst, send_sem=self.send_sem.at[i],
                                            recv_sem=self.recv_sem.at[i], device_id=device, device_id_type=MESH)
        copy.start()
        self.started.append(copy)
        return copy

    def finish(self):
        for copy in self.started:
            copy.wait_send()


ORDERS = {"A": "xyz", "B": "yzx", "C": "zxy"}
LANES = (512, 256, 640, 640)
ROUNDS = [
    [(0, "A", (0, 80), (0, 128)), (0, "B", (0, 80), (128, 256)), (0, "C", (0, 80), (256, 384)),
     (0, "A", (0, 32), (384, 512)), (0, "B", (32, 64), (384, 512)), (0, "C", (64, 80), (384, 512))],
    [(2, "A", (0, 80), (0, 384)), (2, "B", (0, 80), (384, 512)), (2, "C", (0, 80), (512, 640)),
     (1, "B", (0, 80), (0, 128)), (1, "C", (0, 80), (128, 256))],
    [(3, "A", (0, 80), (0, 384)), (3, "B", (0, 80), (384, 512)), (3, "C", (0, 80), (512, 640))],
]


def spans(where):
    out = {}
    for axis in "xz":
        v = where[axis]
        out[axis] = (0, 4) if v is None else ((v[1] * 2, 2) if isinstance(v, tuple) else (v, 1))
    v = where["y"]
    if v is None:
        hi, lo = (0, 2), (0, 2)
    elif isinstance(v, tuple):
        hi, lo = (v[1], 1), (0, 2)
    elif isinstance(v, int):
        hi, lo = (v // 2, 1), (v % 2, 1)
    else:
        hi, lo = (lax.div(v, 2), 1), (lax.rem(v, 2), 1)
    return (hi, out["z"], out["x"], lo)


def span_index(where):
    return tuple(s if n == 1 else pl.ds(s, n) for s, n in spans(where))


def part_slice(part):
    _, _, rows, lanes = part
    return (pl.ds(rows[0], rows[1] - rows[0]), pl.ds(lanes[0], lanes[1] - lanes[0]))


def where_of(pos, part, k, value, half=None):
    order = ORDERS[part[1]]
    where = {}
    for j, axis in enumerate(order):
        where[axis] = None if j < k else (value if j == k else pos[axis])
    if half is not None:
        where[order[k - 1]] = ("half", half)
    return where


class Gather:
    def __init__(self, pos, core, ins, bufs, send):
        self.pos, self.core, self.ins, self.bufs, self.send = pos, core, ins, bufs, send
        self.first, self.second = {}, {}
        self.pushes = {r: [] for r in range(len(ROUNDS))}

    def put(self, part, where, device, src=None):
        ref = self.bufs[part[0]].at[span_index(where) + (self.core,) + part_slice(part)]
        return self.send(ref if src is None else src, ref, device)

    def near(self, axis, by):
        return device_of(shifted(self.pos, axis, by), self.core)

    def partner(self):
        return device_of(self.pos, 1 - self.core)

    def step1(self, k, r):
        for part in ROUNDS[r]:
            axis = ORDERS[part[1]][k]
            where = where_of(self.pos, part, k, self.pos[axis])
            src = self.ins[part[0]].at[part_slice(part)] if k == 0 else None
            self.first[part, k] = (self.put(part, where, self.near(axis, 1), src),
                                   self.put(part, where, self.near(axis, -1), src))
            if k == 2:
                self.pushes[r].append(self.put(part, where, self.partner()))

    def step2(self, k, r):
        for part in ROUNDS[r]:
            axis = ORDERS[part[1]][k]
            right, left = self.first[part, k]
            below, above = (shifted(self.pos, axis, by)[axis] for by in (-1, 1))
            right.wait_recv()
            if k == 0:
                out = (self.put(part, where_of(self.pos, part, k, below), self.near(axis, 1)),)
                left.wait_recv()
            else:
                a = self.put(part, where_of(self.pos, part, k, below, 0), self.near(axis, 1))
                left.wait_recv()
                out = (a, self.put(part, where_of(self.pos, part, k, above, 1), self.near(axis, -1)))
            self.second[part, k] = out
            if k == 2:
                self.pushes[r].append(self.put(part, where_of(self.pos, part, k, below), self.partner()))
                self.pushes[r].append(self.put(part, where_of(self.pos, part, k, above), self.partner()))

    def step3(self, k, r):
        for part in ROUNDS[r]:
            axis = ORDERS[part[1]][k]
            for copy in self.second[part, k]:
                copy.wait_recv()
            if k == 2:
                across = shifted(self.pos, axis, 2)[axis]
                self.pushes[r].append(self.put(part, where_of(self.pos, part, k, across), self.partner()))

    def finish(self, r):
        for copy in self.pushes[r]:
            copy.wait_recv()


class Heads:
    def __init__(self, src, dst, send_sem, recv_sem, local_sem, cut=()):
        self.src, self.dst, self.send_sem, self.recv_sem, self.local_sem, self.cut = src, dst, send_sem, recv_sem, local_sem, cut
        self.dp, self.ctx = lax.axis_index("dp"), lax.axis_index("ctx")

    def copy(self, o, into, arrived):
        return pltpu.make_async_remote_copy(
            src_ref=self.src.at[(o,) + self.cut], dst_ref=self.dst.at[(into,) + self.cut], send_sem=self.send_sem.at[o],
            recv_sem=self.recv_sem.at[arrived], device_id=(self.dp, o), device_id_type=MESH)

    def own(self):
        return pltpu.make_async_copy(self.src.at[(self.ctx,) + self.cut], self.dst.at[(self.ctx,) + self.cut], self.local_sem)

    def start(self, blocks):
        for o in blocks:
            @pl.when(self.ctx == o)
            def _():
                self.own().start()

            @pl.when(self.ctx != o)
            def _():
                self.copy(o, self.ctx, self.ctx).start()

    def wait_recv(self):
        self.own().wait()
        for o in range(8):
            @pl.when(self.ctx != o)
            def _():
                self.copy(o, o, o).wait_recv()

    def wait_send(self):
        for o in range(8):
            @pl.when(self.ctx != o)
            def _():
                self.copy(o, self.ctx, self.ctx).wait_send()


def dot(a, b):
    return jnp.dot(a, b, preferred_element_type=F32)


def dot_nt(a, b):
    return lax.dot_general(a, b, (((1,), (1,)), ((), ())), preferred_element_type=F32)


def dot_tn(a, b):
    return lax.dot_general(a, b, (((0,), (0,)), ((), ())), preferred_element_type=F32)


def turned(a):
    return a.astype(F32).T.astype(a.dtype)


def norm_parts(values):
    center = values - jnp.mean(values, axis=-1, keepdims=True)
    spread = jnp.mean(center * center, axis=-1, keepdims=True)
    r = lax.rsqrt(spread + EPSILON)
    return center * r, r


def norm_back(u, r, gain, e):
    n = e * gain
    dv = r * (n - jnp.mean(n, axis=-1, keepdims=True) - u * jnp.mean(n * u, axis=-1, keepdims=True))
    return dv, jnp.sum(e * u, axis=0, keepdims=True), jnp.sum(e, axis=0, keepdims=True)


VECTOR_ROWS = ((0,), (1,), (2, 3), (4,), (5,), (6,), (8, 9, 10, 11), (7,))


def selector():
    out = np.zeros((1024, 1152), np.float32)
    for m in range(3):
        for j in range(320):
            at = 320 * m + j
            out[(at // 240) * 256 + at % 240, 384 * m + j] = 1
    return out


def place_tables():
    c = np.arange(1280)
    plain = np.stack([c // 10, 0 * c, c % 10])
    c = np.arange(4096)
    off = c % 256
    n = 240 * (c // 256) + off
    e = np.where(n < 1280, n, n - 1280)
    unused = (off >= 240) | ((n >= 1280) & (n < 2560))
    qkv = np.stack([np.where(unused, -1, e // 20), 2 + (e % 20) // 10, e % 10])
    c = np.arange(5120)
    fc = np.stack([c // 40, 8 + (c % 40) // 10, c % 10])
    pad = lambda t: np.concatenate([t, np.zeros((5, t.shape[1]), t.dtype)]).astype(np.int32)
    return pad(plain), pad(qkv), pad(fc)


def row_owner(core):
    v = lax.broadcasted_iota(jnp.int32, (64, 1), 0)
    return (v // 8) * 16 + core * 8 + lax.rem(v, 8)


def row_picker(r):
    v = lax.broadcasted_iota(jnp.int32, (64, 1024), 0)
    c = lax.broadcasted_iota(jnp.int32, (64, 1024), 1)
    return (c == 16 * v + r).astype(F32).astype(BF)


def entry_picker(entry):
    lane = lax.broadcasted_iota(jnp.int32, (128, entry.shape[1]), 0)
    return (lane == 112 + entry).astype(F32).astype(BF)


def fetched_rows(buf, row_ids):
    tiles = [buf[:, :, :, :, h, 0:16, 256 * h + 128:256 * h + 256].reshape(1024, 128) for h in range(2)]
    return {r: [dot(row_picker(r), tile).astype(BF) for tile in tiles] for r in row_ids}


def take_row(rows, table, row_ids):
    owner, row, entry = table[0:1], table[1:2], table[2:3]
    pick = entry_picker(entry)
    total = jnp.zeros((1, table.shape[1]), F32)
    for h in range(2):
        mine = row_owner(h)
        for r in row_ids:
            hit = (mine == owner) if len(row_ids) == 1 else ((mine == owner) & (row == r))
            total += jnp.sum(jnp.where(hit, dot(rows[r][h], pick), 0.0), axis=0, keepdims=True)
    return total


def unpack_first(buf, plain, qkv, vecs, bias_qkv):
    rows = fetched_rows(buf, range(4))
    for r in (0, 1):
        vecs[r:r + 1] = take_row(rows, plain[...], (r,))
    for p in range(8):
        bias_qkv[p:p + 1] = take_row(rows, qkv[:, 512 * p:512 * p + 512], (2, 3))


def unpack_second(buf, plain, fc, vecs, bias_fc):
    rows = fetched_rows(buf, range(4, 12))
    vecs[2:4] = jnp.zeros((2, 1280), F32)
    for r in (4, 5, 6, 7):
        vecs[r:r + 1] = take_row(rows, plain[...], (r,))
    for p in range(8):
        bias_fc[p:p + 1] = take_row(rows, fc[:, 640 * p:640 * p + 640], (8, 9, 10, 11))


def head_lanes(rows, half):
    lane = lax.broadcasted_iota(jnp.int32, (rows, 128), 1)
    return (lane < 64) if half == 0 else (lane >= 64)


def only(values, half):
    return jnp.where(head_lanes(values.shape[0], half), values, jnp.zeros_like(values))


def swapped(values):
    return pltpu.roll(values.astype(F32), 64, 1).astype(values.dtype)


def tile_of(data, a, b, t):
    return data[a:b, :, 128 * t:128 * t + 128].reshape(128 * (b - a), 128)


def segment_views(data):
    tile = tile_of(data, 0, 8, 7).astype(F32)
    return tile[:, 64:65], jnp.transpose(tile)[64:65, :]


def mask_of(column, row, i, wide):
    rows = lax.broadcasted_iota(jnp.int32, (256, wide), 0) + 256 * i
    cols = lax.broadcasted_iota(jnp.int32, (256, wide), 1)
    keep = (cols <= rows) & (column[256 * i:256 * i + 256] == row[:, :wide])
    return jnp.where(keep, 0.0, MASKED_VALUE)


def head_tiles(data, i, j):
    n = 2 * i + 2
    if j < 2:
        return tile_of(data, 2 * i, n, j), tile_of(data, 0, n, 2 + j), tile_of(data, 0, n, 4 + j)
    return tile_of(data, 2 * i, n, 6), swapped(tile_of(data, 0, n, 6)), tile_of(data, 0, n, 7)


def attend_block(data, mixed, column, row, i):
    wide = 256 * (i + 1)
    hide = mask_of(column, row, i, wide)
    for j in range(3):
        q, k, v = head_tiles(data, i, j)
        total = None
        for half in range(2 if j < 2 else 1):
            scores = dot_nt(only(q, half) * jnp.asarray(0.125, BF), k) + hide
            e = jnp.exp(scores - jnp.max(scores, axis=-1, keepdims=True))
            soft = (e / jnp.sum(e, axis=-1, keepdims=True)).astype(BF)
            part = dot(soft, only(v, half))
            total = part if total is None else total + part
        mixed[2 * i:2 * i + 2, :, 128 * j:128 * j + 128] = total.astype(BF).reshape(2, 128, 128)


def front_kernel(qkv_in, out_in, fc_in, pj_in, tokens, seg, select, plain, qkv_table, fc_table,
                 qkv_all, out_all, fc_all, pj_all, normed, data_all, mixed_all, vecs, bias_fc,
                 qkv, bias_qkv, packed, sent, data, mixed_sent, mixed, send_sem, recv_sem, local_sem,
                 heads_send, heads_recv, heads_local):
    pos, core = coords()
    send = Sender(send_sem, recv_sem)
    here = tuple(s for s, _ in spans(pos)) + (core,)
    local = [pltpu.make_async_copy(src, dst.at[here], local_sem.at[n])
             for n, (src, dst) in enumerate([(qkv_in, qkv), (out_in, out_all), (fc_in, fc_all), (pj_in, pj_all)])]
    for copy in local:
        copy.start()
    greet(pos, core, heads=True)()
    g = Gather(pos, core, (qkv_in, out_in, fc_in, pj_in), (qkv, out_all, fc_all, pj_all), send)
    g.step1(0, 0)
    g.step1(0, 1)
    g.step1(0, 2)
    for copy in local:
        copy.wait()
    g.step2(0, 0)
    g.step3(0, 0)
    g.step1(1, 0)
    g.step2(0, 1)
    g.step2(0, 2)
    g.step2(1, 0)
    g.step3(0, 1)
    g.step1(1, 1)
    g.step3(1, 0)
    g.step1(2, 0)
    g.step3(0, 2)
    g.step1(1, 2)
    g.step2(1, 1)
    g.step2(1, 2)
    g.step2(2, 0)
    g.step3(1, 1)
    g.step1(2, 1)
    u, _ = norm_parts(tokens[...].astype(F32))
    g.step3(2, 0)
    g.step3(1, 2)
    g.finish(0)

    keep = pltpu.make_async_copy(qkv, qkv_all, local_sem.at[0])
    keep.start()
    unpack_first(qkv, plain, qkv_table, vecs, bias_qkv)
    normed[...] = (u * vecs[0:1] + vecs[1:2]).astype(BF)

    def project(p, carry):
        w = qkv[lax.div(p, 4), lax.rem(p, 4)].reshape(1280, 512)
        packed[p] = (dot(normed[...], w) + bias_qkv[pl.ds(p, 1)]).astype(BF)
        return carry

    def select_three(i):
        wide = jnp.concatenate([packed[2 * i], packed[2 * i + 1]], axis=1)
        chunks = dot(wide, select[...])
        for m in range(3):
            n = 3 * i + m
            kind, group = n // 4, n % 4
            low = chunks[:, 384 * m:384 * m + 256].astype(BF)
            last = chunks[:, 384 * m + 256:384 * m + 384]
            if kind == 1:
                last = pltpu.roll(last, 64, 1)
            last = last.astype(BF)
            for s in range(2):
                at = s * 4 + group
                rows = slice(128 * s, 128 * s + 128)
                sent[at, :, 256 * kind:256 * kind + 256] = low[rows]
                if kind == 0:
                    sent[at, :, 768:896] = last[rows]
                elif kind == 1:
                    sent[at, :, 768:896] = sent[at, :, 768:896] + last[rows]
                else:
                    sent[at, :, 896:1024] = last[rows] + seg[rows]

    pieces = [Heads(sent, data, heads_send.at[n], heads_recv.at[n], heads_local.at[n], (slice(None), pl.ds(a, b - a)))
              for n, (a, b) in enumerate(((0, 256), (256, 512), (512, 1024)))]
    lax.fori_loop(0, 4, project, 0)
    select_three(0)
    select_three(1)
    pieces[0].start(range(8))
    lax.fori_loop(4, 6, project, 0)
    select_three(2)
    pieces[1].start(range(8))
    lax.fori_loop(6, 8, project, 0)
    select_three(3)
    pieces[2].start(range(8))
    g.step1(2, 2)
    g.step2(2, 1)
    unpack_second(qkv, plain, fc_table, vecs, bias_fc)
    for piece in pieces:
        piece.wait_recv()
    keep_data = pltpu.make_async_copy(data, data_all, local_sem.at[1])
    keep_data.start()
    column, row = segment_views(data)
    back = Heads(mixed_sent, mixed, heads_send.at[3], heads_recv.at[3], heads_local.at[3])
    for i in range(4):
        attend_block(data, mixed_sent, column, row, i)
        back.start((2 * i, 2 * i + 1))
        if i == 1:
            g.step2(2, 2)
    g.step3(2, 1)
    back.wait_recv()
    keep_mixed = pltpu.make_async_copy(mixed, mixed_all, local_sem.at[2])
    keep_mixed.start()
    g.step3(2, 2)
    g.finish(1)
    g.finish(2)
    keep.wait()
    keep_data.wait()
    keep_mixed.wait()
    for piece in pieces:
        piece.wait_send()
    back.wait_send()
    send.finish()


FRONT_SENDS = 15 * sum(len(r) for r in ROUNDS)


def front(blocks, tokens, seg, select, plain, qkv_table, fc_table):
    sds = jax.ShapeDtypeStruct
    whole = pl.BlockSpec(memory_space=pl.ANY)
    near = pl.BlockSpec(memory_space=VMEM)
    return pl.pallas_call(
        front_kernel,
        out_shape=[sds((2, 4, 4, 2, 2, 80, n), BF) for n in LANES] + [
            sds((256, 1280), BF), sds((8, 128, 1024), BF), sds((8, 128, 384), BF), sds((8, 1280), F32), sds((8, 640), F32)],
        in_specs=[near, whole, whole, whole] + [near] * 6,
        out_specs=[whole] * 4 + [near, whole, whole, near, near],
        scratch_shapes=[
            VMEM((2, 4, 4, 2, 2, 80, 512), BF), VMEM((8, 512), F32), VMEM((8, 256, 512), BF), VMEM((8, 128, 1024), BF),
            VMEM((8, 128, 1024), BF), VMEM((8, 128, 384), BF), VMEM((8, 128, 384), BF),
            pltpu.SemaphoreType.DMA((FRONT_SENDS,)), pltpu.SemaphoreType.DMA((FRONT_SENDS,)), pltpu.SemaphoreType.DMA((4,)),
            pltpu.SemaphoreType.DMA((4, 8)), pltpu.SemaphoreType.DMA((4, 8)), pltpu.SemaphoreType.DMA((4,)),
        ],
        compiler_params=pltpu.CompilerParams(collective_id=0, has_side_effects=True, vmem_limit_bytes=60 * MIB),
        name="fetch_and_attend",
    )(*blocks, tokens, seg, select, plain, qkv_table, fc_table)


def attend_back_block(data, grad, out, dk, dv, column, row, i):
    wide = 256 * (i + 1)
    hide = mask_of(column, row, i, wide)
    for j in range(3):
        q, k, v = head_tiles(data, i, j)
        q = q * jnp.asarray(0.125, BF)
        lanes = slice(128 * j, 128 * j + 128)
        g = grad[2 * i:2 * i + 2, :, lanes].reshape(256, 128)
        total = None
        for half in range(2 if j < 2 else 1):
            qh, gh = only(q, half), only(g, half)
            scores = dot_nt(qh, k) + hide
            e = jnp.exp(scores - jnp.max(scores, axis=-1, keepdims=True))
            soft = e / jnp.sum(e, axis=-1, keepdims=True)
            dv[0:wide, lanes] += dot_tn(soft.astype(BF), gh)
            sg = dot_nt(gh, v)
            sg = (soft * (sg - jnp.sum(soft * sg, axis=-1, keepdims=True))).astype(BF)
            dk[0:wide, lanes] += dot_tn(sg, qh)
            part = dot(sg, only(k, half)) * 0.125
            total = part if total is None else total + part
        t = j if j < 2 else 6
        out[2 * i:2 * i + 2, :, 128 * t:128 * t + 128] = total.astype(BF).reshape(2, 128, 128)


def attend_back_end(out, dk, dv, i):
    rows, blocks = slice(256 * i, 256 * i + 256), slice(2 * i, 2 * i + 2)
    for j in range(2):
        lanes = slice(128 * j, 128 * j + 128)
        out[blocks, :, 256 + 128 * j:384 + 128 * j] = dk[rows, lanes].astype(BF).reshape(2, 128, 128)
        out[blocks, :, 512 + 128 * j:640 + 128 * j] = dv[rows, lanes].astype(BF).reshape(2, 128, 128)
    last = pltpu.roll(dk[rows, 256:384], 64, 1).astype(BF).reshape(2, 128, 128)
    out[blocks, :, 768:896] = out[blocks, :, 768:896] + last
    out[blocks, :, 896:1024] = dv[rows, 256:384].astype(BF).reshape(2, 128, 128)


class Scatter:
    def __init__(self, pos, core, sums, slots, outs, send, rounds, base=None):
        self.base = base or {}
        self.pos, self.core, self.sums, self.slots, self.outs, self.send = pos, core, sums, slots, outs, send
        self.rounds, self.first, self.second = rounds, {}, {}

    def near(self, axis, by):
        return device_of(shifted(self.pos, axis, by), self.core)

    def slot_of(self, part, k, slot, half=None):
        order = ORDERS[part[1]]
        where = {}
        for j, axis in enumerate(order):
            where[axis] = None if j < k else (slot if j == k else 3)
        if half is not None:
            where[order[k - 1]] = ("half", half)
        return where

    def sum_at(self, t, idx):
        ref, halves = self.sums[t]
        return ref, (idx + (self.core,) if halves else idx)

    def cut(self, part):
        base = self.base.get(part[0], 0)
        return part_slice((part[0], part[1], part[2], (part[3][0] - base, part[3][1] - base)))

    def sum_view(self, part, where):
        ref, idx = self.sum_at(part[0], span_index(where))
        return ref.at[idx + self.cut(part)]

    def slot_view(self, part, where):
        return self.slots[part[0]].at[span_index(where) + self.cut(part)]

    def add_slot(self, part, where, slot):
        ref, idx = self.sum_at(part[0], span_index(where))
        here = idx + self.cut(part)
        ref[here] = ref[here] + self.slots[part[0]][span_index(slot) + self.cut(part)]

    def step1(self, k, r):
        for part in self.rounds[r]:
            axis = ORDERS[part[1]][k]
            across = shifted(self.pos, axis, 2)[axis]

            def out(half, by):
                return self.send(self.sum_view(part, where_of(self.pos, part, k, across, half)),
                                 self.slot_view(part, self.slot_of(part, k, 0, half)), self.near(axis, by))

            self.first[part, k] = (out(None, 1),) if k == 0 else (out(0, 1), out(1, -1))

    def step2(self, k, r):
        for part in self.rounds[r]:
            axis = ORDERS[part[1]][k]
            above, below = (shifted(self.pos, axis, by)[axis] for by in (1, -1))
            first = self.first[part, k]
            half = (None, None) if k == 0 else (0, 1)
            first[0].wait_recv()
            self.add_slot(part, where_of(self.pos, part, k, above, half[0]), self.slot_of(part, k, 0, half[0]))
            a = self.send(self.sum_view(part, where_of(self.pos, part, k, above)),
                          self.slot_view(part, self.slot_of(part, k, 1)), self.near(axis, 1))
            if k != 0:
                first[1].wait_recv()
                self.add_slot(part, where_of(self.pos, part, k, below, 1), self.slot_of(part, k, 0, 1))
            b = self.send(self.sum_view(part, where_of(self.pos, part, k, below)),
                          self.slot_view(part, self.slot_of(part, k, 2)), self.near(axis, -1))
            self.second[part, k] = (a, b)

    def step3(self, k, r):
        for part in self.rounds[r]:
            t = part[0]
            axis = ORDERS[part[1]][k]
            for copy in self.second[part, k]:
                copy.wait_recv()
            cut = self.cut(part)
            ref, idx = self.sum_at(t, span_index(where_of(self.pos, part, k, self.pos[axis])))
            slots = self.slots[t]
            total = (ref[idx + cut].astype(F32) + slots[span_index(self.slot_of(part, k, 1)) + cut].astype(F32)
                     + slots[span_index(self.slot_of(part, k, 2)) + cut].astype(F32))
            if k == 0:
                self.outs[t][part_slice(part)] = total
            else:
                ref[idx + cut] = total.astype(BF)


class Pairs:
    def __init__(self, scatter, grads, stages, stage_sem, order):
        self.s, self.grads, self.stages, self.stage_sem, self.order = scatter, grads, stages, stage_sem, order
        self.pushed, self.loads = {}, {}

    def where(self, part, which):
        axis = ORDERS[part[1]][2]
        return where_of(self.s.pos, part, 2, shifted(self.s.pos, axis, which)[axis])

    def stage_names(self, r):
        seen = {}
        for part in self.s.rounds[r]:
            n = seen.get(part[1], 0)
            seen[part[1]] = n + 1
            yield part, part[1] + str(n)

    def push_all(self):
        s = self.s
        for r, which in self.order:
            for part in s.rounds[r]:
                where = self.where(part, which)
                src = self.grads[part[0]].at[span_index(where) + (1 - s.core,) + part_slice(part)]
                self.pushed[part, which] = s.send(src, s.sum_view(part, where), device_of(s.pos, 1 - s.core))

    def load(self, n):
        if n >= len(self.order):
            return
        r, which = self.order[n]
        for j, (part, name) in enumerate(self.stage_names(r)):
            src = self.grads[part[0]].at[span_index(self.where(part, which)) + (self.s.core,) + part_slice(part)]
            dst = self.stages[name].at[n % 2].at[..., pl.ds(0, part[2][1] - part[2][0]), pl.ds(0, part[3][1] - part[3][0])]
            copy = pltpu.make_async_copy(src, dst, self.stage_sem.at[n % 2, j])
            copy.start()
            self.loads[n, part] = copy

    def add(self, n):
        r, which = self.order[n]
        s = self.s
        for part, name in self.stage_names(r):
            self.loads[n, part].wait()
            self.pushed[part, which].wait_recv()
            where = self.where(part, which)
            ref, idx = s.sum_at(part[0], span_index(where))
            here = idx + s.cut(part)
            stage = self.stages[name].at[n % 2]
            ref[here] = ref[here] + stage[..., pl.ds(0, part[2][1] - part[2][0]), pl.ds(0, part[3][1] - part[3][0])]
        self.load(n + 2)


def pack_vectors(plain, qkv, fc, d_pre, d_bias_qkv, d_mid, d_bias_fc):
    out = []
    for h in range(2):
        mine = row_owner(h)
        rows = {}

        def give(table, values, row_ids):
            owner, row, entry = table[0:1], table[1:2], table[2:3]
            pick = entry_picker(entry)
            low = values.astype(BF).astype(F32)
            for r in row_ids:
                hit = (mine == owner) if len(row_ids) == 1 else ((mine == owner) & (row == r))
                part = dot_nt(jnp.where(hit, low, 0.0).astype(BF), pick)
                rows[r] = rows[r] + part if r in rows else part

        for r, values in ((0, d_pre[0]), (1, d_pre[1]), (4, d_mid[0:1]), (5, d_mid[1:2]), (6, d_mid[2:3]), (7, d_mid[3:4])):
            give(plain[...], values, (r,))
        for p in range(8):
            give(qkv[:, 512 * p:512 * p + 512], d_bias_qkv[p:p + 1], (2, 3))
            give(fc[:, 640 * p:640 * p + 640], d_bias_fc[p:p + 1], (8, 9, 10, 11))
        total = jnp.zeros((1024, 128), F32)
        for r in range(12):
            total += dot_tn(row_picker(r), rows[r].astype(BF))
        out.append(total.astype(BF))
    return out


BACK_ROUNDS = {
    1: [(2, "A", (0, 80), (0, 384)), (2, "B", (0, 80), (384, 512)), (2, "C", (0, 80), (512, 640)), (1, "B", (0, 80), (0, 128))],
    2: [(3, "A", (0, 80), (0, 384)), (3, "B", (0, 80), (384, 512)), (3, "C", (0, 80), (512, 640)), (1, "C", (0, 80), (128, 256))],
}
BACK_ORDER = [(1, 2), (2, 2), (1, 1), (1, -1), (2, 1), (2, -1), (1, 0), (2, 0)]
STAGES = {"A0": (2, 4, 2, 80, 384), "B0": (2, 4, 2, 80, 128), "B1": (2, 4, 2, 80, 128), "C0": (4, 4, 80, 128),
          "C1": (4, 4, 80, 128)}


def spread_columns(grads, packed):
    for i in range(4):
        chunks = []
        for m in range(3):
            n = 3 * i + m
            kind, group = n // 4, n % 4
            last = (768, 832, 896)[kind]
            pair = [jnp.concatenate([grads[at, :, 256 * kind:256 * kind + 256], grads[at, :, last:last + 64]], axis=1)
                    for at in (group, 4 + group)]
            chunks.append(jnp.concatenate(pair, axis=0))
        wide = jnp.concatenate(chunks, axis=1)
        blank = jnp.zeros((256, 16), BF)
        for m in range(2):
            both = jnp.concatenate([wide[:, 480 * m:480 * m + 240], blank, wide[:, 480 * m + 240:480 * m + 480], blank], axis=1)
            packed[2 * i + m, :, 0:512] = both[0:128]
            packed[2 * i + m, :, 512:1024] = both[128:256]


def rows_of(packed, p):
    return jnp.concatenate([packed[p, :, 0:512], packed[p, :, 512:1024]], axis=0)


def back_kernel(d_out, d_fc, d_pj, mixed_grad, data, tokens, middle_grad, vecs, normed, w_all, plain, qkv_table, fc_table,
                d_mid, d_bias_fc, s_out, s_fc, s_pj, input_grad, d_w, d_vec,
                sum_out, sum_fc, sum_pj, slot_out, slot_fc, slot_pj, *rest):
    stages = dict(zip(sorted(STAGES), rest[:5]))
    (grad, sent, grads, dk, dv, nt, nt_other, packed_other, w, g_w, d_bias, send_sem, recv_sem, stage_sem, heads_send, heads_recv,
     heads_local, w_sem, g_sem, mg_sem) = rest[5:]
    pos, core = coords()
    partner = device_of(pos, 1 - core)
    send = Sender(send_sem, recv_sem)
    s = Scatter(pos, core, {1: (sum_out, False), 2: (sum_fc, False), 3: (sum_pj, False)},
                {1: slot_out, 2: slot_fc, 3: slot_pj}, {1: s_out, 2: s_fc, 3: s_pj}, send, BACK_ROUNDS)
    pairs = Pairs(s, {1: d_out, 2: d_fc, 3: d_pj}, stages, stage_sem, BACK_ORDER)
    pairs.load(0)
    pairs.load(1)
    bring = pltpu.make_async_copy(middle_grad, input_grad, mg_sem.at[0])
    bring.start()

    def fetch(n):
        copy = pltpu.make_async_copy(w_all.at[n // 8, n // 2 % 4, pl.ds(n % 2 * 2, 2)], w.at[n % 2], w_sem.at[n % 2])
        copy.start()
        return copy

    loads = {0: fetch(0), 1: fetch(1)}
    others_here = greet(pos, core, heads=True)
    nt[...] = turned(normed[...]).reshape(8, 2, 80, 256)
    others_here()
    first = Heads(mixed_grad, grad, heads_send.at[0], heads_recv.at[0], heads_local.at[0])
    second = Heads(sent, grads, heads_send.at[1], heads_recv.at[1], heads_local.at[1])
    first.start(range(8))
    pairs.push_all()
    push_nt = send(nt.at[:, 1 - core], nt_other, partner)
    dk[...] = jnp.zeros_like(dk)
    dv[...] = jnp.zeros_like(dv)
    column, row = segment_views(data)

    def attend_step(i):
        attend_back_block(data, grad, sent, dk, dv, column, row, i)
        attend_back_end(sent, dk, dv, i)
        second.start((2 * i, 2 * i + 1))

    pairs.add(0)
    s.step1(2, 1)
    pairs.add(1)
    s.step1(2, 2)
    first.wait_recv()
    attend_step(3)
    pairs.add(2)
    pairs.add(3)
    s.step2(2, 1)
    attend_step(2)
    pairs.add(4)
    pairs.add(5)
    s.step2(2, 2)
    attend_step(1)
    attend_step(0)
    pairs.add(6)
    pairs.add(7)
    second.wait_recv()
    second.wait_send()
    packed = sent
    spread_columns(grads, packed)
    push_packed = send(packed, packed_other, partner)
    s.step3(2, 1)
    s.step1(1, 1)
    total = [jnp.zeros((256, 640), F32), jnp.zeros((256, 640), F32)]

    def back_through(p):
        mine = rows_of(packed, p)
        for half in range(2):
            n = 2 * p + half
            loads[n].wait()
            total[half] += dot_nt(mine, w[half].reshape(640, 512))
            if n + 2 < 16:
                loads[n + 2] = fetch(n + 2)
        d_bias[p:p + 1] = jnp.sum(mine.astype(F32), axis=0, keepdims=True)

    for p in range(4):
        back_through(p)
    s.step2(1, 1)
    for p in range(4, 8):
        back_through(p)
    s.step3(2, 2)
    s.step1(1, 2)
    s.step3(1, 1)
    s.step1(0, 1)
    push_nt.wait_recv()
    push_packed.wait_recv()
    stores = []

    def weight_grad(p):
        if p >= 2:
            stores[p - 2].wait()
        both = dot(nt[:, core].reshape(640, 256), rows_of(packed, p)) + dot(nt_other[...].reshape(640, 256), rows_of(packed_other, p))
        g_w[p % 2] = both.astype(BF).reshape(4, 2, 80, 512)
        copy = pltpu.make_async_copy(g_w.at[p % 2], d_w.at[p // 4, p % 4], g_sem.at[p % 2])
        copy.start()
        stores.append(copy)

    for p in range(3):
        weight_grad(p)
    s.step2(1, 2)
    s.step2(0, 1)
    for p in range(3, 8):
        weight_grad(p)
    s.step3(1, 2)
    s.step1(0, 2)
    s.step3(0, 1)
    u, r = norm_parts(tokens[...].astype(F32))
    back, dg, db = norm_back(u, r, vecs[0:1], jnp.concatenate(total, axis=1))
    bring.wait()
    input_grad[...] = input_grad[...] + back
    s.step2(0, 2)
    for h, part in enumerate(pack_vectors(plain, qkv_table, fc_table, (dg, db), d_bias, d_mid, d_bias_fc)):
        d_vec[:, :, :, :, h] = part.reshape(2, 4, 4, 2, 16, 128)
    s.step3(0, 2)
    stores[6].wait()
    stores[7].wait()
    first.wait_send()
    send.finish()


BACK_SENDS = 2 + sum(15 * len(r) for r in BACK_ROUNDS.values())


def back(d_out, d_fc, d_pj, mixed_grad, data, tokens, middle_grad, vecs, normed, w_all, plain, qkv_table, fc_table, d_mid,
         d_bias_fc):
    sds = jax.ShapeDtypeStruct
    whole = pl.BlockSpec(memory_space=pl.ANY)
    near = pl.BlockSpec(memory_space=VMEM)
    dma = pltpu.SemaphoreType.DMA
    big = [VMEM((2, 4, 4, 2, 80, n), BF) for n in LANES[1:]]
    return pl.pallas_call(
        back_kernel,
        out_shape=[sds((80, n), F32) for n in LANES[1:]] + [
            sds((256, 1280), F32), sds((2, 4, 4, 2, 80, 512), BF), sds((2, 4, 4, 2, 2, 16, 128), BF)],
        in_specs=[whole] * 4 + [near] * 2 + [whole] + [near] * 2 + [whole] + [near] * 5,
        out_specs=[near] * 4 + [whole, near],
        scratch_shapes=big + big + [VMEM((2,) + STAGES[n], BF) for n in sorted(STAGES)] + [
            VMEM((8, 128, 384), BF), VMEM((8, 128, 1024), BF), VMEM((8, 128, 1024), BF),
            VMEM((1024, 384), F32), VMEM((1024, 384), F32), VMEM((8, 2, 80, 256), BF), VMEM((8, 80, 256), BF),
            VMEM((8, 128, 1024), BF), VMEM((2, 2, 2, 2, 80, 512), BF), VMEM((2, 4, 2, 80, 512), BF), VMEM((8, 512), F32),
            dma((BACK_SENDS,)), dma((BACK_SENDS,)), dma((2, 5)), dma((2, 8)), dma((2, 8)), dma((2,)),
            dma((2,)), dma((2,)), dma((1,)),
        ],
        compiler_params=pltpu.CompilerParams(collective_id=1, has_side_effects=True, vmem_limit_bytes=63 * MIB),
        name="attend_back_and_scatter",
    )(d_out, d_fc, d_pj, mixed_grad, data, tokens, middle_grad, vecs, normed, w_all, plain, qkv_table, fc_table, d_mid, d_bias_fc)


VECTOR_ROUND = [(4, "A", (0, 16), (0, 128))]


def end_kernel(d_w, d_vec_in, s_qkv, s_vec, sums, slot, d_vec, got_vec, slot_vec, send_sem, recv_sem, load_sem):
    pos, core = coords()
    send = Sender(send_sem, recv_sem)
    s = Scatter(pos, core, {0: (sums, False), 4: (d_vec, True)}, {0: slot, 4: slot_vec}, {0: s_qkv, 4: s_vec}, send,
                {0: ROUNDS[0], 4: VECTOR_ROUND})
    bring = pltpu.make_async_copy(d_w, sums, load_sem.at[0])
    bring.start()
    others_here = greet(pos, core)
    d_vec[...] = d_vec_in[...]
    others_here()
    push = send(d_vec_in.at[:, :, :, :, 1 - core], got_vec, device_of(pos, 1 - core))
    bring.wait()
    s.step1(2, 0)
    push.wait_recv()
    d_vec[:, :, :, :, core] = d_vec[:, :, :, :, core] + got_vec[...]
    s.step1(2, 4)
    s.step2(2, 0)
    s.step2(2, 4)
    s.step3(2, 4)
    s.step1(1, 4)
    s.step3(2, 0)
    s.step1(1, 0)
    s.step2(1, 4)
    s.step2(1, 0)
    s.step3(1, 4)
    s.step1(0, 4)
    s.step3(1, 0)
    s.step1(0, 0)
    s.step2(0, 4)
    s.step2(0, 0)
    s.step3(0, 4)
    s.step3(0, 0)
    send.finish()


END_SENDS = 1 + 11 * (len(ROUNDS[0]) + 1)


def end(d_w, d_vec):
    sds = jax.ShapeDtypeStruct
    whole = pl.BlockSpec(memory_space=pl.ANY)
    near = pl.BlockSpec(memory_space=VMEM)
    dma = pltpu.SemaphoreType.DMA
    half = (2, 4, 4, 2, 80, 512)
    return pl.pallas_call(
        end_kernel,
        out_shape=[sds((80, 512), F32), sds((16, 128), F32)],
        in_specs=[whole, near],
        out_specs=[near] * 2,
        scratch_shapes=[
            VMEM(half, BF), VMEM(half, BF), VMEM((2, 4, 4, 2, 2, 16, 128), BF), VMEM((2, 4, 4, 2, 16, 128), BF),
            VMEM((2, 4, 4, 2, 16, 128), BF), dma((END_SENDS,)), dma((END_SENDS,)), dma((1,)),
        ],
        compiler_params=pltpu.CompilerParams(collective_id=2, has_side_effects=True, vmem_limit_bytes=62 * MIB),
        name="scatter_qkv",
    )(d_w, d_vec)


GELU_A = 0.7978845608028654
GELU_B = 0.044715


def joined(mixed, s):
    return jnp.concatenate([mixed[4 * s + g, :, 0:320] for g in range(4)], axis=1)


def feed_kernel(tokens, cotangent, mixed, w_out, vecs, fc, pj, bias_fc,
                block_out, middle_grad, mixed_grad, d_fc, d_pj, d_out, d_bias_fc, d_vec,
                middle, a2, a2_t, bg_t, mixed_t, out_sum, a2_sum):
    p = pl.program_id(0)

    @pl.when(p == 0)
    def _():
        rows = jnp.concatenate([joined(mixed, 0), joined(mixed, 1)], axis=0)
        mixed_t[...] = turned(rows)
        parts = [dot(rows, w_out[n])[:, 0:160] for n in range(8)]
        total = tokens[...].astype(F32) + (jnp.concatenate(parts, axis=1) + vecs[4:5])
        middle[...] = total
        u, _ = norm_parts(total)
        low = (u * vecs[5:6] + vecs[6:7]).astype(BF)
        a2[...] = low
        a2_t[...] = turned(low)
        bg_t[...] = turned(cotangent[...])
        out_sum[...] = jnp.zeros_like(out_sum)
        a2_sum[...] = jnp.zeros_like(a2_sum)

    pre = dot(a2[...], fc[0]) + bias_fc[pl.ds(p, 1)]
    square = pre * pre
    t = jnp.tanh(GELU_A * (pre + GELU_B * pre * square))
    act = (0.5 * pre * (1.0 + t)).astype(BF)
    slope = 0.5 * (1.0 + t) + 0.5 * pre * (1.0 - t * t) * (GELU_A * (1.0 + 3.0 * GELU_B * square))
    out_sum[...] += dot_nt(act, pj[0])
    d_pj[0] = dot(bg_t[...], act).astype(BF)
    pre_grad = (slope * dot(cotangent[...], pj[0])).astype(BF)
    d_bias_fc[pl.ds(p, 1)] = jnp.sum(pre_grad.astype(F32), axis=0, keepdims=True)
    d_fc[0] = dot(a2_t[...], pre_grad).astype(BF)
    a2_sum[...] += dot_nt(pre_grad, fc[0])

    @pl.when(p == 7)
    def _():
        block_out[...] = (middle[...] + (out_sum[...] + vecs[7:8])).astype(BF)
        u, r = norm_parts(middle[...])
        dv, dg, db = norm_back(u, r, vecs[5:6], a2_sum[...])
        c = cotangent[...].astype(F32)
        total = c + dv
        middle_grad[...] = total
        low = total.astype(BF)
        d_vec[0:1] = jnp.sum(low.astype(F32), axis=0, keepdims=True)
        d_vec[1:2] = dg
        d_vec[2:3] = db
        d_vec[3:4] = jnp.sum(c, axis=0, keepdims=True)
        back_sum = jnp.zeros((256, 1280), F32)
        for n in range(8):
            mine = jnp.concatenate([low[:, 160 * n:160 * n + 160], jnp.zeros((256, 96), BF)], axis=1)
            d_out[n] = dot(mixed_t[...], mine).astype(BF)
            back_sum += dot_nt(mine, w_out[n])
        back_low = back_sum.astype(BF)
        for g in range(4):
            rows = jnp.concatenate([back_low[:, 320 * g:320 * g + 320], jnp.zeros((256, 64), BF)], axis=1)
            for s in range(2):
                mixed_grad[s * 4 + g] = rows[s * 128:(s + 1) * 128]


def feed(tokens, cotangent, mixed, w_out, vecs, fc, pj, bias_fc):
    full = lambda *shape: pl.BlockSpec(shape, lambda p: (0,) * len(shape))
    step = lambda *shape: pl.BlockSpec((1,) + shape, lambda p: (p,) + (0,) * len(shape))
    sds = jax.ShapeDtypeStruct
    return pl.pallas_call(
        feed_kernel,
        grid=(8,),
        in_specs=[full(256, 1280), full(256, 1280), full(8, 128, 384), full(8, 1280, 256), full(8, 1280),
                  step(1280, 640), step(1280, 640), full(8, 640)],
        out_specs=[full(256, 1280), full(256, 1280), full(8, 128, 384), step(1280, 640), step(1280, 640),
                   full(8, 1280, 256), full(8, 640), full(4, 1280)],
        out_shape=[sds((256, 1280), BF), sds((256, 1280), F32), sds((8, 128, 384), BF), sds((8, 1280, 640), BF),
                   sds((8, 1280, 640), BF), sds((8, 1280, 256), BF), sds((8, 640), F32), sds((4, 1280), F32)],
        scratch_shapes=[VMEM((256, 1280), F32), VMEM((256, 1280), BF), VMEM((1280, 256), BF), VMEM((1280, 256), BF),
                        VMEM((1280, 256), BF), VMEM((256, 1280), F32), VMEM((256, 1280), F32)],
        compiler_params=pltpu.CompilerParams(vmem_limit_bytes=60 * MIB),
        name="feed_forward_and_back",
    )(tokens, cotangent, mixed, w_out, vecs, fc, pj, bias_fc)


def body(tokens, segments, cotangent, w_qkv, w_out, w_fc, w_proj, *vectors):
    core = lax.rem(lax.axis_index("dp"), 2)
    pairs = [(i, i ^ 1) for i in range(16)]
    rows = jnp.concatenate(
        [vectors[n].reshape(-1, 10) for n in (0, 1, 2, 3, 4, 5, 7, 6)] + [jnp.zeros((4, 10), BF)], axis=0)
    rows = jnp.pad(rows, ((0, 64), (0, 6)))
    rows = jnp.where(core == 0, jnp.concatenate([rows, jnp.zeros_like(rows)], axis=0),
                     jnp.concatenate([jnp.zeros_like(rows), rows], axis=0))
    mine = jnp.concatenate([w_fc, w_proj.T, w_qkv, rows, w_out, jnp.zeros((160, 48), BF)], axis=1)
    mine = mine.reshape(2, 80, 1024)
    kept = lax.dynamic_index_in_dim(mine, core, 0, False)
    got = lax.ppermute(lax.dynamic_index_in_dim(mine, 1 - core, 0, False), "dp", pairs)
    one, two = jnp.where(core == 0, kept, got), jnp.where(core == 0, got, kept)
    blocks = (
        jnp.concatenate([one[:, 640:896], two[:, 640:896]], axis=1),
        jnp.concatenate([one[:, 896:976], two[:, 896:976], jnp.zeros((80, 96), BF)], axis=1),
        jnp.concatenate([one[:, 0:320], two[:, 0:320]], axis=1),
        jnp.concatenate([one[:, 320:640], two[:, 320:640]], axis=1),
    )
    select = jnp.asarray(selector(), BF)
    plain, qkv_table, fc_table = (jnp.asarray(t) for t in place_tables())
    tokens = tokens.reshape(256, 1280)
    cotangent = cotangent.reshape(256, 1280)
    seg = jnp.pad(jnp.broadcast_to(segments.reshape(256, 1).astype(BF), (256, 64)), ((0, 0), (64, 0)))
    qkv, out, fc, pj, normed, data, mixed, vecs, bias_fc = front(blocks, tokens, seg, select, plain, qkv_table, fc_table)
    (block_out, middle_grad, mixed_grad, d_fc, d_pj, d_out, d_bias_fc, d_mid) = feed(
        tokens, cotangent, mixed, out.reshape(8, 1280, 256), vecs, fc.reshape(8, 1280, 640), pj.reshape(8, 1280, 640), bias_fc)
    shape = (2, 4, 4, 2, 2, 80)
    s_out, s_fc, s_pj, input_grad, d_w, d_vec = back(
        d_out.reshape(shape + (256,)), d_fc.reshape(shape + (640,)), d_pj.reshape(shape + (640,)), mixed_grad, data, tokens,
        middle_grad, vecs, normed, qkv, plain, qkv_table, fc_table, d_mid, d_bias_fc)
    s_qkv, s_vec = end(d_w, d_vec)
    halves = [jnp.concatenate([s_fc[:, 320 * c:320 * c + 320], s_pj[:, 320 * c:320 * c + 320],
                               s_qkv[:, 256 * c:256 * c + 240], s_out[:, 80 * c:80 * c + 80]], axis=1) for c in range(2)]
    kept, sent = jnp.where(core == 0, halves[0], halves[1]), jnp.where(core == 0, halves[1], halves[0])
    got = lax.ppermute(sent, "dp", pairs)
    rows = jnp.concatenate([jnp.where(core == 0, kept, got), jnp.where(core == 0, got, kept)], axis=0)
    small = s_vec[:, 112:122]
    ends = tuple(small[ids[0]:ids[-1] + 1].reshape(-1) for ids in VECTOR_ROWS)
    return (block_out.reshape(2, 128, 1280), input_grad.reshape(2, 128, 1280), rows[:, 640:880], rows[:, 880:960],
            rows[:, 0:320], rows[:, 320:640].T) + ends


def solution(mesh):
    weights = (P("ctx", "dp"), P("ctx", "dp"), P("ctx", "dp"), P("dp", "ctx"))
    vectors = (P(("dp", "ctx")),) * 8
    rows = P("dp", "ctx", None)
    return jax.shard_map(
        body,
        mesh=mesh,
        in_specs=(rows, P("dp", "ctx"), rows) + weights + vectors,
        out_specs=(rows, rows) + weights + vectors,
        check_vma=False,
    )
```

```python
import numpy as np
import jax
import jax.numpy as jnp
from jax import lax
from jax.experimental import pallas as pl
from jax.experimental.pallas import tpu as pltpu
from jax.sharding import PartitionSpec as P

MESH = pl.DeviceIdType.MESH
EPSILON = 1e-05
MASKED_VALUE = -1e30
BF = jnp.bfloat16
F32 = jnp.float32
MIB = 1024 * 1024
VMEM = pltpu.VMEM


def coords():
    dp = lax.axis_index("dp")
    ctx = lax.axis_index("ctx")
    core = lax.rem(dp, 2)
    z = lax.rem(lax.div(dp, 2), 4)
    y = lax.div(dp, 8) * 2 + lax.rem(ctx, 2)
    x = lax.div(ctx, 2)
    return dict(x=x, y=y, z=z), core


def device_of(pos, core):
    dp = (lax.div(pos["y"], 2) * 4 + pos["z"]) * 2 + core
    ctx = pos["x"] * 2 + lax.rem(pos["y"], 2)
    return (dp, ctx)


def shifted(pos, axis, by):
    return {**pos, axis: lax.rem(pos[axis] + by + 4, 4)}


def ring_devices(pos, core):
    return [device_of(shifted(pos, axis, by), core) for axis in "xyz" for by in (1, -1, 2)]


def greet(pos, core, heads=False):
    barrier = pltpu.get_barrier_semaphore()
    devices = ring_devices(pos, core)
    devices.append(device_of(pos, 1 - core))
    if heads:
        dp, ctx = lax.axis_index("dp"), lax.axis_index("ctx")
        lo = lax.rem(ctx, 2)
        for by in (1, 2, 3):
            devices.append((dp, lax.rem(pos["x"] + by, 4) * 2 + 1 - lo))
    for device in devices:
        pl.semaphore_signal(barrier, inc=1, device_id=device, device_id_type=MESH)
    return lambda: pl.semaphore_wait(barrier, len(devices))


class Sender:
    def __init__(self, send_sem, recv_sem):
        self.send_sem, self.recv_sem, self.started, self.count = send_sem, recv_sem, [], 0

    def __call__(self, src, dst, device):
        i = self.count
        self.count += 1
        copy = pltpu.make_async_remote_copy(src_ref=src, dst_ref=dst, send_sem=self.send_sem.at[i],
                                            recv_sem=self.recv_sem.at[i], device_id=device, device_id_type=MESH)
        copy.start()
        self.started.append(copy)
        return copy

    def finish(self, copies=None):
        for copy in self.started if copies is None else copies:
            copy.wait_send()
        self.started = [] if copies is None else [c for c in self.started if all(c is not d for d in copies)]


ORDERS = {"A": "xyz", "B": "yzx", "C": "zxy"}
LANES = (512, 256, 640, 640)
ROUNDS = [
    [(0, "A", (0, 80), (0, 128)), (0, "B", (0, 80), (128, 256)), (0, "C", (0, 80), (256, 384)),
     (0, "A", (0, 32), (384, 512)), (0, "B", (32, 64), (384, 512)), (0, "C", (64, 80), (384, 512))],
    [(2, "A", (0, 80), (0, 384)), (2, "B", (0, 80), (384, 512)), (2, "C", (0, 80), (512, 640)),
     (1, "B", (0, 80), (0, 128)), (1, "C", (0, 80), (128, 256))],
    [(3, "A", (0, 80), (0, 384)), (3, "B", (0, 80), (384, 512)), (3, "C", (0, 80), (512, 640))],
]


def spans(where):
    out = {}
    for axis in "xz":
        v = where[axis]
        out[axis] = (0, 4) if v is None else ((v[1] * 2, 2) if isinstance(v, tuple) else (v, 1))
    v = where["y"]
    if v is None:
        hi, lo = (0, 2), (0, 2)
    elif isinstance(v, tuple):
        hi, lo = (v[1], 1), (0, 2)
    elif isinstance(v, int):
        hi, lo = (v // 2, 1), (v % 2, 1)
    else:
        hi, lo = (lax.div(v, 2), 1), (lax.rem(v, 2), 1)
    return (hi, out["z"], out["x"], lo)


def span_index(where):
    return tuple(s if n == 1 else pl.ds(s, n) for s, n in spans(where))


def part_slice(part):
    _, _, rows, lanes = part
    return (pl.ds(rows[0], rows[1] - rows[0]), pl.ds(lanes[0], lanes[1] - lanes[0]))


def where_of(pos, part, k, value, half=None):
    order = ORDERS[part[1]]
    where = {}
    for j, axis in enumerate(order):
        where[axis] = None if j < k else (value if j == k else pos[axis])
    if half is not None:
        where[order[k - 1]] = ("half", half)
    return where


class Gather:
    def __init__(self, pos, core, ins, bufs, send):
        self.pos, self.core, self.ins, self.bufs, self.send = pos, core, ins, bufs, send
        self.first, self.second = {}, {}
        self.pushes = {r: [] for r in range(len(ROUNDS))}

    def put(self, part, where, device, src=None):
        ref = self.bufs[part[0]].at[span_index(where) + (self.core,) + part_slice(part)]
        return self.send(ref if src is None else src, ref, device)

    def near(self, axis, by):
        return device_of(shifted(self.pos, axis, by), self.core)

    def partner(self):
        return device_of(self.pos, 1 - self.core)

    def step1(self, k, r):
        for part in ROUNDS[r]:
            axis = ORDERS[part[1]][k]
            where = where_of(self.pos, part, k, self.pos[axis])
            src = self.ins[part[0]].at[part_slice(part)] if k == 0 else None
            self.first[part, k] = tuple(self.put(part, where, self.near(axis, by), src) for by in ((1, -1) if k else (1, -1, 2)))
            if k == 2:
                self.pushes[r].append(self.put(part, where, self.partner()))

    def step2(self, k, r):
        for part in ROUNDS[r]:
            axis = ORDERS[part[1]][k]
            if k == 0:
                self.second[part, k] = self.first[part, k]
                continue
            right, left = self.first[part, k]
            below, above = (shifted(self.pos, axis, by)[axis] for by in (-1, 1))
            right.wait_recv()
            a = self.put(part, where_of(self.pos, part, k, below, 0), self.near(axis, 1))
            left.wait_recv()
            self.second[part, k] = (a, self.put(part, where_of(self.pos, part, k, above, 1), self.near(axis, -1)))
            if k == 2:
                self.pushes[r].append(self.put(part, where_of(self.pos, part, k, below), self.partner()))
                self.pushes[r].append(self.put(part, where_of(self.pos, part, k, above), self.partner()))

    def step3(self, k, r):
        for part in ROUNDS[r]:
            axis = ORDERS[part[1]][k]
            for copy in self.second[part, k]:
                copy.wait_recv()
            if k == 2:
                across = shifted(self.pos, axis, 2)[axis]
                self.pushes[r].append(self.put(part, where_of(self.pos, part, k, across), self.partner()))

    def finish(self, r):
        for copy in self.pushes[r]:
            copy.wait_recv()


class Heads:
    def __init__(self, src, dst, send_sem, recv_sem, local_sem, cut=()):
        self.src, self.dst, self.send_sem, self.recv_sem, self.local_sem, self.cut = src, dst, send_sem, recv_sem, local_sem, cut
        self.dp, self.ctx = lax.axis_index("dp"), lax.axis_index("ctx")

    def copy(self, o, into, arrived):
        return pltpu.make_async_remote_copy(
            src_ref=self.src.at[(o,) + self.cut], dst_ref=self.dst.at[(into,) + self.cut], send_sem=self.send_sem.at[o],
            recv_sem=self.recv_sem.at[arrived], device_id=(self.dp, o), device_id_type=MESH)

    def own(self):
        return pltpu.make_async_copy(self.src.at[(self.ctx,) + self.cut], self.dst.at[(self.ctx,) + self.cut], self.local_sem)

    def start(self, blocks):
        for o in blocks:
            @pl.when(self.ctx == o)
            def _():
                self.own().start()

            @pl.when(self.ctx != o)
            def _():
                self.copy(o, self.ctx, self.ctx).start()

    def wait_recv(self):
        self.own().wait()
        for o in range(8):
            @pl.when(self.ctx != o)
            def _():
                self.copy(o, o, o).wait_recv()

    def wait_send(self):
        for o in range(8):
            @pl.when(self.ctx != o)
            def _():
                self.copy(o, self.ctx, self.ctx).wait_send()


def dot(a, b):
    return jnp.dot(a, b, preferred_element_type=F32)


def dot_nt(a, b):
    return lax.dot_general(a, b, (((1,), (1,)), ((), ())), preferred_element_type=F32)


def dot_tn(a, b):
    return lax.dot_general(a, b, (((0,), (0,)), ((), ())), preferred_element_type=F32)


def turned(a):
    return a.astype(F32).T.astype(a.dtype)


def norm_parts(values):
    center = values - jnp.mean(values, axis=-1, keepdims=True)
    spread = jnp.mean(center * center, axis=-1, keepdims=True)
    r = lax.rsqrt(spread + EPSILON)
    return center * r, r


def norm_back(u, r, gain, e):
    n = e * gain
    dv = r * (n - jnp.mean(n, axis=-1, keepdims=True) - u * jnp.mean(n * u, axis=-1, keepdims=True))
    return dv, jnp.sum(e * u, axis=0, keepdims=True), jnp.sum(e, axis=0, keepdims=True)


VECTOR_ROWS = ((0,), (1,), (2, 3), (4,), (5,), (6,), (8, 9, 10, 11), (7,))


def selector():
    out = np.zeros((1024, 1152), np.float32)
    for m in range(3):
        for j in range(320):
            at = 320 * m + j
            out[(at // 240) * 256 + at % 240, 384 * m + j] = 1
    return out


def place_tables():
    c = np.arange(1280)
    plain = np.stack([c // 10, 0 * c, c % 10])
    c = np.arange(4096)
    off = c % 256
    n = 240 * (c // 256) + off
    e = np.where(n < 1280, n, n - 1280)
    unused = (off >= 240) | ((n >= 1280) & (n < 2560))
    qkv = np.stack([np.where(unused, -1, e // 20), 2 + (e % 20) // 10, e % 10])
    c = np.arange(5120)
    fc = np.stack([c // 40, 8 + (c % 40) // 10, c % 10])
    pad = lambda t: np.concatenate([t, np.zeros((5, t.shape[1]), t.dtype)]).astype(np.int32)
    return pad(plain), pad(qkv), pad(fc)


def row_owner(core):
    v = lax.broadcasted_iota(jnp.int32, (64, 1), 0)
    return (v // 8) * 16 + core * 8 + lax.rem(v, 8)


def row_picker(r):
    v = lax.broadcasted_iota(jnp.int32, (64, 1024), 0)
    c = lax.broadcasted_iota(jnp.int32, (64, 1024), 1)
    return (c == 16 * v + r).astype(F32).astype(BF)


def entry_picker(entry):
    lane = lax.broadcasted_iota(jnp.int32, (128, entry.shape[1]), 0)
    return (lane == 112 + entry).astype(F32).astype(BF)


def fetched_rows(buf, row_ids):
    tiles = [buf[:, :, :, :, h, 0:16, 256 * h + 128:256 * h + 256].reshape(1024, 128) for h in range(2)]
    return {r: [dot(row_picker(r), tile).astype(BF) for tile in tiles] for r in row_ids}


def take_row(rows, table, row_ids):
    owner, row, entry = table[0:1], table[1:2], table[2:3]
    pick = entry_picker(entry)
    total = jnp.zeros((1, table.shape[1]), F32)
    for h in range(2):
        mine = row_owner(h)
        for r in row_ids:
            hit = (mine == owner) if len(row_ids) == 1 else ((mine == owner) & (row == r))
            total += jnp.sum(jnp.where(hit, dot(rows[r][h], pick), 0.0), axis=0, keepdims=True)
    return total


def unpack_first(buf, plain, qkv, vecs, bias_qkv):
    rows = fetched_rows(buf, range(4))
    for r in (0, 1):
        vecs[r:r + 1] = take_row(rows, plain[...], (r,))
    for p in range(8):
        bias_qkv[p:p + 1] = take_row(rows, qkv[:, 512 * p:512 * p + 512], (2, 3))


def unpack_second(buf, plain, fc, vecs, bias_fc):
    rows = fetched_rows(buf, range(4, 12))
    vecs[2:4] = jnp.zeros((2, 1280), F32)
    for r in (4, 5, 6, 7):
        vecs[r:r + 1] = take_row(rows, plain[...], (r,))
    for p in range(8):
        bias_fc[p:p + 1] = take_row(rows, fc[:, 640 * p:640 * p + 640], (8, 9, 10, 11))


def head_lanes(rows, half):
    lane = lax.broadcasted_iota(jnp.int32, (rows, 128), 1)
    return (lane < 64) if half == 0 else (lane >= 64)


def only(values, half):
    return jnp.where(head_lanes(values.shape[0], half), values, jnp.zeros_like(values))


def swapped(values):
    return pltpu.roll(values.astype(F32), 64, 1).astype(values.dtype)


def tile_of(data, a, b, t):
    return data[a:b, :, 128 * t:128 * t + 128].reshape(128 * (b - a), 128)


def segment_views(data):
    tile = tile_of(data, 0, 8, 7).astype(F32)
    return tile[:, 64:65], jnp.transpose(tile)[64:65, :]


def mask_of(column, row, i, wide):
    rows = lax.broadcasted_iota(jnp.int32, (256, wide), 0) + 256 * i
    cols = lax.broadcasted_iota(jnp.int32, (256, wide), 1)
    keep = (cols <= rows) & (column[256 * i:256 * i + 256] == row[:, :wide])
    return jnp.where(keep, 0.0, MASKED_VALUE)


def head_tiles(data, i, j):
    n = 2 * i + 2
    if j < 2:
        return tile_of(data, 2 * i, n, j), tile_of(data, 0, n, 2 + j), tile_of(data, 0, n, 4 + j)
    return tile_of(data, 2 * i, n, 6), swapped(tile_of(data, 0, n, 6)), tile_of(data, 0, n, 7)


def attend_block(data, mixed, column, row, i):
    wide = 256 * (i + 1)
    hide = mask_of(column, row, i, wide)
    for j in range(3):
        q, k, v = head_tiles(data, i, j)
        total = None
        for half in range(2 if j < 2 else 1):
            scores = dot_nt(only(q, half) * jnp.asarray(0.125, BF), k) + hide
            e = jnp.exp(scores - jnp.max(scores, axis=-1, keepdims=True))
            soft = (e / jnp.sum(e, axis=-1, keepdims=True)).astype(BF)
            part = dot(soft, only(v, half))
            total = part if total is None else total + part
        mixed[2 * i:2 * i + 2, :, 128 * j:128 * j + 128] = total.astype(BF).reshape(2, 128, 128)


def front_kernel(qkv_in, out_in, fc_in, pj_in, tokens, seg, select, plain, qkv_table, fc_table,
                 qkv_all, out_all, fc_all, pj_all, normed, data_all, mixed_all, vecs, bias_fc,
                 qkv, bias_qkv, packed, sent, data, mixed_sent, mixed, send_sem, recv_sem, local_sem,
                 heads_send, heads_recv, heads_local):
    pos, core = coords()
    send = Sender(send_sem, recv_sem)
    here = tuple(s for s, _ in spans(pos)) + (core,)
    local = [pltpu.make_async_copy(src, dst.at[here], local_sem.at[n])
             for n, (src, dst) in enumerate([(qkv_in, qkv), (out_in, out_all), (fc_in, fc_all), (pj_in, pj_all)])]
    for copy in local:
        copy.start()
    greet(pos, core, heads=True)()
    g = Gather(pos, core, (qkv_in, out_in, fc_in, pj_in), (qkv, out_all, fc_all, pj_all), send)
    g.step1(0, 0)
    g.step1(0, 1)
    g.step1(0, 2)
    for copy in local:
        copy.wait()
    g.step2(0, 0)
    g.step3(0, 0)
    g.step1(1, 0)
    g.step2(0, 1)
    g.step2(0, 2)
    g.step2(1, 0)
    g.step3(0, 1)
    g.step1(1, 1)
    g.step3(1, 0)
    g.step1(2, 0)
    g.step3(0, 2)
    g.step1(1, 2)
    g.step2(1, 1)
    g.step2(1, 2)
    g.step2(2, 0)
    g.step3(1, 1)
    g.step1(2, 1)
    u, _ = norm_parts(tokens[...].astype(F32))
    g.step3(2, 0)
    g.step3(1, 2)
    g.finish(0)

    keep = pltpu.make_async_copy(qkv, qkv_all, local_sem.at[0])
    keep.start()
    unpack_first(qkv, plain, qkv_table, vecs, bias_qkv)
    normed[...] = (u * vecs[0:1] + vecs[1:2]).astype(BF)

    def project(p, carry):
        w = qkv[lax.div(p, 4), lax.rem(p, 4)].reshape(1280, 512)
        packed[p] = (dot(normed[...], w) + bias_qkv[pl.ds(p, 1)]).astype(BF)
        return carry

    def select_three(i):
        wide = jnp.concatenate([packed[2 * i], packed[2 * i + 1]], axis=1)
        chunks = dot(wide, select[...])
        for m in range(3):
            n = 3 * i + m
            kind, group = n // 4, n % 4
            low = chunks[:, 384 * m:384 * m + 256].astype(BF)
            last = chunks[:, 384 * m + 256:384 * m + 384]
            if kind == 1:
                last = pltpu.roll(last, 64, 1)
            last = last.astype(BF)
            for s in range(2):
                at = s * 4 + group
                rows = slice(128 * s, 128 * s + 128)
                sent[at, :, 256 * kind:256 * kind + 256] = low[rows]
                if kind == 0:
                    sent[at, :, 768:896] = last[rows]
                elif kind == 1:
                    sent[at, :, 768:896] = sent[at, :, 768:896] + last[rows]
                else:
                    sent[at, :, 896:1024] = last[rows] + seg[rows]

    pieces = [Heads(sent, data, heads_send.at[n], heads_recv.at[n], heads_local.at[n], (slice(None), pl.ds(a, b - a)))
              for n, (a, b) in enumerate(((0, 256), (256, 512), (512, 1024)))]
    lax.fori_loop(0, 4, project, 0)
    select_three(0)
    select_three(1)
    pieces[0].start(range(8))
    lax.fori_loop(4, 6, project, 0)
    select_three(2)
    pieces[1].start(range(8))
    lax.fori_loop(6, 8, project, 0)
    select_three(3)
    pieces[2].start(range(8))
    g.step1(2, 2)
    g.step2(2, 1)
    unpack_second(qkv, plain, fc_table, vecs, bias_fc)
    for piece in pieces:
        piece.wait_recv()
    keep_data = pltpu.make_async_copy(data, data_all, local_sem.at[1])
    keep_data.start()
    column, row = segment_views(data)
    back = Heads(mixed_sent, mixed, heads_send.at[3], heads_recv.at[3], heads_local.at[3])
    for i in range(4):
        attend_block(data, mixed_sent, column, row, i)
        back.start((2 * i, 2 * i + 1))
        if i == 1:
            g.step2(2, 2)
    g.step3(2, 1)
    back.wait_recv()
    keep_mixed = pltpu.make_async_copy(mixed, mixed_all, local_sem.at[2])
    keep_mixed.start()
    g.step3(2, 2)
    g.finish(1)
    g.finish(2)
    keep.wait()
    keep_data.wait()
    keep_mixed.wait()
    for piece in pieces:
        piece.wait_send()
    back.wait_send()
    send.finish()


FRONT_SENDS = 15 * sum(len(r) for r in ROUNDS)


def front(blocks, tokens, seg, select, plain, qkv_table, fc_table):
    sds = jax.ShapeDtypeStruct
    whole = pl.BlockSpec(memory_space=pl.ANY)
    near = pl.BlockSpec(memory_space=VMEM)
    return pl.pallas_call(
        front_kernel,
        out_shape=[sds((2, 4, 4, 2, 2, 80, n), BF) for n in LANES] + [
            sds((256, 1280), BF), sds((8, 128, 1024), BF), sds((8, 128, 384), BF), sds((8, 1280), F32), sds((8, 640), F32)],
        in_specs=[near, whole, whole, whole] + [near] * 6,
        out_specs=[whole] * 4 + [near, whole, whole, near, near],
        scratch_shapes=[
            VMEM((2, 4, 4, 2, 2, 80, 512), BF), VMEM((8, 512), F32), VMEM((8, 256, 512), BF), VMEM((8, 128, 1024), BF),
            VMEM((8, 128, 1024), BF), VMEM((8, 128, 384), BF), VMEM((8, 128, 384), BF),
            pltpu.SemaphoreType.DMA((FRONT_SENDS,)), pltpu.SemaphoreType.DMA((FRONT_SENDS,)), pltpu.SemaphoreType.DMA((4,)),
            pltpu.SemaphoreType.DMA((4, 8)), pltpu.SemaphoreType.DMA((4, 8)), pltpu.SemaphoreType.DMA((4,)),
        ],
        compiler_params=pltpu.CompilerParams(collective_id=0, has_side_effects=True, vmem_limit_bytes=60 * MIB),
        name="fetch_and_attend",
    )(*blocks, tokens, seg, select, plain, qkv_table, fc_table)


def attend_back_block(data, grad, out, dk, dv, column, row, i):
    wide = 256 * (i + 1)
    hide = mask_of(column, row, i, wide)
    for j in range(3):
        q, k, v = head_tiles(data, i, j)
        q = q * jnp.asarray(0.125, BF)
        lanes = slice(128 * j, 128 * j + 128)
        g = grad[2 * i:2 * i + 2, :, lanes].reshape(256, 128)
        total = None
        for half in range(2 if j < 2 else 1):
            qh, gh = only(q, half), only(g, half)
            scores = dot_nt(qh, k) + hide
            e = jnp.exp(scores - jnp.max(scores, axis=-1, keepdims=True))
            soft = e / jnp.sum(e, axis=-1, keepdims=True)
            dv[0:wide, lanes] += dot_tn(soft.astype(BF), gh)
            sg = dot_nt(gh, v)
            sg = (soft * (sg - jnp.sum(soft * sg, axis=-1, keepdims=True))).astype(BF)
            dk[0:wide, lanes] += dot_tn(sg, qh)
            part = dot(sg, only(k, half)) * 0.125
            total = part if total is None else total + part
        t = j if j < 2 else 6
        out[2 * i:2 * i + 2, :, 128 * t:128 * t + 128] = total.astype(BF).reshape(2, 128, 128)


def attend_back_end(out, dk, dv, i):
    rows, blocks = slice(256 * i, 256 * i + 256), slice(2 * i, 2 * i + 2)
    for j in range(2):
        lanes = slice(128 * j, 128 * j + 128)
        out[blocks, :, 256 + 128 * j:384 + 128 * j] = dk[rows, lanes].astype(BF).reshape(2, 128, 128)
        out[blocks, :, 512 + 128 * j:640 + 128 * j] = dv[rows, lanes].astype(BF).reshape(2, 128, 128)
    last = pltpu.roll(dk[rows, 256:384], 64, 1).astype(BF).reshape(2, 128, 128)
    out[blocks, :, 768:896] = out[blocks, :, 768:896] + last
    out[blocks, :, 896:1024] = dv[rows, 256:384].astype(BF).reshape(2, 128, 128)


class Scatter:
    def __init__(self, pos, core, sums, slots, outs, send, rounds, base=None):
        self.base = base or {}
        self.pos, self.core, self.sums, self.slots, self.outs, self.send = pos, core, sums, slots, outs, send
        self.rounds, self.first, self.second = rounds, {}, {}

    def near(self, axis, by):
        return device_of(shifted(self.pos, axis, by), self.core)

    def slot_of(self, part, k, slot, half=None):
        order = ORDERS[part[1]]
        where = {}
        for j, axis in enumerate(order):
            where[axis] = None if j < k else (slot if j == k else 3)
        if half is not None:
            where[order[k - 1]] = ("half", half)
        return where

    def sum_at(self, t, idx):
        ref, halves = self.sums[t]
        return ref, (idx + (self.core,) if halves else idx)

    def cut(self, part):
        base = self.base.get(part[0], 0)
        return part_slice((part[0], part[1], part[2], (part[3][0] - base, part[3][1] - base)))

    def sum_view(self, part, where):
        ref, idx = self.sum_at(part[0], span_index(where))
        return ref.at[idx + self.cut(part)]

    def slot_view(self, part, where):
        return self.slots[part[0]].at[span_index(where) + self.cut(part)]

    def add_slot(self, part, where, slot):
        ref, idx = self.sum_at(part[0], span_index(where))
        here = idx + self.cut(part)
        ref[here] = ref[here] + self.slots[part[0]][span_index(slot) + self.cut(part)]

    def step1(self, k, r):
        for part in self.rounds[r]:
            axis = ORDERS[part[1]][k]
            across = shifted(self.pos, axis, 2)[axis]

            def out(half, by):
                return self.send(self.sum_view(part, where_of(self.pos, part, k, across, half)),
                                 self.slot_view(part, self.slot_of(part, k, 0, half)), self.near(axis, by))

            def straight(slot, by):
                return self.send(self.sum_view(part, where_of(self.pos, part, k, shifted(self.pos, axis, by)[axis])),
                                 self.slot_view(part, self.slot_of(part, k, slot)), self.near(axis, by))

            if k == 0:
                self.second[part, k] = (straight(0, 2), straight(1, 1), straight(2, -1))
            else:
                self.first[part, k] = (out(0, 1), out(1, -1))

    def step2(self, k, r):
        for part in self.rounds[r] if k else ():
            axis = ORDERS[part[1]][k]
            above, below = (shifted(self.pos, axis, by)[axis] for by in (1, -1))
            first = self.first[part, k]
            first[0].wait_recv()
            self.add_slot(part, where_of(self.pos, part, k, above, 0), self.slot_of(part, k, 0, 0))
            a = self.send(self.sum_view(part, where_of(self.pos, part, k, above)),
                          self.slot_view(part, self.slot_of(part, k, 1)), self.near(axis, 1))
            first[1].wait_recv()
            self.add_slot(part, where_of(self.pos, part, k, below, 1), self.slot_of(part, k, 0, 1))
            b = self.send(self.sum_view(part, where_of(self.pos, part, k, below)),
                          self.slot_view(part, self.slot_of(part, k, 2)), self.near(axis, -1))
            self.second[part, k] = (a, b)

    def copies_of(self, t, r):
        return [c for part in self.rounds[r] if part[0] == t for k in range(3) for held in (self.first, self.second)
                for c in held.get((part, k), ())]

    def step3(self, k, r):
        for part in self.rounds[r]:
            t = part[0]
            axis = ORDERS[part[1]][k]
            for copy in self.second[part, k]:
                copy.wait_recv()
            cut = self.cut(part)
            ref, idx = self.sum_at(t, span_index(where_of(self.pos, part, k, self.pos[axis])))
            slots = self.slots[t]
            total = (ref[idx + cut].astype(F32) + slots[span_index(self.slot_of(part, k, 1)) + cut].astype(F32)
                     + slots[span_index(self.slot_of(part, k, 2)) + cut].astype(F32))
            if k == 0:
                self.outs[t][part_slice(part)] = total + slots[span_index(self.slot_of(part, k, 0)) + cut].astype(F32)
            else:
                ref[idx + cut] = total.astype(BF)


class Pairs:
    def __init__(self, scatter, grads, stages, stage_sem, order):
        self.s, self.grads, self.stages, self.stage_sem, self.order = scatter, grads, stages, stage_sem, order
        self.pushed, self.loads = {}, {}

    def where(self, part, which):
        axis = ORDERS[part[1]][2]
        return where_of(self.s.pos, part, 2, shifted(self.s.pos, axis, which)[axis])

    def stage_names(self, r):
        seen = {}
        for part in self.s.rounds[r]:
            n = seen.get(part[1], 0)
            seen[part[1]] = n + 1
            yield part, part[1] + str(n)

    def push_all(self):
        s = self.s
        for r, which in self.order:
            for part in s.rounds[r]:
                where = self.where(part, which)
                src = self.grads[part[0]].at[span_index(where) + (1 - s.core,) + part_slice(part)]
                self.pushed[part, which] = s.send(src, s.sum_view(part, where), device_of(s.pos, 1 - s.core))

    def load(self, n):
        if n >= len(self.order):
            return
        r, which = self.order[n]
        for j, (part, name) in enumerate(self.stage_names(r)):
            src = self.grads[part[0]].at[span_index(self.where(part, which)) + (self.s.core,) + part_slice(part)]
            dst = self.stages[name].at[n % 2].at[..., pl.ds(0, part[2][1] - part[2][0]), pl.ds(0, part[3][1] - part[3][0])]
            copy = pltpu.make_async_copy(src, dst, self.stage_sem.at[n % 2, j])
            copy.start()
            self.loads[n, part] = copy

    def add(self, n):
        r, which = self.order[n]
        s = self.s
        for part, name in self.stage_names(r):
            self.loads[n, part].wait()
            self.pushed[part, which].wait_recv()
            where = self.where(part, which)
            ref, idx = s.sum_at(part[0], span_index(where))
            here = idx + s.cut(part)
            stage = self.stages[name].at[n % 2]
            ref[here] = ref[here] + stage[..., pl.ds(0, part[2][1] - part[2][0]), pl.ds(0, part[3][1] - part[3][0])]
        self.load(n + 2)


def pack_vectors(plain, qkv, fc, d_pre, d_bias_qkv, d_mid, d_bias_fc):
    out = []
    for h in range(2):
        mine = row_owner(h)
        rows = {}

        def give(table, values, row_ids):
            owner, row, entry = table[0:1], table[1:2], table[2:3]
            pick = entry_picker(entry)
            low = values.astype(BF).astype(F32)
            for r in row_ids:
                hit = (mine == owner) if len(row_ids) == 1 else ((mine == owner) & (row == r))
                part = dot_nt(jnp.where(hit, low, 0.0).astype(BF), pick)
                rows[r] = rows[r] + part if r in rows else part

        for r, values in ((0, d_pre[0]), (1, d_pre[1]), (4, d_mid[0:1]), (5, d_mid[1:2]), (6, d_mid[2:3]), (7, d_mid[3:4])):
            give(plain[...], values, (r,))
        for p in range(8):
            give(qkv[:, 512 * p:512 * p + 512], d_bias_qkv[p:p + 1], (2, 3))
            give(fc[:, 640 * p:640 * p + 640], d_bias_fc[p:p + 1], (8, 9, 10, 11))
        total = jnp.zeros((1024, 128), F32)
        for r in range(12):
            total += dot_tn(row_picker(r), rows[r].astype(BF))
        out.append(total.astype(BF))
    return out


BACK_ROUNDS = {
    1: [(2, "A", (0, 80), (0, 384)), (2, "B", (0, 80), (384, 512)), (2, "C", (0, 80), (512, 640)), (1, "B", (0, 80), (0, 128))],
    2: [(3, "A", (0, 80), (0, 384)), (3, "B", (0, 80), (384, 512)), (3, "C", (0, 80), (512, 640)), (1, "C", (0, 80), (128, 256))],
}
VECTOR_ROUND = [(4, "A", (0, 16), (0, 128))]
BACK_ORDER = [(1, 2), (2, 2), (1, 1), (1, -1), (2, 1), (2, -1), (1, 0), (2, 0)]
STAGES = {"A0": (2, 4, 2, 80, 384), "B0": (2, 4, 2, 80, 128), "B1": (2, 4, 2, 80, 128), "C0": (4, 4, 80, 128),
          "C1": (4, 4, 80, 128)}


def spread_columns(grads, packed):
    for i in range(4):
        chunks = []
        for m in range(3):
            n = 3 * i + m
            kind, group = n // 4, n % 4
            last = (768, 832, 896)[kind]
            pair = [jnp.concatenate([grads[at, :, 256 * kind:256 * kind + 256], grads[at, :, last:last + 64]], axis=1)
                    for at in (group, 4 + group)]
            chunks.append(jnp.concatenate(pair, axis=0))
        wide = jnp.concatenate(chunks, axis=1)
        blank = jnp.zeros((256, 16), BF)
        for m in range(2):
            both = jnp.concatenate([wide[:, 480 * m:480 * m + 240], blank, wide[:, 480 * m + 240:480 * m + 480], blank], axis=1)
            packed[2 * i + m, :, 0:512] = both[0:128]
            packed[2 * i + m, :, 512:1024] = both[128:256]


def rows_of(packed, p):
    return jnp.concatenate([packed[p, :, 0:512], packed[p, :, 512:1024]], axis=0)


def back_kernel(d_out, d_fc, d_pj, mixed_grad, data, tokens, middle_grad, vecs, normed, w_all, plain, qkv_table, fc_table,
                d_mid, d_bias_fc, s_out, s_fc, s_pj, input_grad, s_qkv, s_vec,
                sum_out, sum_fc, sum_pj, slot_out, slot_fc, slot_pj, *rest):
    stages = dict(zip(sorted(STAGES), rest[:5]))
    (grad, sent, grads, dk, dv, nt, nt_other, packed_other, w, d_bias, d_vec, got_vec, slot_vec, send_sem, recv_sem, stage_sem, heads_send,
     heads_recv, heads_local, w_sem, mg_sem, free_sem) = rest[5:]
    pos, core = coords()
    partner = device_of(pos, 1 - core)
    send = Sender(send_sem, recv_sem)
    s = Scatter(pos, core, {0: (sum_fc, False), 1: (sum_out, False), 2: (sum_fc, False), 3: (sum_pj, False), 4: (d_vec, True)},
                {0: slot_fc, 1: slot_out, 2: slot_fc, 3: slot_pj, 4: slot_vec},
                {0: s_qkv, 1: s_out, 2: s_fc, 3: s_pj, 4: s_vec}, send, {**BACK_ROUNDS, 0: ROUNDS[0], 4: VECTOR_ROUND})
    pairs = Pairs(s, {1: d_out, 2: d_fc, 3: d_pj}, stages, stage_sem, BACK_ORDER)
    pairs.load(0)
    pairs.load(1)
    bring = pltpu.make_async_copy(middle_grad, input_grad, mg_sem.at[0])
    bring.start()

    def fetch(n):
        copy = pltpu.make_async_copy(w_all.at[n // 8, n // 2 % 4, pl.ds(n % 2 * 2, 2)], w.at[n % 2], w_sem.at[n % 2])
        copy.start()
        return copy

    loads = {0: fetch(0), 1: fetch(1)}
    others_here = greet(pos, core, heads=True)
    nt[...] = turned(normed[...]).reshape(8, 2, 80, 256)
    others_here()
    first = Heads(mixed_grad, grad, heads_send.at[0], heads_recv.at[0], heads_local.at[0])
    second = Heads(sent, grads, heads_send.at[1], heads_recv.at[1], heads_local.at[1])
    first.start(range(8))
    pairs.push_all()
    push_nt = send(nt.at[:, 1 - core], nt_other, partner)
    dk[...] = jnp.zeros_like(dk)
    dv[...] = jnp.zeros_like(dv)
    column, row = segment_views(data)

    def attend_step(i):
        attend_back_block(data, grad, sent, dk, dv, column, row, i)
        attend_back_end(sent, dk, dv, i)
        second.start((2 * i, 2 * i + 1))

    pairs.add(0)
    s.step1(2, 1)
    pairs.add(1)
    s.step1(2, 2)
    first.wait_recv()
    attend_step(3)
    pairs.add(2)
    pairs.add(3)
    s.step2(2, 1)
    attend_step(2)
    pairs.add(4)
    pairs.add(5)
    s.step2(2, 2)
    attend_step(1)
    attend_step(0)
    pairs.add(6)
    s.step3(2, 1)
    s.step1(1, 1)
    pairs.add(7)
    second.wait_recv()
    second.wait_send()
    packed = sent
    spread_columns(grads, packed)
    push_packed = send(packed, packed_other, partner)
    s.step2(1, 1)
    total = [jnp.zeros((256, 640), F32), jnp.zeros((256, 640), F32)]

    def back_through(p):
        mine = rows_of(packed, p)
        for half in range(2):
            n = 2 * p + half
            loads[n].wait()
            total[half] += dot_nt(mine, w[half].reshape(640, 512))
            if n + 2 < 16:
                loads[n + 2] = fetch(n + 2)
        d_bias[p:p + 1] = jnp.sum(mine.astype(F32), axis=0, keepdims=True)

    for p in range(3):
        back_through(p)
    s.step3(1, 1)
    s.step1(0, 1)
    for p in range(3, 6):
        back_through(p)
    s.step3(0, 1)
    send.finish(s.copies_of(2, 1))
    for device in ring_devices(pos, core):
        pl.semaphore_signal(free_sem, inc=1, device_id=device, device_id_type=MESH)
    s.step3(2, 2)
    s.step1(1, 2)
    for p in range(6, 8):
        back_through(p)
    push_nt.wait_recv()
    push_packed.wait_recv()

    def weight_grad(p):
        both = dot(nt[:, core].reshape(640, 256), rows_of(packed, p)) + dot(nt_other[...].reshape(640, 256), rows_of(packed_other, p))
        sum_fc[p // 4, p % 4, :, :, :, 0:512] = both.astype(BF).reshape(4, 2, 80, 512)

    for p in range(4):
        weight_grad(p)
    s.step2(1, 2)
    for p in range(4, 8):
        weight_grad(p)
    pl.semaphore_wait(free_sem, 9)
    s.step1(2, 0)
    s.step3(1, 2)
    s.step1(0, 2)
    u, r = norm_parts(tokens[...].astype(F32))
    back, dg, db = norm_back(u, r, vecs[0:1], jnp.concatenate(total, axis=1))
    bring.wait()
    input_grad[...] = input_grad[...] + back
    s.step2(2, 0)
    for h, part in enumerate(pack_vectors(plain, qkv_table, fc_table, (dg, db), d_bias, d_mid, d_bias_fc)):
        d_vec[:, :, :, :, h] = part.reshape(2, 4, 4, 2, 16, 128)
    push = send(d_vec.at[:, :, :, :, 1 - core], got_vec, partner)
    s.step3(0, 2)
    s.step3(2, 0)
    s.step1(1, 0)
    push.wait_recv()
    d_vec[:, :, :, :, core] = d_vec[:, :, :, :, core] + got_vec[...]
    s.step1(2, 4)
    s.step2(1, 0)
    s.step2(2, 4)
    s.step3(2, 4)
    s.step1(1, 4)
    s.step3(1, 0)
    s.step1(0, 0)
    s.step2(1, 4)
    s.step3(1, 4)
    s.step1(0, 4)
    s.step3(0, 0)
    s.step3(0, 4)
    first.wait_send()
    send.finish()


BACK_SENDS = 3 + sum(15 * len(r) for r in BACK_ROUNDS.values()) + 11 * (len(ROUNDS[0]) + 1)


def back(d_out, d_fc, d_pj, mixed_grad, data, tokens, middle_grad, vecs, normed, w_all, plain, qkv_table, fc_table, d_mid,
         d_bias_fc):
    sds = jax.ShapeDtypeStruct
    whole = pl.BlockSpec(memory_space=pl.ANY)
    near = pl.BlockSpec(memory_space=VMEM)
    dma = pltpu.SemaphoreType.DMA
    big = [VMEM((2, 4, 4, 2, 80, n), BF) for n in LANES[1:]]
    return pl.pallas_call(
        back_kernel,
        out_shape=[sds((80, n), F32) for n in LANES[1:]] + [
            sds((256, 1280), F32), sds((80, 512), F32), sds((16, 128), F32)],
        in_specs=[whole] * 4 + [near] * 2 + [whole] + [near] * 2 + [whole] + [near] * 5,
        out_specs=[near] * 6,
        scratch_shapes=big + big + [VMEM((2,) + STAGES[n], BF) for n in sorted(STAGES)] + [
            VMEM((8, 128, 384), BF), VMEM((8, 128, 1024), BF), VMEM((8, 128, 1024), BF),
            VMEM((1024, 384), F32), VMEM((1024, 384), F32), VMEM((8, 2, 80, 256), BF), VMEM((8, 80, 256), BF),
            VMEM((8, 128, 1024), BF), VMEM((2, 2, 2, 2, 80, 512), BF), VMEM((8, 512), F32),
            VMEM((2, 4, 4, 2, 2, 16, 128), BF), VMEM((2, 4, 4, 2, 16, 128), BF), VMEM((2, 4, 4, 2, 16, 128), BF),
            dma((BACK_SENDS,)), dma((BACK_SENDS,)), dma((2, 5)), dma((2, 8)), dma((2, 8)), dma((2,)),
            dma((2,)), dma((1,)), pltpu.SemaphoreType.REGULAR,
        ],
        compiler_params=pltpu.CompilerParams(collective_id=1, has_side_effects=True, vmem_limit_bytes=63 * MIB),
        name="attend_back_and_scatter",
    )(d_out, d_fc, d_pj, mixed_grad, data, tokens, middle_grad, vecs, normed, w_all, plain, qkv_table, fc_table, d_mid, d_bias_fc)


GELU_A = 0.7978845608028654
GELU_B = 0.044715


def joined(mixed, s):
    return jnp.concatenate([mixed[4 * s + g, :, 0:320] for g in range(4)], axis=1)


def feed_kernel(tokens, cotangent, mixed, w_out, vecs, fc, pj, bias_fc,
                block_out, middle_grad, mixed_grad, d_fc, d_pj, d_out, d_bias_fc, d_vec,
                middle, a2, a2_t, bg_t, mixed_t, out_sum, a2_sum):
    p = pl.program_id(0)

    @pl.when(p == 0)
    def _():
        rows = jnp.concatenate([joined(mixed, 0), joined(mixed, 1)], axis=0)
        mixed_t[...] = turned(rows)
        parts = [dot(rows, w_out[n])[:, 0:160] for n in range(8)]
        total = tokens[...].astype(F32) + (jnp.concatenate(parts, axis=1) + vecs[4:5])
        middle[...] = total
        u, _ = norm_parts(total)
        low = (u * vecs[5:6] + vecs[6:7]).astype(BF)
        a2[...] = low
        a2_t[...] = turned(low)
        bg_t[...] = turned(cotangent[...])
        out_sum[...] = jnp.zeros_like(out_sum)
        a2_sum[...] = jnp.zeros_like(a2_sum)

    pre = dot(a2[...], fc[0]) + bias_fc[pl.ds(p, 1)]
    square = pre * pre
    t = jnp.tanh(GELU_A * (pre + GELU_B * pre * square))
    act = (0.5 * pre * (1.0 + t)).astype(BF)
    slope = 0.5 * (1.0 + t) + 0.5 * pre * (1.0 - t * t) * (GELU_A * (1.0 + 3.0 * GELU_B * square))
    out_sum[...] += dot_nt(act, pj[0])
    d_pj[0] = dot(bg_t[...], act).astype(BF)
    pre_grad = (slope * dot(cotangent[...], pj[0])).astype(BF)
    d_bias_fc[pl.ds(p, 1)] = jnp.sum(pre_grad.astype(F32), axis=0, keepdims=True)
    d_fc[0] = dot(a2_t[...], pre_grad).astype(BF)
    a2_sum[...] += dot_nt(pre_grad, fc[0])

    @pl.when(p == 7)
    def _():
        block_out[...] = (middle[...] + (out_sum[...] + vecs[7:8])).astype(BF)
        u, r = norm_parts(middle[...])
        dv, dg, db = norm_back(u, r, vecs[5:6], a2_sum[...])
        c = cotangent[...].astype(F32)
        total = c + dv
        middle_grad[...] = total
        low = total.astype(BF)
        d_vec[0:1] = jnp.sum(low.astype(F32), axis=0, keepdims=True)
        d_vec[1:2] = dg
        d_vec[2:3] = db
        d_vec[3:4] = jnp.sum(c, axis=0, keepdims=True)
        back_sum = jnp.zeros((256, 1280), F32)
        for n in range(8):
            mine = jnp.concatenate([low[:, 160 * n:160 * n + 160], jnp.zeros((256, 96), BF)], axis=1)
            d_out[n] = dot(mixed_t[...], mine).astype(BF)
            back_sum += dot_nt(mine, w_out[n])
        back_low = back_sum.astype(BF)
        for g in range(4):
            rows = jnp.concatenate([back_low[:, 320 * g:320 * g + 320], jnp.zeros((256, 64), BF)], axis=1)
            for s in range(2):
                mixed_grad[s * 4 + g] = rows[s * 128:(s + 1) * 128]


def feed(tokens, cotangent, mixed, w_out, vecs, fc, pj, bias_fc):
    full = lambda *shape: pl.BlockSpec(shape, lambda p: (0,) * len(shape))
    step = lambda *shape: pl.BlockSpec((1,) + shape, lambda p: (p,) + (0,) * len(shape))
    sds = jax.ShapeDtypeStruct
    return pl.pallas_call(
        feed_kernel,
        grid=(8,),
        in_specs=[full(256, 1280), full(256, 1280), full(8, 128, 384), full(8, 1280, 256), full(8, 1280),
                  step(1280, 640), step(1280, 640), full(8, 640)],
        out_specs=[full(256, 1280), full(256, 1280), full(8, 128, 384), step(1280, 640), step(1280, 640),
                   full(8, 1280, 256), full(8, 640), full(4, 1280)],
        out_shape=[sds((256, 1280), BF), sds((256, 1280), F32), sds((8, 128, 384), BF), sds((8, 1280, 640), BF),
                   sds((8, 1280, 640), BF), sds((8, 1280, 256), BF), sds((8, 640), F32), sds((4, 1280), F32)],
        scratch_shapes=[VMEM((256, 1280), F32), VMEM((256, 1280), BF), VMEM((1280, 256), BF), VMEM((1280, 256), BF),
                        VMEM((1280, 256), BF), VMEM((256, 1280), F32), VMEM((256, 1280), F32)],
        compiler_params=pltpu.CompilerParams(vmem_limit_bytes=60 * MIB),
        name="feed_forward_and_back",
    )(tokens, cotangent, mixed, w_out, vecs, fc, pj, bias_fc)


def body(tokens, segments, cotangent, w_qkv, w_out, w_fc, w_proj, *vectors):
    core = lax.rem(lax.axis_index("dp"), 2)
    pairs = [(i, i ^ 1) for i in range(16)]
    rows = jnp.concatenate(
        [vectors[n].reshape(-1, 10) for n in (0, 1, 2, 3, 4, 5, 7, 6)] + [jnp.zeros((4, 10), BF)], axis=0)
    rows = jnp.pad(rows, ((0, 64), (0, 6)))
    rows = jnp.where(core == 0, jnp.concatenate([rows, jnp.zeros_like(rows)], axis=0),
                     jnp.concatenate([jnp.zeros_like(rows), rows], axis=0))
    mine = jnp.concatenate([w_fc, w_proj.T, w_qkv, rows, w_out, jnp.zeros((160, 48), BF)], axis=1)
    mine = mine.reshape(2, 80, 1024)
    kept = lax.dynamic_index_in_dim(mine, core, 0, False)
    got = lax.ppermute(lax.dynamic_index_in_dim(mine, 1 - core, 0, False), "dp", pairs)
    one, two = jnp.where(core == 0, kept, got), jnp.where(core == 0, got, kept)
    blocks = (
        jnp.concatenate([one[:, 640:896], two[:, 640:896]], axis=1),
        jnp.concatenate([one[:, 896:976], two[:, 896:976], jnp.zeros((80, 96), BF)], axis=1),
        jnp.concatenate([one[:, 0:320], two[:, 0:320]], axis=1),
        jnp.concatenate([one[:, 320:640], two[:, 320:640]], axis=1),
    )
    select = jnp.asarray(selector(), BF)
    plain, qkv_table, fc_table = (jnp.asarray(t) for t in place_tables())
    tokens = tokens.reshape(256, 1280)
    cotangent = cotangent.reshape(256, 1280)
    seg = jnp.pad(jnp.broadcast_to(segments.reshape(256, 1).astype(BF), (256, 64)), ((0, 0), (64, 0)))
    qkv, out, fc, pj, normed, data, mixed, vecs, bias_fc = front(blocks, tokens, seg, select, plain, qkv_table, fc_table)
    (block_out, middle_grad, mixed_grad, d_fc, d_pj, d_out, d_bias_fc, d_mid) = feed(
        tokens, cotangent, mixed, out.reshape(8, 1280, 256), vecs, fc.reshape(8, 1280, 640), pj.reshape(8, 1280, 640), bias_fc)
    shape = (2, 4, 4, 2, 2, 80)
    s_out, s_fc, s_pj, input_grad, s_qkv, s_vec = back(
        d_out.reshape(shape + (256,)), d_fc.reshape(shape + (640,)), d_pj.reshape(shape + (640,)), mixed_grad, data, tokens,
        middle_grad, vecs, normed, qkv, plain, qkv_table, fc_table, d_mid, d_bias_fc)
    halves = [jnp.concatenate([s_fc[:, 320 * c:320 * c + 320], s_pj[:, 320 * c:320 * c + 320],
                               s_qkv[:, 256 * c:256 * c + 240], s_out[:, 80 * c:80 * c + 80]], axis=1) for c in range(2)]
    kept, sent = jnp.where(core == 0, halves[0], halves[1]), jnp.where(core == 0, halves[1], halves[0])
    got = lax.ppermute(sent, "dp", pairs)
    rows = jnp.concatenate([jnp.where(core == 0, kept, got), jnp.where(core == 0, got, kept)], axis=0)
    small = s_vec[:, 112:122]
    ends = tuple(small[ids[0]:ids[-1] + 1].reshape(-1) for ids in VECTOR_ROWS)
    return (block_out.reshape(2, 128, 1280), input_grad.reshape(2, 128, 1280), rows[:, 640:880], rows[:, 880:960],
            rows[:, 0:320], rows[:, 320:640].T) + ends


def solution(mesh):
    weights = (P("ctx", "dp"), P("ctx", "dp"), P("ctx", "dp"), P("dp", "ctx"))
    vectors = (P(("dp", "ctx")),) * 8
    rows = P("dp", "ctx", None)
    return jax.shard_map(
        body,
        mesh=mesh,
        in_specs=(rows, P("dp", "ctx"), rows) + weights + vectors,
        out_specs=(rows, rows) + weights + vectors,
        check_vma=False,
    )
```

```python
import numpy as np
import jax
import jax.numpy as jnp
from jax import lax
from jax.experimental import pallas as pl
from jax.experimental.pallas import tpu as pltpu
from jax.sharding import PartitionSpec as P

MESH = pl.DeviceIdType.MESH
EPSILON = 1e-05
MASKED_VALUE = -1e30
BF = jnp.bfloat16
F32 = jnp.float32
MIB = 1024 * 1024
VMEM = pltpu.VMEM


def coords():
    dp = lax.axis_index("dp")
    ctx = lax.axis_index("ctx")
    core = lax.rem(dp, 2)
    z = lax.rem(lax.div(dp, 2), 4)
    y = lax.div(dp, 8) * 2 + lax.rem(ctx, 2)
    x = lax.div(ctx, 2)
    return dict(x=x, y=y, z=z), core


def device_of(pos, core):
    dp = (lax.div(pos["y"], 2) * 4 + pos["z"]) * 2 + core
    ctx = pos["x"] * 2 + lax.rem(pos["y"], 2)
    return (dp, ctx)


def shifted(pos, axis, by):
    return {**pos, axis: lax.rem(pos[axis] + by + 4, 4)}


def ring_devices(pos, core):
    return [device_of(shifted(pos, axis, by), core) for axis in "xyz" for by in (1, -1, 2)]


def greet(pos, core, heads=False):
    barrier = pltpu.get_barrier_semaphore()
    devices = ring_devices(pos, core)
    devices.append(device_of(pos, 1 - core))
    if heads:
        dp, ctx = lax.axis_index("dp"), lax.axis_index("ctx")
        lo = lax.rem(ctx, 2)
        for by in (1, 2, 3):
            devices.append((dp, lax.rem(pos["x"] + by, 4) * 2 + 1 - lo))
    for device in devices:
        pl.semaphore_signal(barrier, inc=1, device_id=device, device_id_type=MESH)
    return lambda: pl.semaphore_wait(barrier, len(devices))


class Sender:
    def __init__(self, send_sem, recv_sem):
        self.send_sem, self.recv_sem, self.started, self.count = send_sem, recv_sem, [], 0

    def __call__(self, src, dst, device):
        i = self.count
        self.count += 1
        copy = pltpu.make_async_remote_copy(src_ref=src, dst_ref=dst, send_sem=self.send_sem.at[i],
                                            recv_sem=self.recv_sem.at[i], device_id=device, device_id_type=MESH)
        copy.start()
        self.started.append(copy)
        return copy

    def finish(self, copies=None):
        for copy in self.started if copies is None else copies:
            copy.wait_send()
        self.started = [] if copies is None else [c for c in self.started if all(c is not d for d in copies)]


ORDERS = {"A": "xyz", "B": "yzx", "C": "zxy"}
LANES = (512, 256, 640, 640)
ROUNDS = [
    [(0, "A", (0, 80), (0, 128)), (0, "B", (0, 80), (128, 256)), (0, "C", (0, 80), (256, 384)),
     (0, "A", (0, 32), (384, 512)), (0, "B", (32, 64), (384, 512)), (0, "C", (64, 80), (384, 512))],
    [(2, "A", (0, 80), (0, 384)), (2, "B", (0, 80), (384, 512)), (2, "C", (0, 80), (512, 640)),
     (1, "B", (0, 80), (0, 128)), (1, "C", (0, 80), (128, 256))],
    [(3, "A", (0, 80), (0, 384)), (3, "B", (0, 80), (384, 512)), (3, "C", (0, 80), (512, 640))],
]


def spans(where):
    out = {}
    for axis in "xz":
        v = where[axis]
        out[axis] = (0, 4) if v is None else ((v[1] * 2, 2) if isinstance(v, tuple) else (v, 1))
    v = where["y"]
    if v is None:
        hi, lo = (0, 2), (0, 2)
    elif isinstance(v, tuple):
        hi, lo = (v[1], 1), (0, 2)
    elif isinstance(v, int):
        hi, lo = (v // 2, 1), (v % 2, 1)
    else:
        hi, lo = (lax.div(v, 2), 1), (lax.rem(v, 2), 1)
    return (hi, out["z"], out["x"], lo)


def span_index(where):
    return tuple(s if n == 1 else pl.ds(s, n) for s, n in spans(where))


def part_slice(part):
    _, _, rows, lanes = part
    return (pl.ds(rows[0], rows[1] - rows[0]), pl.ds(lanes[0], lanes[1] - lanes[0]))


def where_of(pos, part, k, value, half=None):
    order = ORDERS[part[1]]
    where = {}
    for j, axis in enumerate(order):
        where[axis] = None if j < k else (value if j == k else pos[axis])
    if half is not None:
        where[order[k - 1]] = ("half", half)
    return where


class Gather:
    def __init__(self, pos, core, ins, bufs, send):
        self.pos, self.core, self.ins, self.bufs, self.send = pos, core, ins, bufs, send
        self.first, self.second = {}, {}
        self.pushes = {r: [] for r in range(len(ROUNDS))}

    def put(self, part, where, device, src=None):
        ref = self.bufs[part[0]].at[span_index(where) + (self.core,) + part_slice(part)]
        return self.send(ref if src is None else src, ref, device)

    def near(self, axis, by):
        return device_of(shifted(self.pos, axis, by), self.core)

    def partner(self):
        return device_of(self.pos, 1 - self.core)

    def step1(self, k, r):
        for part in ROUNDS[r]:
            axis = ORDERS[part[1]][k]
            where = where_of(self.pos, part, k, self.pos[axis])
            src = self.ins[part[0]].at[part_slice(part)] if k == 0 else None
            self.first[part, k] = tuple(self.put(part, where, self.near(axis, by), src) for by in ((1, -1) if k else (1, -1, 2)))
            if k == 2:
                self.pushes[r].append(self.put(part, where, self.partner()))

    def step2(self, k, r):
        for part in ROUNDS[r]:
            axis = ORDERS[part[1]][k]
            if k == 0:
                self.second[part, k] = self.first[part, k]
                continue
            right, left = self.first[part, k]
            below, above = (shifted(self.pos, axis, by)[axis] for by in (-1, 1))
            right.wait_recv()
            a = self.put(part, where_of(self.pos, part, k, below, 0), self.near(axis, 1))
            left.wait_recv()
            self.second[part, k] = (a, self.put(part, where_of(self.pos, part, k, above, 1), self.near(axis, -1)))
            if k == 2:
                self.pushes[r].append(self.put(part, where_of(self.pos, part, k, below), self.partner()))
                self.pushes[r].append(self.put(part, where_of(self.pos, part, k, above), self.partner()))

    def step3(self, k, r):
        for part in ROUNDS[r]:
            axis = ORDERS[part[1]][k]
            for copy in self.second[part, k]:
                copy.wait_recv()
            if k == 2:
                across = shifted(self.pos, axis, 2)[axis]
                self.pushes[r].append(self.put(part, where_of(self.pos, part, k, across), self.partner()))

    def finish(self, r):
        for copy in self.pushes[r]:
            copy.wait_recv()


class Heads:
    def __init__(self, src, dst, send_sem, recv_sem, local_sem, cut=()):
        self.src, self.dst, self.send_sem, self.recv_sem, self.local_sem, self.cut = src, dst, send_sem, recv_sem, local_sem, cut
        self.dp, self.ctx = lax.axis_index("dp"), lax.axis_index("ctx")

    def copy(self, o, into, arrived):
        return pltpu.make_async_remote_copy(
            src_ref=self.src.at[(o,) + self.cut], dst_ref=self.dst.at[(into,) + self.cut], send_sem=self.send_sem.at[o],
            recv_sem=self.recv_sem.at[arrived], device_id=(self.dp, o), device_id_type=MESH)

    def own(self):
        return pltpu.make_async_copy(self.src.at[(self.ctx,) + self.cut], self.dst.at[(self.ctx,) + self.cut], self.local_sem)

    def start(self, blocks):
        for o in blocks:
            @pl.when(self.ctx == o)
            def _():
                self.own().start()

            @pl.when(self.ctx != o)
            def _():
                self.copy(o, self.ctx, self.ctx).start()

    def wait_recv(self):
        self.own().wait()
        for o in range(8):
            @pl.when(self.ctx != o)
            def _():
                self.copy(o, o, o).wait_recv()

    def wait_send(self):
        for o in range(8):
            @pl.when(self.ctx != o)
            def _():
                self.copy(o, self.ctx, self.ctx).wait_send()


def dot(a, b):
    return jnp.dot(a, b, preferred_element_type=F32)


def dot_nt(a, b):
    return lax.dot_general(a, b, (((1,), (1,)), ((), ())), preferred_element_type=F32)


def dot_tn(a, b):
    return lax.dot_general(a, b, (((0,), (0,)), ((), ())), preferred_element_type=F32)


def turned(a):
    return a.astype(F32).T.astype(a.dtype)


def norm_parts(values):
    center = values - jnp.mean(values, axis=-1, keepdims=True)
    spread = jnp.mean(center * center, axis=-1, keepdims=True)
    r = lax.rsqrt(spread + EPSILON)
    return center * r, r


def norm_back(u, r, gain, e):
    n = e * gain
    dv = r * (n - jnp.mean(n, axis=-1, keepdims=True) - u * jnp.mean(n * u, axis=-1, keepdims=True))
    return dv, jnp.sum(e * u, axis=0, keepdims=True), jnp.sum(e, axis=0, keepdims=True)


VECTOR_ROWS = ((0,), (1,), (2, 3), (4,), (5,), (6,), (8, 9, 10, 11), (7,))


def selector():
    out = np.zeros((1024, 1152), np.float32)
    for m in range(3):
        for j in range(320):
            at = 320 * m + j
            out[(at // 240) * 256 + at % 240, 384 * m + j] = 1
    return out


def place_tables():
    c = np.arange(1280)
    plain = np.stack([c // 10, 0 * c, c % 10])
    c = np.arange(4096)
    off = c % 256
    n = 240 * (c // 256) + off
    e = np.where(n < 1280, n, n - 1280)
    unused = (off >= 240) | ((n >= 1280) & (n < 2560))
    qkv = np.stack([np.where(unused, -1, e // 20), 2 + (e % 20) // 10, e % 10])
    c = np.arange(5120)
    fc = np.stack([c // 40, 8 + (c % 40) // 10, c % 10])
    pad = lambda t: np.concatenate([t, np.zeros((5, t.shape[1]), t.dtype)]).astype(np.int32)
    return pad(plain), pad(qkv), pad(fc)


def row_owner(core):
    v = lax.broadcasted_iota(jnp.int32, (64, 1), 0)
    return (v // 8) * 16 + core * 8 + lax.rem(v, 8)


def row_picker(r):
    v = lax.broadcasted_iota(jnp.int32, (64, 1024), 0)
    c = lax.broadcasted_iota(jnp.int32, (64, 1024), 1)
    return (c == 16 * v + r).astype(F32).astype(BF)


def entry_picker(entry):
    lane = lax.broadcasted_iota(jnp.int32, (128, entry.shape[1]), 0)
    return (lane == 112 + entry).astype(F32).astype(BF)


def fetched_rows(buf, row_ids):
    tiles = [buf[:, :, :, :, h, 0:16, 256 * h + 128:256 * h + 256].reshape(1024, 128) for h in range(2)]
    return {r: [dot(row_picker(r), tile).astype(BF) for tile in tiles] for r in row_ids}


def take_row(rows, table, row_ids):
    owner, row, entry = table[0:1], table[1:2], table[2:3]
    pick = entry_picker(entry)
    total = jnp.zeros((1, table.shape[1]), F32)
    for h in range(2):
        mine = row_owner(h)
        for r in row_ids:
            hit = (mine == owner) if len(row_ids) == 1 else ((mine == owner) & (row == r))
            total += jnp.sum(jnp.where(hit, dot(rows[r][h], pick), 0.0), axis=0, keepdims=True)
    return total


def unpack_first(buf, plain, qkv, vecs, bias_qkv):
    rows = fetched_rows(buf, range(4))
    for r in (0, 1):
        vecs[r:r + 1] = take_row(rows, plain[...], (r,))
    for p in range(8):
        bias_qkv[p:p + 1] = take_row(rows, qkv[:, 512 * p:512 * p + 512], (2, 3))


def unpack_second(buf, plain, fc, vecs, bias_fc):
    rows = fetched_rows(buf, range(4, 12))
    vecs[2:4] = jnp.zeros((2, 1280), F32)
    for r in (4, 5, 6, 7):
        vecs[r:r + 1] = take_row(rows, plain[...], (r,))
    for p in range(8):
        bias_fc[p:p + 1] = take_row(rows, fc[:, 640 * p:640 * p + 640], (8, 9, 10, 11))


def head_lanes(rows, half):
    lane = lax.broadcasted_iota(jnp.int32, (rows, 128), 1)
    return (lane < 64) if half == 0 else (lane >= 64)


def only(values, half):
    return jnp.where(head_lanes(values.shape[0], half), values, jnp.zeros_like(values))


def swapped(values):
    return pltpu.roll(values.astype(F32), 64, 1).astype(values.dtype)


def tile_of(data, a, b, t):
    return data[a:b, :, 128 * t:128 * t + 128].reshape(128 * (b - a), 128)


def segment_views(data):
    tile = tile_of(data, 0, 8, 7).astype(F32)
    return tile[:, 64:65], jnp.transpose(tile)[64:65, :]


def mask_of(column, row, i, wide):
    rows = lax.broadcasted_iota(jnp.int32, (256, wide), 0) + 256 * i
    cols = lax.broadcasted_iota(jnp.int32, (256, wide), 1)
    keep = (cols <= rows) & (column[256 * i:256 * i + 256] == row[:, :wide])
    return jnp.where(keep, 0.0, MASKED_VALUE)


def head_tiles(data, i, j):
    n = 2 * i + 2
    if j < 2:
        return tile_of(data, 2 * i, n, j), tile_of(data, 0, n, 2 + j), tile_of(data, 0, n, 4 + j)
    return tile_of(data, 2 * i, n, 6), swapped(tile_of(data, 0, n, 6)), tile_of(data, 0, n, 7)


def attend_block(data, mixed, column, row, i):
    wide = 256 * (i + 1)
    hide = mask_of(column, row, i, wide)
    for j in range(3):
        q, k, v = head_tiles(data, i, j)
        total = None
        for half in range(2 if j < 2 else 1):
            scores = dot_nt(only(q, half) * jnp.asarray(0.125, BF), k) + hide
            e = jnp.exp(scores - jnp.max(scores, axis=-1, keepdims=True))
            soft = (e / jnp.sum(e, axis=-1, keepdims=True)).astype(BF)
            part = dot(soft, only(v, half))
            total = part if total is None else total + part
        mixed[2 * i:2 * i + 2, :, 128 * j:128 * j + 128] = total.astype(BF).reshape(2, 128, 128)


def front_kernel(kept, got, tokens, seg, select, plain, qkv_table, fc_table,
                 qkv_all, out_all, fc_all, pj_all, normed, data_all, mixed_all, vecs, bias_fc,
                 qkv, bias_qkv, packed, sent, data, mixed_sent, mixed, send_sem, recv_sem, local_sem,
                 heads_send, heads_recv, heads_local, qkv_in, out_in, fc_in, pj_in):
    pos, core = coords()
    send = Sender(send_sem, recv_sem)
    here = tuple(s for s, _ in spans(pos)) + (core,)
    for which, (one, two) in enumerate(((kept, got), (got, kept))):
        @pl.when(core == which)
        def _():
            qkv_in[...] = jnp.concatenate([one[:, 640:896], two[:, 640:896]], axis=1)
            out_in[...] = jnp.concatenate([one[:, 896:976], two[:, 896:976], jnp.zeros((80, 96), BF)], axis=1)
            fc_in[...] = jnp.concatenate([one[:, 0:320], two[:, 0:320]], axis=1)
            pj_in[...] = jnp.concatenate([one[:, 320:640], two[:, 320:640]], axis=1)

    local = [pltpu.make_async_copy(src, dst.at[here], local_sem.at[n])
             for n, (src, dst) in enumerate([(qkv_in, qkv), (out_in, out_all), (fc_in, fc_all), (pj_in, pj_all)])]
    for copy in local:
        copy.start()
    greet(pos, core, heads=True)()
    g = Gather(pos, core, (qkv_in, out_in, fc_in, pj_in), (qkv, out_all, fc_all, pj_all), send)
    g.step1(0, 0)
    g.step1(0, 1)
    g.step1(0, 2)
    for copy in local:
        copy.wait()
    g.step2(0, 0)
    g.step3(0, 0)
    g.step1(1, 0)
    g.step2(0, 1)
    g.step2(0, 2)
    g.step2(1, 0)
    g.step3(0, 1)
    g.step1(1, 1)
    g.step3(1, 0)
    g.step1(2, 0)
    g.step3(0, 2)
    g.step1(1, 2)
    g.step2(1, 1)
    g.step2(1, 2)
    g.step2(2, 0)
    g.step3(1, 1)
    g.step1(2, 1)
    u, _ = norm_parts(tokens[...].astype(F32))
    g.step3(2, 0)
    g.step3(1, 2)
    g.finish(0)

    keep = pltpu.make_async_copy(qkv, qkv_all, local_sem.at[0])
    keep.start()
    unpack_first(qkv, plain, qkv_table, vecs, bias_qkv)
    normed[...] = (u * vecs[0:1] + vecs[1:2]).astype(BF)

    def project(p, carry):
        w = qkv[lax.div(p, 4), lax.rem(p, 4)].reshape(1280, 512)
        packed[p] = (dot(normed[...], w) + bias_qkv[pl.ds(p, 1)]).astype(BF)
        return carry

    def select_three(i):
        wide = jnp.concatenate([packed[2 * i], packed[2 * i + 1]], axis=1)
        chunks = dot(wide, select[...])
        for m in range(3):
            n = 3 * i + m
            kind, group = n // 4, n % 4
            low = chunks[:, 384 * m:384 * m + 256].astype(BF)
            last = chunks[:, 384 * m + 256:384 * m + 384]
            if kind == 1:
                last = pltpu.roll(last, 64, 1)
            last = last.astype(BF)
            for s in range(2):
                at = s * 4 + group
                rows = slice(128 * s, 128 * s + 128)
                sent[at, :, 256 * kind:256 * kind + 256] = low[rows]
                if kind == 0:
                    sent[at, :, 768:896] = last[rows]
                elif kind == 1:
                    sent[at, :, 768:896] = sent[at, :, 768:896] + last[rows]
                else:
                    sent[at, :, 896:1024] = last[rows] + seg[rows]

    pieces = [Heads(sent, data, heads_send.at[n], heads_recv.at[n], heads_local.at[n], (slice(None), pl.ds(a, b - a)))
              for n, (a, b) in enumerate(((0, 256), (256, 512), (512, 1024)))]
    lax.fori_loop(0, 4, project, 0)
    select_three(0)
    select_three(1)
    pieces[0].start(range(8))
    lax.fori_loop(4, 6, project, 0)
    select_three(2)
    pieces[1].start(range(8))
    lax.fori_loop(6, 8, project, 0)
    select_three(3)
    pieces[2].start(range(8))
    g.step1(2, 2)
    g.step2(2, 1)
    unpack_second(qkv, plain, fc_table, vecs, bias_fc)
    for piece in pieces:
        piece.wait_recv()
    keep_data = pltpu.make_async_copy(data, data_all, local_sem.at[1])
    keep_data.start()
    column, row = segment_views(data)
    back = Heads(mixed_sent, mixed, heads_send.at[3], heads_recv.at[3], heads_local.at[3])
    for i in range(4):
        attend_block(data, mixed_sent, column, row, i)
        back.start((2 * i, 2 * i + 1))
        if i == 1:
            g.step2(2, 2)
    g.step3(2, 1)
    back.wait_recv()
    keep_mixed = pltpu.make_async_copy(mixed, mixed_all, local_sem.at[2])
    keep_mixed.start()
    g.step3(2, 2)
    g.finish(1)
    g.finish(2)
    keep.wait()
    keep_data.wait()
    keep_mixed.wait()
    for piece in pieces:
        piece.wait_send()
    back.wait_send()
    send.finish()


FRONT_SENDS = 15 * sum(len(r) for r in ROUNDS)


def front(kept, got, tokens, seg, select, plain, qkv_table, fc_table):
    sds = jax.ShapeDtypeStruct
    whole = pl.BlockSpec(memory_space=pl.ANY)
    near = pl.BlockSpec(memory_space=VMEM)
    return pl.pallas_call(
        front_kernel,
        out_shape=[sds((2, 4, 4, 2, 2, 80, n), BF) for n in LANES] + [
            sds((256, 1280), BF), sds((8, 128, 1024), BF), sds((8, 128, 384), BF), sds((8, 1280), F32), sds((8, 640), F32)],
        in_specs=[near] * 8,
        out_specs=[whole] * 4 + [near, whole, whole, near, near],
        scratch_shapes=[
            VMEM((2, 4, 4, 2, 2, 80, 512), BF), VMEM((8, 512), F32), VMEM((8, 256, 512), BF), VMEM((8, 128, 1024), BF),
            VMEM((8, 128, 1024), BF), VMEM((8, 128, 384), BF), VMEM((8, 128, 384), BF),
            pltpu.SemaphoreType.DMA((FRONT_SENDS,)), pltpu.SemaphoreType.DMA((FRONT_SENDS,)), pltpu.SemaphoreType.DMA((4,)),
            pltpu.SemaphoreType.DMA((4, 8)), pltpu.SemaphoreType.DMA((4, 8)), pltpu.SemaphoreType.DMA((4,)),
            VMEM((80, 512), BF), VMEM((80, 256), BF), VMEM((80, 640), BF), VMEM((80, 640), BF),
        ],
        compiler_params=pltpu.CompilerParams(collective_id=0, has_side_effects=True, vmem_limit_bytes=60 * MIB),
        name="fetch_and_attend",
    )(kept, got, tokens, seg, select, plain, qkv_table, fc_table)


def attend_back_block(data, grad, out, dk, dv, column, row, i):
    wide = 256 * (i + 1)
    hide = mask_of(column, row, i, wide)
    for j in range(3):
        q, k, v = head_tiles(data, i, j)
        q = q * jnp.asarray(0.125, BF)
        lanes = slice(128 * j, 128 * j + 128)
        g = grad[2 * i:2 * i + 2, :, lanes].reshape(256, 128)
        total = None
        for half in range(2 if j < 2 else 1):
            qh, gh = only(q, half), only(g, half)
            scores = dot_nt(qh, k) + hide
            e = jnp.exp(scores - jnp.max(scores, axis=-1, keepdims=True))
            soft = e / jnp.sum(e, axis=-1, keepdims=True)
            dv[0:wide, lanes] += dot_tn(soft.astype(BF), gh)
            sg = dot_nt(gh, v)
            sg = (soft * (sg - jnp.sum(soft * sg, axis=-1, keepdims=True))).astype(BF)
            dk[0:wide, lanes] += dot_tn(sg, qh)
            part = dot(sg, only(k, half)) * 0.125
            total = part if total is None else total + part
        t = j if j < 2 else 6
        out[2 * i:2 * i + 2, :, 128 * t:128 * t + 128] = total.astype(BF).reshape(2, 128, 128)


def attend_back_end(out, dk, dv, i):
    rows, blocks = slice(256 * i, 256 * i + 256), slice(2 * i, 2 * i + 2)
    for j in range(2):
        lanes = slice(128 * j, 128 * j + 128)
        out[blocks, :, 256 + 128 * j:384 + 128 * j] = dk[rows, lanes].astype(BF).reshape(2, 128, 128)
        out[blocks, :, 512 + 128 * j:640 + 128 * j] = dv[rows, lanes].astype(BF).reshape(2, 128, 128)
    last = pltpu.roll(dk[rows, 256:384], 64, 1).astype(BF).reshape(2, 128, 128)
    out[blocks, :, 768:896] = out[blocks, :, 768:896] + last
    out[blocks, :, 896:1024] = dv[rows, 256:384].astype(BF).reshape(2, 128, 128)


class Scatter:
    def __init__(self, pos, core, sums, slots, outs, send, rounds, base=None):
        self.base = base or {}
        self.pos, self.core, self.sums, self.slots, self.outs, self.send = pos, core, sums, slots, outs, send
        self.rounds, self.first, self.second = rounds, {}, {}

    def near(self, axis, by):
        return device_of(shifted(self.pos, axis, by), self.core)

    def slot_of(self, part, k, slot, half=None):
        order = ORDERS[part[1]]
        where = {}
        for j, axis in enumerate(order):
            where[axis] = None if j < k else (slot if j == k else 3)
        if half is not None:
            where[order[k - 1]] = ("half", half)
        return where

    def sum_at(self, t, idx):
        ref, halves = self.sums[t]
        return ref, (idx + (self.core,) if halves else idx)

    def cut(self, part):
        base = self.base.get(part[0], 0)
        return part_slice((part[0], part[1], part[2], (part[3][0] - base, part[3][1] - base)))

    def sum_view(self, part, where):
        ref, idx = self.sum_at(part[0], span_index(where))
        return ref.at[idx + self.cut(part)]

    def slot_view(self, part, where):
        return self.slots[part[0]].at[span_index(where) + self.cut(part)]

    def add_slot(self, part, where, slot):
        ref, idx = self.sum_at(part[0], span_index(where))
        here = idx + self.cut(part)
        ref[here] = ref[here] + self.slots[part[0]][span_index(slot) + self.cut(part)]

    def step1(self, k, r):
        for part in self.rounds[r]:
            axis = ORDERS[part[1]][k]
            across = shifted(self.pos, axis, 2)[axis]

            def out(half, by):
                return self.send(self.sum_view(part, where_of(self.pos, part, k, across, half)),
                                 self.slot_view(part, self.slot_of(part, k, 0, half)), self.near(axis, by))

            def straight(slot, by):
                return self.send(self.sum_view(part, where_of(self.pos, part, k, shifted(self.pos, axis, by)[axis])),
                                 self.slot_view(part, self.slot_of(part, k, slot)), self.near(axis, by))

            if k == 0:
                self.second[part, k] = (straight(0, 2), straight(1, 1), straight(2, -1))
            else:
                self.first[part, k] = (out(0, 1), out(1, -1))

    def step2(self, k, r):
        for part in self.rounds[r] if k else ():
            axis = ORDERS[part[1]][k]
            above, below = (shifted(self.pos, axis, by)[axis] for by in (1, -1))
            first = self.first[part, k]
            first[0].wait_recv()
            self.add_slot(part, where_of(self.pos, part, k, above, 0), self.slot_of(part, k, 0, 0))
            a = self.send(self.sum_view(part, where_of(self.pos, part, k, above)),
                          self.slot_view(part, self.slot_of(part, k, 1)), self.near(axis, 1))
            first[1].wait_recv()
            self.add_slot(part, where_of(self.pos, part, k, below, 1), self.slot_of(part, k, 0, 1))
            b = self.send(self.sum_view(part, where_of(self.pos, part, k, below)),
                          self.slot_view(part, self.slot_of(part, k, 2)), self.near(axis, -1))
            self.second[part, k] = (a, b)

    def copies_of(self, t, r):
        return [c for part in self.rounds[r] if part[0] == t for k in range(3) for held in (self.first, self.second)
                for c in held.get((part, k), ())]

    def step3(self, k, r):
        for part in self.rounds[r]:
            t = part[0]
            axis = ORDERS[part[1]][k]
            for copy in self.second[part, k]:
                copy.wait_recv()
            cut = self.cut(part)
            ref, idx = self.sum_at(t, span_index(where_of(self.pos, part, k, self.pos[axis])))
            slots = self.slots[t]
            total = (ref[idx + cut].astype(F32) + slots[span_index(self.slot_of(part, k, 1)) + cut].astype(F32)
                     + slots[span_index(self.slot_of(part, k, 2)) + cut].astype(F32))
            if k == 0:
                self.outs[t][part_slice(part)] = total + slots[span_index(self.slot_of(part, k, 0)) + cut].astype(F32)
            else:
                ref[idx + cut] = total.astype(BF)


class Pairs:
    def __init__(self, scatter, grads, stages, stage_sem, order):
        self.s, self.grads, self.stages, self.stage_sem, self.order = scatter, grads, stages, stage_sem, order
        self.pushed, self.loads = {}, {}

    def where(self, part, which):
        axis = ORDERS[part[1]][2]
        return where_of(self.s.pos, part, 2, shifted(self.s.pos, axis, which)[axis])

    def stage_names(self, r):
        seen = {}
        for part in self.s.rounds[r]:
            n = seen.get(part[1], 0)
            seen[part[1]] = n + 1
            yield part, part[1] + str(n)

    def push_all(self):
        s = self.s
        for r, which in self.order:
            for part in s.rounds[r]:
                where = self.where(part, which)
                src = self.grads[part[0]].at[span_index(where) + (1 - s.core,) + part_slice(part)]
                self.pushed[part, which] = s.send(src, s.sum_view(part, where), device_of(s.pos, 1 - s.core))

    def load(self, n):
        if n >= len(self.order):
            return
        r, which = self.order[n]
        for j, (part, name) in enumerate(self.stage_names(r)):
            src = self.grads[part[0]].at[span_index(self.where(part, which)) + (self.s.core,) + part_slice(part)]
            dst = self.stages[name].at[n % 2].at[..., pl.ds(0, part[2][1] - part[2][0]), pl.ds(0, part[3][1] - part[3][0])]
            copy = pltpu.make_async_copy(src, dst, self.stage_sem.at[n % 2, j])
            copy.start()
            self.loads[n, part] = copy

    def add(self, n):
        r, which = self.order[n]
        s = self.s
        for part, name in self.stage_names(r):
            self.loads[n, part].wait()
            self.pushed[part, which].wait_recv()
            where = self.where(part, which)
            ref, idx = s.sum_at(part[0], span_index(where))
            here = idx + s.cut(part)
            stage = self.stages[name].at[n % 2]
            ref[here] = ref[here] + stage[..., pl.ds(0, part[2][1] - part[2][0]), pl.ds(0, part[3][1] - part[3][0])]
        self.load(n + 2)


def pack_vectors(plain, qkv, fc, d_pre, d_bias_qkv, d_mid, d_bias_fc):
    out = []
    for h in range(2):
        mine = row_owner(h)
        rows = {}

        def give(table, values, row_ids):
            owner, row, entry = table[0:1], table[1:2], table[2:3]
            pick = entry_picker(entry)
            low = values.astype(BF).astype(F32)
            for r in row_ids:
                hit = (mine == owner) if len(row_ids) == 1 else ((mine == owner) & (row == r))
                part = dot_nt(jnp.where(hit, low, 0.0).astype(BF), pick)
                rows[r] = rows[r] + part if r in rows else part

        for r, values in ((0, d_pre[0]), (1, d_pre[1]), (4, d_mid[0:1]), (5, d_mid[1:2]), (6, d_mid[2:3]), (7, d_mid[3:4])):
            give(plain[...], values, (r,))
        for p in range(8):
            give(qkv[:, 512 * p:512 * p + 512], d_bias_qkv[p:p + 1], (2, 3))
            give(fc[:, 640 * p:640 * p + 640], d_bias_fc[p:p + 1], (8, 9, 10, 11))
        total = jnp.zeros((1024, 128), F32)
        for r in range(12):
            total += dot_tn(row_picker(r), rows[r].astype(BF))
        out.append(total.astype(BF))
    return out


BACK_ROUNDS = {
    1: [(2, "A", (0, 80), (0, 384)), (2, "B", (0, 80), (384, 512)), (2, "C", (0, 80), (512, 640)), (1, "B", (0, 80), (0, 128))],
    2: [(3, "A", (0, 80), (0, 384)), (3, "B", (0, 80), (384, 512)), (3, "C", (0, 80), (512, 640)), (1, "C", (0, 80), (128, 256))],
}
VECTOR_ROUND = [(4, "A", (0, 16), (0, 128))]
BACK_ORDER = [(1, 2), (2, 2), (1, 1), (1, -1), (2, 1), (2, -1), (1, 0), (2, 0)]
STAGES = {"A0": (2, 4, 2, 80, 384), "B0": (2, 4, 2, 80, 128), "B1": (2, 4, 2, 80, 128), "C0": (4, 4, 80, 128),
          "C1": (4, 4, 80, 128)}


def spread_columns(grads, packed):
    for i in range(4):
        chunks = []
        for m in range(3):
            n = 3 * i + m
            kind, group = n // 4, n % 4
            last = (768, 832, 896)[kind]
            pair = [jnp.concatenate([grads[at, :, 256 * kind:256 * kind + 256], grads[at, :, last:last + 64]], axis=1)
                    for at in (group, 4 + group)]
            chunks.append(jnp.concatenate(pair, axis=0))
        wide = jnp.concatenate(chunks, axis=1)
        blank = jnp.zeros((256, 16), BF)
        for m in range(2):
            both = jnp.concatenate([wide[:, 480 * m:480 * m + 240], blank, wide[:, 480 * m + 240:480 * m + 480], blank], axis=1)
            packed[2 * i + m, :, 0:512] = both[0:128]
            packed[2 * i + m, :, 512:1024] = both[128:256]


def rows_of(packed, p):
    return jnp.concatenate([packed[p, :, 0:512], packed[p, :, 512:1024]], axis=0)


def back_kernel(d_out, d_fc, d_pj, mixed_grad, data, tokens, middle_grad, vecs, normed, w_all, plain, qkv_table, fc_table,
                d_mid, d_bias_fc, kept, given, input_grad, s_vec,
                sum_out, sum_fc, sum_pj, slot_out, slot_fc, slot_pj, *rest):
    stages = dict(zip(sorted(STAGES), rest[:5]))
    (grad, sent, grads, dk, dv, nt, nt_other, packed_other, w, d_bias, d_vec, got_vec, slot_vec, send_sem, recv_sem, stage_sem, heads_send,
     heads_recv, heads_local, w_sem, mg_sem, free_sem, s_out, s_fc, s_pj, s_qkv) = rest[5:]
    pos, core = coords()
    partner = device_of(pos, 1 - core)
    send = Sender(send_sem, recv_sem)
    s = Scatter(pos, core, {0: (sum_fc, False), 1: (sum_out, False), 2: (sum_fc, False), 3: (sum_pj, False), 4: (d_vec, True)},
                {0: slot_fc, 1: slot_out, 2: slot_fc, 3: slot_pj, 4: slot_vec},
                {0: s_qkv, 1: s_out, 2: s_fc, 3: s_pj, 4: s_vec}, send, {**BACK_ROUNDS, 0: ROUNDS[0], 4: VECTOR_ROUND})
    pairs = Pairs(s, {1: d_out, 2: d_fc, 3: d_pj}, stages, stage_sem, BACK_ORDER)
    pairs.load(0)
    pairs.load(1)
    bring = pltpu.make_async_copy(middle_grad, input_grad, mg_sem.at[0])
    bring.start()

    def fetch(n):
        copy = pltpu.make_async_copy(w_all.at[n // 8, n // 2 % 4, pl.ds(n % 2 * 2, 2)], w.at[n % 2], w_sem.at[n % 2])
        copy.start()
        return copy

    loads = {0: fetch(0), 1: fetch(1)}
    others_here = greet(pos, core, heads=True)
    nt[...] = turned(normed[...]).reshape(8, 2, 80, 256)
    others_here()
    first = Heads(mixed_grad, grad, heads_send.at[0], heads_recv.at[0], heads_local.at[0])
    second = Heads(sent, grads, heads_send.at[1], heads_recv.at[1], heads_local.at[1])
    first.start(range(8))
    pairs.push_all()
    push_nt = send(nt.at[:, 1 - core], nt_other, partner)
    dk[...] = jnp.zeros_like(dk)
    dv[...] = jnp.zeros_like(dv)
    column, row = segment_views(data)

    def attend_step(i):
        attend_back_block(data, grad, sent, dk, dv, column, row, i)
        attend_back_end(sent, dk, dv, i)
        second.start((2 * i, 2 * i + 1))

    pairs.add(0)
    s.step1(2, 1)
    pairs.add(1)
    s.step1(2, 2)
    first.wait_recv()
    attend_step(3)
    pairs.add(2)
    pairs.add(3)
    s.step2(2, 1)
    attend_step(2)
    pairs.add(4)
    pairs.add(5)
    s.step2(2, 2)
    attend_step(1)
    attend_step(0)
    pairs.add(6)
    s.step3(2, 1)
    s.step1(1, 1)
    pairs.add(7)
    second.wait_recv()
    second.wait_send()
    packed = sent
    spread_columns(grads, packed)
    push_packed = send(packed, packed_other, partner)
    s.step2(1, 1)
    total = [jnp.zeros((256, 640), F32), jnp.zeros((256, 640), F32)]

    def back_through(p):
        mine = rows_of(packed, p)
        for half in range(2):
            n = 2 * p + half
            loads[n].wait()
            total[half] += dot_nt(mine, w[half].reshape(640, 512))
            if n + 2 < 16:
                loads[n + 2] = fetch(n + 2)
        d_bias[p:p + 1] = jnp.sum(mine.astype(F32), axis=0, keepdims=True)

    for p in range(3):
        back_through(p)
    s.step3(1, 1)
    s.step1(0, 1)
    for p in range(3, 6):
        back_through(p)
    s.step3(0, 1)
    send.finish(s.copies_of(2, 1))
    for device in ring_devices(pos, core):
        pl.semaphore_signal(free_sem, inc=1, device_id=device, device_id_type=MESH)
    s.step3(2, 2)
    s.step1(1, 2)
    for p in range(6, 8):
        back_through(p)
    push_nt.wait_recv()
    push_packed.wait_recv()

    def weight_grad(p):
        both = dot(nt[:, core].reshape(640, 256), rows_of(packed, p)) + dot(nt_other[...].reshape(640, 256), rows_of(packed_other, p))
        sum_fc[p // 4, p % 4, :, :, :, 0:512] = both.astype(BF).reshape(4, 2, 80, 512)

    for p in range(4):
        weight_grad(p)
    s.step2(1, 2)
    for p in range(4, 8):
        weight_grad(p)
    pl.semaphore_wait(free_sem, 9)
    s.step1(2, 0)
    s.step3(1, 2)
    s.step1(0, 2)
    u, r = norm_parts(tokens[...].astype(F32))
    back, dg, db = norm_back(u, r, vecs[0:1], jnp.concatenate(total, axis=1))
    bring.wait()
    input_grad[...] = input_grad[...] + back
    s.step2(2, 0)
    for h, part in enumerate(pack_vectors(plain, qkv_table, fc_table, (dg, db), d_bias, d_mid, d_bias_fc)):
        d_vec[:, :, :, :, h] = part.reshape(2, 4, 4, 2, 16, 128)
    push = send(d_vec.at[:, :, :, :, 1 - core], got_vec, partner)
    s.step3(0, 2)
    s.step3(2, 0)
    s.step1(1, 0)
    push.wait_recv()
    d_vec[:, :, :, :, core] = d_vec[:, :, :, :, core] + got_vec[...]
    s.step1(2, 4)
    s.step2(1, 0)
    s.step2(2, 4)
    s.step3(2, 4)
    s.step1(1, 4)
    s.step3(1, 0)
    s.step1(0, 0)
    s.step2(1, 4)
    s.step3(1, 4)
    s.step1(0, 4)
    s.step3(0, 0)
    for c in range(2):
        mine = jnp.concatenate([s_fc[:, 320 * c:320 * c + 320], s_pj[:, 320 * c:320 * c + 320],
                                s_qkv[:, 256 * c:256 * c + 240], s_out[:, 80 * c:80 * c + 80]], axis=1)

        @pl.when(core == c)
        def _():
            kept[...] = mine

        @pl.when(core != c)
        def _():
            given[...] = mine

    s.step3(0, 4)
    first.wait_send()
    send.finish()


BACK_SENDS = 3 + sum(15 * len(r) for r in BACK_ROUNDS.values()) + 11 * (len(ROUNDS[0]) + 1)


def back(d_out, d_fc, d_pj, mixed_grad, data, tokens, middle_grad, vecs, normed, w_all, plain, qkv_table, fc_table, d_mid,
         d_bias_fc):
    sds = jax.ShapeDtypeStruct
    whole = pl.BlockSpec(memory_space=pl.ANY)
    near = pl.BlockSpec(memory_space=VMEM)
    dma = pltpu.SemaphoreType.DMA
    big = [VMEM((2, 4, 4, 2, 80, n), BF) for n in LANES[1:]]
    return pl.pallas_call(
        back_kernel,
        out_shape=[sds((80, 960), F32), sds((80, 960), F32), sds((256, 1280), F32), sds((16, 128), F32)],
        in_specs=[whole] * 4 + [near] * 2 + [whole] + [near] * 2 + [whole] + [near] * 5,
        out_specs=[near] * 4,
        scratch_shapes=big + big + [VMEM((2,) + STAGES[n], BF) for n in sorted(STAGES)] + [
            VMEM((8, 128, 384), BF), VMEM((8, 128, 1024), BF), VMEM((8, 128, 1024), BF),
            VMEM((1024, 384), F32), VMEM((1024, 384), F32), VMEM((8, 2, 80, 256), BF), VMEM((8, 80, 256), BF),
            VMEM((8, 128, 1024), BF), VMEM((2, 2, 2, 2, 80, 512), BF), VMEM((8, 512), F32),
            VMEM((2, 4, 4, 2, 2, 16, 128), BF), VMEM((2, 4, 4, 2, 16, 128), BF), VMEM((2, 4, 4, 2, 16, 128), BF),
            dma((BACK_SENDS,)), dma((BACK_SENDS,)), dma((2, 5)), dma((2, 8)), dma((2, 8)), dma((2,)),
            dma((2,)), dma((1,)), pltpu.SemaphoreType.REGULAR,
        ] + [VMEM((80, n), F32) for n in LANES[1:] + LANES[:1]],
        compiler_params=pltpu.CompilerParams(collective_id=1, has_side_effects=True, vmem_limit_bytes=63 * MIB),
        name="attend_back_and_scatter",
    )(d_out, d_fc, d_pj, mixed_grad, data, tokens, middle_grad, vecs, normed, w_all, plain, qkv_table, fc_table, d_mid, d_bias_fc)


GELU_A = 0.7978845608028654
GELU_B = 0.044715


def joined(mixed, s):
    return jnp.concatenate([mixed[4 * s + g, :, 0:320] for g in range(4)], axis=1)


def feed_kernel(tokens, cotangent, mixed, w_out, vecs, fc, pj, bias_fc,
                block_out, middle_grad, mixed_grad, d_fc, d_pj, d_out, d_bias_fc, d_vec,
                middle, a2, a2_t, bg_t, mixed_t, out_sum, a2_sum):
    p = pl.program_id(0)

    @pl.when(p == 0)
    def _():
        rows = jnp.concatenate([joined(mixed, 0), joined(mixed, 1)], axis=0)
        mixed_t[...] = turned(rows)
        parts = [dot(rows, w_out[n])[:, 0:160] for n in range(8)]
        total = tokens[...].astype(F32) + (jnp.concatenate(parts, axis=1) + vecs[4:5])
        middle[...] = total
        u, _ = norm_parts(total)
        low = (u * vecs[5:6] + vecs[6:7]).astype(BF)
        a2[...] = low
        a2_t[...] = turned(low)
        bg_t[...] = turned(cotangent[...])
        out_sum[...] = jnp.zeros_like(out_sum)
        a2_sum[...] = jnp.zeros_like(a2_sum)

    pre = dot(a2[...], fc[0]) + bias_fc[pl.ds(p, 1)]
    square = pre * pre
    t = jnp.tanh(GELU_A * (pre + GELU_B * pre * square))
    act = (0.5 * pre * (1.0 + t)).astype(BF)
    slope = 0.5 * (1.0 + t) + 0.5 * pre * (1.0 - t * t) * (GELU_A * (1.0 + 3.0 * GELU_B * square))
    out_sum[...] += dot_nt(act, pj[0])
    d_pj[0] = dot(bg_t[...], act).astype(BF)
    pre_grad = (slope * dot(cotangent[...], pj[0])).astype(BF)
    d_bias_fc[pl.ds(p, 1)] = jnp.sum(pre_grad.astype(F32), axis=0, keepdims=True)
    d_fc[0] = dot(a2_t[...], pre_grad).astype(BF)
    a2_sum[...] += dot_nt(pre_grad, fc[0])

    @pl.when(p == 7)
    def _():
        block_out[...] = (middle[...] + (out_sum[...] + vecs[7:8])).astype(BF)
        u, r = norm_parts(middle[...])
        dv, dg, db = norm_back(u, r, vecs[5:6], a2_sum[...])
        c = cotangent[...].astype(F32)
        total = c + dv
        middle_grad[...] = total
        low = total.astype(BF)
        d_vec[0:1] = jnp.sum(low.astype(F32), axis=0, keepdims=True)
        d_vec[1:2] = dg
        d_vec[2:3] = db
        d_vec[3:4] = jnp.sum(c, axis=0, keepdims=True)
        back_sum = jnp.zeros((256, 1280), F32)
        for n in range(8):
            mine = jnp.concatenate([low[:, 160 * n:160 * n + 160], jnp.zeros((256, 96), BF)], axis=1)
            d_out[n] = dot(mixed_t[...], mine).astype(BF)
            back_sum += dot_nt(mine, w_out[n])
        back_low = back_sum.astype(BF)
        for g in range(4):
            rows = jnp.concatenate([back_low[:, 320 * g:320 * g + 320], jnp.zeros((256, 64), BF)], axis=1)
            for s in range(2):
                mixed_grad[s * 4 + g] = rows[s * 128:(s + 1) * 128]


def feed(tokens, cotangent, mixed, w_out, vecs, fc, pj, bias_fc):
    full = lambda *shape: pl.BlockSpec(shape, lambda p: (0,) * len(shape))
    step = lambda *shape: pl.BlockSpec((1,) + shape, lambda p: (p,) + (0,) * len(shape))
    sds = jax.ShapeDtypeStruct
    return pl.pallas_call(
        feed_kernel,
        grid=(8,),
        in_specs=[full(256, 1280), full(256, 1280), full(8, 128, 384), full(8, 1280, 256), full(8, 1280),
                  step(1280, 640), step(1280, 640), full(8, 640)],
        out_specs=[full(256, 1280), full(256, 1280), full(8, 128, 384), step(1280, 640), step(1280, 640),
                   full(8, 1280, 256), full(8, 640), full(4, 1280)],
        out_shape=[sds((256, 1280), BF), sds((256, 1280), F32), sds((8, 128, 384), BF), sds((8, 1280, 640), BF),
                   sds((8, 1280, 640), BF), sds((8, 1280, 256), BF), sds((8, 640), F32), sds((4, 1280), F32)],
        scratch_shapes=[VMEM((256, 1280), F32), VMEM((256, 1280), BF), VMEM((1280, 256), BF), VMEM((1280, 256), BF),
                        VMEM((1280, 256), BF), VMEM((256, 1280), F32), VMEM((256, 1280), F32)],
        compiler_params=pltpu.CompilerParams(vmem_limit_bytes=60 * MIB),
        name="feed_forward_and_back",
    )(tokens, cotangent, mixed, w_out, vecs, fc, pj, bias_fc)


def body(tokens, segments, cotangent, w_qkv, w_out, w_fc, w_proj, *vectors):
    core = lax.rem(lax.axis_index("dp"), 2)
    pairs = [(i, i ^ 1) for i in range(16)]
    rows = jnp.concatenate(
        [vectors[n].reshape(-1, 10) for n in (0, 1, 2, 3, 4, 5, 7, 6)] + [jnp.zeros((4, 10), BF)], axis=0)
    rows = jnp.pad(rows, ((0, 64), (0, 6)))
    rows = jnp.where(core == 0, jnp.concatenate([rows, jnp.zeros_like(rows)], axis=0),
                     jnp.concatenate([jnp.zeros_like(rows), rows], axis=0))
    mine = jnp.concatenate([w_fc, w_proj.T, w_qkv, rows, w_out, jnp.zeros((160, 48), BF)], axis=1)
    mine = mine.reshape(2, 80, 1024)
    kept = lax.dynamic_index_in_dim(mine, core, 0, False)
    got = lax.ppermute(lax.dynamic_index_in_dim(mine, 1 - core, 0, False), "dp", pairs)
    select = jnp.asarray(selector(), BF)
    plain, qkv_table, fc_table = (jnp.asarray(t) for t in place_tables())
    tokens = tokens.reshape(256, 1280)
    cotangent = cotangent.reshape(256, 1280)
    seg = jnp.pad(jnp.broadcast_to(segments.reshape(256, 1).astype(BF), (256, 64)), ((0, 0), (64, 0)))
    qkv, out, fc, pj, normed, data, mixed, vecs, bias_fc = front(kept, got, tokens, seg, select, plain, qkv_table, fc_table)
    (block_out, middle_grad, mixed_grad, d_fc, d_pj, d_out, d_bias_fc, d_mid) = feed(
        tokens, cotangent, mixed, out.reshape(8, 1280, 256), vecs, fc.reshape(8, 1280, 640), pj.reshape(8, 1280, 640), bias_fc)
    shape = (2, 4, 4, 2, 2, 80)
    kept, given, input_grad, s_vec = back(
        d_out.reshape(shape + (256,)), d_fc.reshape(shape + (640,)), d_pj.reshape(shape + (640,)), mixed_grad, data, tokens,
        middle_grad, vecs, normed, qkv, plain, qkv_table, fc_table, d_mid, d_bias_fc)
    got = lax.ppermute(given, "dp", pairs)
    rows = jnp.concatenate([jnp.where(core == 0, kept, got), jnp.where(core == 0, got, kept)], axis=0)
    small = s_vec[:, 112:122]
    ends = tuple(small[ids[0]:ids[-1] + 1].reshape(-1) for ids in VECTOR_ROWS)
    return (block_out.reshape(2, 128, 1280), input_grad.reshape(2, 128, 1280), rows[:, 640:880], rows[:, 880:960],
            rows[:, 0:320], rows[:, 320:640].T) + ends


def solution(mesh):
    weights = (P("ctx", "dp"), P("ctx", "dp"), P("ctx", "dp"), P("dp", "ctx"))
    vectors = (P(("dp", "ctx")),) * 8
    rows = P("dp", "ctx", None)
    return jax.shard_map(
        body,
        mesh=mesh,
        in_specs=(rows, P("dp", "ctx"), rows) + weights + vectors,
        out_specs=(rows, rows) + weights + vectors,
        check_vma=False,
    )
```

```python
import numpy as np
import jax
import jax.numpy as jnp
from jax import lax
from jax.experimental import pallas as pl
from jax.experimental.pallas import tpu as pltpu
from jax.sharding import PartitionSpec as P

MESH = pl.DeviceIdType.MESH
EPSILON = 1e-05
MASKED_VALUE = -1e30
BF = jnp.bfloat16
F32 = jnp.float32
MIB = 1024 * 1024
VMEM = pltpu.VMEM


def coords():
    dp = lax.axis_index("dp")
    ctx = lax.axis_index("ctx")
    core = lax.rem(dp, 2)
    z = lax.rem(lax.div(dp, 2), 4)
    y = lax.div(dp, 8) * 2 + lax.rem(ctx, 2)
    x = lax.div(ctx, 2)
    return dict(x=x, y=y, z=z), core


def device_of(pos, core):
    dp = (lax.div(pos["y"], 2) * 4 + pos["z"]) * 2 + core
    ctx = pos["x"] * 2 + lax.rem(pos["y"], 2)
    return (dp, ctx)


def shifted(pos, axis, by):
    return {**pos, axis: lax.rem(pos[axis] + by + 4, 4)}


def ring_devices(pos, core):
    return [device_of(shifted(pos, axis, by), core) for axis in "xyz" for by in (1, -1, 2)]


def greet(pos, core, heads=False):
    barrier = pltpu.get_barrier_semaphore()
    devices = ring_devices(pos, core)
    devices.append(device_of(pos, 1 - core))
    if heads:
        dp, ctx = lax.axis_index("dp"), lax.axis_index("ctx")
        lo = lax.rem(ctx, 2)
        for by in (1, 2, 3):
            devices.append((dp, lax.rem(pos["x"] + by, 4) * 2 + 1 - lo))
    for device in devices:
        pl.semaphore_signal(barrier, inc=1, device_id=device, device_id_type=MESH)
    return lambda: pl.semaphore_wait(barrier, len(devices))


class Sender:
    def __init__(self, send_sem, recv_sem):
        self.send_sem, self.recv_sem, self.started, self.count = send_sem, recv_sem, [], 0

    def __call__(self, src, dst, device):
        i = self.count
        self.count += 1
        copy = pltpu.make_async_remote_copy(src_ref=src, dst_ref=dst, send_sem=self.send_sem.at[i],
                                            recv_sem=self.recv_sem.at[i], device_id=device, device_id_type=MESH)
        copy.start()
        self.started.append(copy)
        return copy

    def finish(self, copies=None):
        for copy in self.started if copies is None else copies:
            copy.wait_send()
        self.started = [] if copies is None else [c for c in self.started if all(c is not d for d in copies)]


ORDERS = {"A": "xyz", "B": "yzx", "C": "zxy"}
LANES = (512, 256, 640, 640)
ROUNDS = [
    [(0, "A", (0, 80), (0, 128)), (0, "B", (0, 80), (128, 256)), (0, "C", (0, 80), (256, 384)),
     (0, "A", (0, 32), (384, 512)), (0, "B", (32, 64), (384, 512)), (0, "C", (64, 80), (384, 512))],
    [(2, "B", (0, 80), (384, 512)), (2, "C", (0, 80), (512, 640)), (1, "B", (0, 80), (0, 128)), (1, "C", (0, 80), (128, 256)),
     (2, "A", (0, 80), (0, 384))],
    [(3, "B", (0, 80), (384, 512)), (3, "C", (0, 80), (512, 640)), (3, "A", (0, 80), (0, 384))],
]


def spans(where):
    out = {}
    for axis in "xz":
        v = where[axis]
        out[axis] = (0, 4) if v is None else ((v[1] * 2, 2) if isinstance(v, tuple) else (v, 1))
    v = where["y"]
    if v is None:
        hi, lo = (0, 2), (0, 2)
    elif isinstance(v, tuple):
        hi, lo = (v[1], 1), (0, 2)
    elif isinstance(v, int):
        hi, lo = (v // 2, 1), (v % 2, 1)
    else:
        hi, lo = (lax.div(v, 2), 1), (lax.rem(v, 2), 1)
    return (hi, out["z"], out["x"], lo)


def span_index(where):
    return tuple(s if n == 1 else pl.ds(s, n) for s, n in spans(where))


def part_slice(part):
    _, _, rows, lanes = part
    return (pl.ds(rows[0], rows[1] - rows[0]), pl.ds(lanes[0], lanes[1] - lanes[0]))


def where_of(pos, part, k, value, half=None):
    order = ORDERS[part[1]]
    where = {}
    for j, axis in enumerate(order):
        where[axis] = None if j < k else (value if j == k else pos[axis])
    if half is not None:
        where[order[k - 1]] = ("half", half)
    return where


class Gather:
    def __init__(self, pos, core, ins, bufs, send):
        self.pos, self.core, self.ins, self.bufs, self.send = pos, core, ins, bufs, send
        self.first, self.second = {}, {}
        self.pushes = {r: [] for r in range(len(ROUNDS))}

    def put(self, part, where, device, src=None):
        ref = self.bufs[part[0]].at[span_index(where) + (self.core,) + part_slice(part)]
        return self.send(ref if src is None else src, ref, device)

    def near(self, axis, by):
        return device_of(shifted(self.pos, axis, by), self.core)

    def partner(self):
        return device_of(self.pos, 1 - self.core)

    def step1(self, k, r):
        for part in ROUNDS[r]:
            axis = ORDERS[part[1]][k]
            where = where_of(self.pos, part, k, self.pos[axis])
            src = self.ins[part[0]].at[part_slice(part)] if k == 0 else None
            self.first[part, k] = tuple(self.put(part, where, self.near(axis, by), src) for by in ((1, -1) if k else (1, -1, 2)))
            if k == 2:
                self.pushes[r].append(self.put(part, where, self.partner()))

    def step2(self, k, r):
        for part in ROUNDS[r]:
            axis = ORDERS[part[1]][k]
            if k == 0:
                self.second[part, k] = self.first[part, k]
                continue
            right, left = self.first[part, k]
            below, above = (shifted(self.pos, axis, by)[axis] for by in (-1, 1))
            right.wait_recv()
            a = self.put(part, where_of(self.pos, part, k, below, 0), self.near(axis, 1))
            left.wait_recv()
            self.second[part, k] = (a, self.put(part, where_of(self.pos, part, k, above, 1), self.near(axis, -1)))
            if k == 2:
                self.pushes[r].append(self.put(part, where_of(self.pos, part, k, below), self.partner()))
                self.pushes[r].append(self.put(part, where_of(self.pos, part, k, above), self.partner()))

    def step3(self, k, r):
        for part in ROUNDS[r]:
            axis = ORDERS[part[1]][k]
            for copy in self.second[part, k]:
                copy.wait_recv()
            if k == 2:
                across = shifted(self.pos, axis, 2)[axis]
                self.pushes[r].append(self.put(part, where_of(self.pos, part, k, across), self.partner()))

    def finish(self, r):
        for copy in self.pushes[r]:
            copy.wait_recv()


class Heads:
    def __init__(self, src, dst, send_sem, recv_sem, local_sem, cut=()):
        self.src, self.dst, self.send_sem, self.recv_sem, self.local_sem, self.cut = src, dst, send_sem, recv_sem, local_sem, cut
        self.dp, self.ctx = lax.axis_index("dp"), lax.axis_index("ctx")

    def copy(self, o, into, arrived):
        return pltpu.make_async_remote_copy(
            src_ref=self.src.at[(o,) + self.cut], dst_ref=self.dst.at[(into,) + self.cut], send_sem=self.send_sem.at[o],
            recv_sem=self.recv_sem.at[arrived], device_id=(self.dp, o), device_id_type=MESH)

    def own(self):
        return pltpu.make_async_copy(self.src.at[(self.ctx,) + self.cut], self.dst.at[(self.ctx,) + self.cut], self.local_sem)

    def start(self, blocks):
        for o in blocks:
            @pl.when(self.ctx == o)
            def _():
                self.own().start()

            @pl.when(self.ctx != o)
            def _():
                self.copy(o, self.ctx, self.ctx).start()

    def wait_recv(self):
        self.own().wait()
        for o in range(8):
            @pl.when(self.ctx != o)
            def _():
                self.copy(o, o, o).wait_recv()

    def wait_send(self):
        for o in range(8):
            @pl.when(self.ctx != o)
            def _():
                self.copy(o, self.ctx, self.ctx).wait_send()


def dot(a, b):
    return jnp.dot(a, b, preferred_element_type=F32)


def dot_nt(a, b):
    return lax.dot_general(a, b, (((1,), (1,)), ((), ())), preferred_element_type=F32)


def dot_tn(a, b):
    return lax.dot_general(a, b, (((0,), (0,)), ((), ())), preferred_element_type=F32)


def turned(a):
    return a.astype(F32).T.astype(a.dtype)


def norm_parts(values):
    center = values - jnp.mean(values, axis=-1, keepdims=True)
    spread = jnp.mean(center * center, axis=-1, keepdims=True)
    r = lax.rsqrt(spread + EPSILON)
    return center * r, r


def norm_back(u, r, gain, e):
    n = e * gain
    dv = r * (n - jnp.mean(n, axis=-1, keepdims=True) - u * jnp.mean(n * u, axis=-1, keepdims=True))
    return dv, jnp.sum(e * u, axis=0, keepdims=True), jnp.sum(e, axis=0, keepdims=True)


VECTOR_ROWS = ((0,), (1,), (2, 3), (4,), (5,), (6,), (8, 9, 10, 11), (7,))


def selector():
    out = np.zeros((1024, 1152), np.float32)
    for m in range(3):
        for j in range(320):
            at = 320 * m + j
            out[(at // 240) * 256 + at % 240, 384 * m + j] = 1
    return out


def place_tables():
    c = np.arange(1280)
    plain = np.stack([c // 10, 0 * c, c % 10])
    c = np.arange(4096)
    off = c % 256
    n = 240 * (c // 256) + off
    e = np.where(n < 1280, n, n - 1280)
    unused = (off >= 240) | ((n >= 1280) & (n < 2560))
    qkv = np.stack([np.where(unused, -1, e // 20), 2 + (e % 20) // 10, e % 10])
    c = np.arange(5120)
    fc = np.stack([c // 40, 8 + (c % 40) // 10, c % 10])
    pad = lambda t: np.concatenate([t, np.zeros((5, t.shape[1]), t.dtype)]).astype(np.int32)
    return pad(plain), pad(qkv), pad(fc)


def vector_tile(flat):
    row = lax.broadcasted_iota(jnp.int32, (16, 128), 0)
    at = lax.broadcasted_iota(jnp.int32, (16, 128), 1)
    rows = jnp.where((at >= 10 * row) & (at < 10 * row + 10), flat[...].astype(F32), 0.0).astype(BF)
    entry = lax.rem(lax.broadcasted_iota(jnp.int32, (128, 128), 0), 10)
    lane = lax.broadcasted_iota(jnp.int32, (128, 128), 1)
    return dot(rows, (lane == 112 + entry).astype(F32).astype(BF)).astype(BF)


def vector_flat(tile):
    row = lax.broadcasted_iota(jnp.int32, (16, 128), 0)
    at = lax.broadcasted_iota(jnp.int32, (16, 128), 1)
    total = jnp.zeros((16, 128), F32)
    for r in range(12):
        hit = (row == r) & (at >= 10 * r) & (at < 10 * r + 10)
        total += jnp.where(hit, pltpu.roll(tile, (10 * r + 16) % 128, 1), 0.0)
    return jnp.sum(total, axis=0, keepdims=True)


def row_owner(core):
    v = lax.broadcasted_iota(jnp.int32, (64, 1), 0)
    return (v // 8) * 16 + core * 8 + lax.rem(v, 8)


def row_picker(r):
    v = lax.broadcasted_iota(jnp.int32, (64, 1024), 0)
    c = lax.broadcasted_iota(jnp.int32, (64, 1024), 1)
    return (c == 16 * v + r).astype(F32).astype(BF)


def entry_picker(entry):
    lane = lax.broadcasted_iota(jnp.int32, (128, entry.shape[1]), 0)
    return (lane == 112 + entry).astype(F32).astype(BF)


def fetched_rows(buf, row_ids):
    tiles = [buf[:, :, :, :, h, 0:16, 256 * h + 128:256 * h + 256].reshape(1024, 128) for h in range(2)]
    return {r: [dot(row_picker(r), tile).astype(BF) for tile in tiles] for r in row_ids}


def take_row(rows, table, row_ids):
    owner, row, entry = table[0:1], table[1:2], table[2:3]
    pick = entry_picker(entry)
    total = jnp.zeros((1, table.shape[1]), F32)
    for h in range(2):
        mine = row_owner(h)
        for r in row_ids:
            hit = (mine == owner) if len(row_ids) == 1 else ((mine == owner) & (row == r))
            total += jnp.sum(jnp.where(hit, dot(rows[r][h], pick), 0.0), axis=0, keepdims=True)
    return total


def unpack_first(buf, plain, qkv, vecs, bias_qkv):
    rows = fetched_rows(buf, range(4))
    for r in (0, 1):
        vecs[r:r + 1] = take_row(rows, plain[...], (r,))
    for p in range(8):
        bias_qkv[p:p + 1] = take_row(rows, qkv[:, 512 * p:512 * p + 512], (2, 3))


def unpack_second(buf, plain, fc, vecs, bias_fc):
    rows = fetched_rows(buf, range(4, 12))
    vecs[2:4] = jnp.zeros((2, 1280), F32)
    for r in (4, 5, 6, 7):
        vecs[r:r + 1] = take_row(rows, plain[...], (r,))
    for p in range(8):
        bias_fc[p:p + 1] = take_row(rows, fc[:, 640 * p:640 * p + 640], (8, 9, 10, 11))


def head_lanes(rows, half):
    lane = lax.broadcasted_iota(jnp.int32, (rows, 128), 1)
    return (lane < 64) if half == 0 else (lane >= 64)


def only(values, half):
    return jnp.where(head_lanes(values.shape[0], half), values, jnp.zeros_like(values))


def swapped(values):
    return pltpu.roll(values.astype(F32), 64, 1).astype(values.dtype)


def tile_of(data, a, b, t):
    return data[a:b, :, 128 * t:128 * t + 128].reshape(128 * (b - a), 128)


def segment_views(data):
    tile = tile_of(data, 0, 8, 7).astype(F32)
    return tile[:, 64:65], jnp.transpose(tile)[64:65, :]


def mask_of(column, row, i, wide):
    rows = lax.broadcasted_iota(jnp.int32, (256, wide), 0) + 256 * i
    cols = lax.broadcasted_iota(jnp.int32, (256, wide), 1)
    keep = (cols <= rows) & (column[256 * i:256 * i + 256] == row[:, :wide])
    return jnp.where(keep, 0.0, MASKED_VALUE)


def head_tiles(data, i, j):
    n = 2 * i + 2
    if j < 2:
        return tile_of(data, 2 * i, n, j), tile_of(data, 0, n, 2 + j), tile_of(data, 0, n, 4 + j)
    return tile_of(data, 2 * i, n, 6), swapped(tile_of(data, 0, n, 6)), tile_of(data, 0, n, 7)


def attend_block(data, mixed, column, row, i):
    wide = 256 * (i + 1)
    hide = mask_of(column, row, i, wide)
    for j in range(3):
        q, k, v = head_tiles(data, i, j)
        total = None
        for half in range(2 if j < 2 else 1):
            scores = dot_nt(only(q, half) * jnp.asarray(0.125, BF), k) + hide
            e = jnp.exp(scores - jnp.max(scores, axis=-1, keepdims=True))
            soft = (e / jnp.sum(e, axis=-1, keepdims=True)).astype(BF)
            part = dot(soft, only(v, half))
            total = part if total is None else total + part
        mixed[2 * i:2 * i + 2, :, 128 * j:128 * j + 128] = total.astype(BF).reshape(2, 128, 128)


def front_kernel(kept, got, flat, tokens, seg, select, plain, qkv_table, fc_table,
                 qkv_all, out_all, fc_all, pj_all, normed, data_all, mixed_all, vecs, bias_fc,
                 qkv, bias_qkv, packed, sent, data, mixed_sent, mixed, send_sem, recv_sem, local_sem,
                 heads_send, heads_recv, heads_local, qkv_in, out_in, fc_in, pj_in):
    pos, core = coords()
    send = Sender(send_sem, recv_sem)
    here = tuple(s for s, _ in spans(pos)) + (core,)
    tile = vector_tile(flat)
    for which, (one, two) in enumerate(((kept, got), (got, kept))):
        @pl.when(core == which)
        def _():
            qkv_in[...] = jnp.concatenate([one[:, 640:896], two[:, 640:896]], axis=1)
            out_in[...] = jnp.concatenate([one[:, 896:976], two[:, 896:976], jnp.zeros((80, 96), BF)], axis=1)
            fc_in[...] = jnp.concatenate([one[:, 0:320], two[:, 0:320]], axis=1)
            pj_in[...] = jnp.concatenate([one[:, 320:640], two[:, 320:640]], axis=1)
            own = slice(256 * which + 128, 256 * which + 256)
            qkv_in[0:16, own] = qkv_in[0:16, own] + tile

    local = [pltpu.make_async_copy(src, dst.at[here], local_sem.at[n])
             for n, (src, dst) in enumerate([(qkv_in, qkv), (out_in, out_all), (fc_in, fc_all), (pj_in, pj_all)])]
    for copy in local:
        copy.start()
    greet(pos, core, heads=True)()
    g = Gather(pos, core, (qkv_in, out_in, fc_in, pj_in), (qkv, out_all, fc_all, pj_all), send)
    g.step1(0, 0)
    g.step1(0, 1)
    g.step1(0, 2)
    for copy in local:
        copy.wait()
    g.step2(0, 0)
    g.step3(0, 0)
    g.step1(1, 0)
    g.step2(0, 1)
    g.step2(0, 2)
    g.step2(1, 0)
    g.step3(0, 1)
    g.step1(1, 1)
    g.step3(1, 0)
    g.step1(2, 0)
    g.step3(0, 2)
    g.step1(1, 2)
    g.step2(1, 1)
    g.step2(1, 2)
    g.step2(2, 0)
    g.step3(1, 1)
    g.step1(2, 1)
    u, _ = norm_parts(tokens[...].astype(F32))
    g.step3(2, 0)
    g.step3(1, 2)
    g.finish(0)

    keep = pltpu.make_async_copy(qkv, qkv_all, local_sem.at[0])
    keep.start()
    unpack_first(qkv, plain, qkv_table, vecs, bias_qkv)
    normed[...] = (u * vecs[0:1] + vecs[1:2]).astype(BF)

    def project(p, carry):
        w = qkv[lax.div(p, 4), lax.rem(p, 4)].reshape(1280, 512)
        packed[p] = (dot(normed[...], w) + bias_qkv[pl.ds(p, 1)]).astype(BF)
        return carry

    def select_three(i):
        wide = jnp.concatenate([packed[2 * i], packed[2 * i + 1]], axis=1)
        chunks = dot(wide, select[...])
        for m in range(3):
            n = 3 * i + m
            kind, group = n // 4, n % 4
            low = chunks[:, 384 * m:384 * m + 256].astype(BF)
            last = chunks[:, 384 * m + 256:384 * m + 384]
            if kind == 1:
                last = pltpu.roll(last, 64, 1)
            last = last.astype(BF)
            for s in range(2):
                at = s * 4 + group
                rows = slice(128 * s, 128 * s + 128)
                sent[at, :, 256 * kind:256 * kind + 256] = low[rows]
                if kind == 0:
                    sent[at, :, 768:896] = last[rows]
                elif kind == 1:
                    sent[at, :, 768:896] = sent[at, :, 768:896] + last[rows]
                else:
                    sent[at, :, 896:1024] = last[rows] + seg[rows]

    pieces = [Heads(sent, data, heads_send.at[n], heads_recv.at[n], heads_local.at[n], (slice(None), pl.ds(a, b - a)))
              for n, (a, b) in enumerate(((0, 256), (256, 512), (512, 1024)))]
    lax.fori_loop(0, 4, project, 0)
    select_three(0)
    select_three(1)
    pieces[0].start(range(8))
    lax.fori_loop(4, 6, project, 0)
    select_three(2)
    pieces[1].start(range(8))
    lax.fori_loop(6, 8, project, 0)
    select_three(3)
    pieces[2].start(range(8))
    g.step1(2, 2)
    g.step2(2, 1)
    unpack_second(qkv, plain, fc_table, vecs, bias_fc)
    for piece in pieces:
        piece.wait_recv()
    keep_data = pltpu.make_async_copy(data, data_all, local_sem.at[1])
    keep_data.start()
    column, row = segment_views(data)
    back = Heads(mixed_sent, mixed, heads_send.at[3], heads_recv.at[3], heads_local.at[3])
    for i in range(4):
        attend_block(data, mixed_sent, column, row, i)
        back.start((2 * i, 2 * i + 1))
        if i == 1:
            g.step2(2, 2)
    g.step3(2, 1)
    back.wait_recv()
    keep_mixed = pltpu.make_async_copy(mixed, mixed_all, local_sem.at[2])
    keep_mixed.start()
    g.step3(2, 2)
    g.finish(1)
    g.finish(2)
    keep.wait()
    keep_data.wait()
    keep_mixed.wait()
    for piece in pieces:
        piece.wait_send()
    back.wait_send()
    send.finish()


FRONT_SENDS = 15 * sum(len(r) for r in ROUNDS)


def front(kept, got, flat, tokens, seg, select, plain, qkv_table, fc_table):
    sds = jax.ShapeDtypeStruct
    whole = pl.BlockSpec(memory_space=pl.ANY)
    near = pl.BlockSpec(memory_space=VMEM)
    return pl.pallas_call(
        front_kernel,
        out_shape=[sds((2, 4, 4, 2, 2, 80, n), BF) for n in LANES] + [
            sds((256, 1280), BF), sds((8, 128, 1024), BF), sds((8, 128, 384), BF), sds((8, 1280), F32), sds((8, 640), F32)],
        in_specs=[near] * 9,
        out_specs=[whole] * 4 + [near, whole, whole, near, near],
        scratch_shapes=[
            VMEM((2, 4, 4, 2, 2, 80, 512), BF), VMEM((8, 512), F32), VMEM((8, 256, 512), BF), VMEM((8, 128, 1024), BF),
            VMEM((8, 128, 1024), BF), VMEM((8, 128, 384), BF), VMEM((8, 128, 384), BF),
            pltpu.SemaphoreType.DMA((FRONT_SENDS,)), pltpu.SemaphoreType.DMA((FRONT_SENDS,)), pltpu.SemaphoreType.DMA((4,)),
            pltpu.SemaphoreType.DMA((4, 8)), pltpu.SemaphoreType.DMA((4, 8)), pltpu.SemaphoreType.DMA((4,)),
            VMEM((80, 512), BF), VMEM((80, 256), BF), VMEM((80, 640), BF), VMEM((80, 640), BF),
        ],
        compiler_params=pltpu.CompilerParams(collective_id=0, has_side_effects=True, vmem_limit_bytes=60 * MIB),
        name="fetch_and_attend",
    )(kept, got, flat, tokens, seg, select, plain, qkv_table, fc_table)


def attend_back_block(data, grad, out, dk, dv, column, row, i):
    wide = 256 * (i + 1)
    hide = mask_of(column, row, i, wide)
    for j in range(3):
        q, k, v = head_tiles(data, i, j)
        q = q * jnp.asarray(0.125, BF)
        lanes = slice(128 * j, 128 * j + 128)
        g = grad[2 * i:2 * i + 2, :, lanes].reshape(256, 128)
        total = None
        for half in range(2 if j < 2 else 1):
            qh, gh = only(q, half), only(g, half)
            scores = dot_nt(qh, k) + hide
            e = jnp.exp(scores - jnp.max(scores, axis=-1, keepdims=True))
            soft = e / jnp.sum(e, axis=-1, keepdims=True)
            dv[0:wide, lanes] += dot_tn(soft.astype(BF), gh)
            sg = dot_nt(gh, v)
            sg = (soft * (sg - jnp.sum(soft * sg, axis=-1, keepdims=True))).astype(BF)
            dk[0:wide, lanes] += dot_tn(sg, qh)
            part = dot(sg, only(k, half)) * 0.125
            total = part if total is None else total + part
        t = j if j < 2 else 6
        out[2 * i:2 * i + 2, :, 128 * t:128 * t + 128] = total.astype(BF).reshape(2, 128, 128)


def attend_back_end(out, dk, dv, i):
    rows, blocks = slice(256 * i, 256 * i + 256), slice(2 * i, 2 * i + 2)
    for j in range(2):
        lanes = slice(128 * j, 128 * j + 128)
        out[blocks, :, 256 + 128 * j:384 + 128 * j] = dk[rows, lanes].astype(BF).reshape(2, 128, 128)
        out[blocks, :, 512 + 128 * j:640 + 128 * j] = dv[rows, lanes].astype(BF).reshape(2, 128, 128)
    last = pltpu.roll(dk[rows, 256:384], 64, 1).astype(BF).reshape(2, 128, 128)
    out[blocks, :, 768:896] = out[blocks, :, 768:896] + last
    out[blocks, :, 896:1024] = dv[rows, 256:384].astype(BF).reshape(2, 128, 128)


class Scatter:
    def __init__(self, pos, core, sums, slots, outs, send, rounds, base=None):
        self.base = base or {}
        self.pos, self.core, self.sums, self.slots, self.outs, self.send = pos, core, sums, slots, outs, send
        self.rounds, self.first, self.second = rounds, {}, {}

    def near(self, axis, by):
        return device_of(shifted(self.pos, axis, by), self.core)

    def slot_of(self, part, k, slot, half=None):
        order = ORDERS[part[1]]
        where = {}
        for j, axis in enumerate(order):
            where[axis] = None if j < k else (slot if j == k else 3)
        if half is not None:
            where[order[k - 1]] = ("half", half)
        return where

    def sum_at(self, t, idx):
        ref, halves = self.sums[t]
        return ref, (idx + (self.core,) if halves else idx)

    def cut(self, part):
        base = self.base.get(part[0], 0)
        return part_slice((part[0], part[1], part[2], (part[3][0] - base, part[3][1] - base)))

    def sum_view(self, part, where):
        ref, idx = self.sum_at(part[0], span_index(where))
        return ref.at[idx + self.cut(part)]

    def slot_view(self, part, where):
        return self.slots[part[0]].at[span_index(where) + self.cut(part)]

    def add_slot(self, part, where, slot):
        ref, idx = self.sum_at(part[0], span_index(where))
        here = idx + self.cut(part)
        ref[here] = ref[here] + self.slots[part[0]][span_index(slot) + self.cut(part)]

    def step1(self, k, r):
        for part in self.rounds[r]:
            axis = ORDERS[part[1]][k]
            across = shifted(self.pos, axis, 2)[axis]

            def out(half, by):
                return self.send(self.sum_view(part, where_of(self.pos, part, k, across, half)),
                                 self.slot_view(part, self.slot_of(part, k, 0, half)), self.near(axis, by))

            def straight(slot, by):
                return self.send(self.sum_view(part, where_of(self.pos, part, k, shifted(self.pos, axis, by)[axis])),
                                 self.slot_view(part, self.slot_of(part, k, slot)), self.near(axis, by))

            if k == 0:
                self.second[part, k] = (straight(0, 2), straight(1, 1), straight(2, -1))
            else:
                self.first[part, k] = (out(0, 1), out(1, -1))

    def step2(self, k, r):
        for part in self.rounds[r] if k else ():
            axis = ORDERS[part[1]][k]
            above, below = (shifted(self.pos, axis, by)[axis] for by in (1, -1))
            first = self.first[part, k]
            first[0].wait_recv()
            self.add_slot(part, where_of(self.pos, part, k, above, 0), self.slot_of(part, k, 0, 0))
            a = self.send(self.sum_view(part, where_of(self.pos, part, k, above)),
                          self.slot_view(part, self.slot_of(part, k, 1)), self.near(axis, 1))
            first[1].wait_recv()
            self.add_slot(part, where_of(self.pos, part, k, below, 1), self.slot_of(part, k, 0, 1))
            b = self.send(self.sum_view(part, where_of(self.pos, part, k, below)),
                          self.slot_view(part, self.slot_of(part, k, 2)), self.near(axis, -1))
            self.second[part, k] = (a, b)

    def copies_of(self, t, r):
        return [c for part in self.rounds[r] if part[0] == t for k in range(3) for held in (self.first, self.second)
                for c in held.get((part, k), ())]

    def step3(self, k, r):
        for part in self.rounds[r]:
            t = part[0]
            axis = ORDERS[part[1]][k]
            for copy in self.second[part, k]:
                copy.wait_recv()
            cut = self.cut(part)
            ref, idx = self.sum_at(t, span_index(where_of(self.pos, part, k, self.pos[axis])))
            slots = self.slots[t]
            total = (ref[idx + cut].astype(F32) + slots[span_index(self.slot_of(part, k, 1)) + cut].astype(F32)
                     + slots[span_index(self.slot_of(part, k, 2)) + cut].astype(F32))
            if k == 0:
                self.outs[t][part_slice(part)] = total + slots[span_index(self.slot_of(part, k, 0)) + cut].astype(F32)
            else:
                ref[idx + cut] = total.astype(BF)


class Pairs:
    def __init__(self, scatter, grads, stages, stage_sem, order):
        self.s, self.grads, self.stages, self.stage_sem, self.order = scatter, grads, stages, stage_sem, order
        self.pushed, self.loads = {}, {}

    def where(self, part, which):
        axis = ORDERS[part[1]][2]
        return where_of(self.s.pos, part, 2, shifted(self.s.pos, axis, which)[axis])

    def stage_names(self, r):
        seen = {}
        for part in self.s.rounds[r]:
            n = seen.get(part[1], 0)
            seen[part[1]] = n + 1
            yield part, part[1] + str(n)

    def push_all(self):
        s = self.s
        for r, which in self.order:
            for part in s.rounds[r]:
                where = self.where(part, which)
                src = self.grads[part[0]].at[span_index(where) + (1 - s.core,) + part_slice(part)]
                self.pushed[part, which] = s.send(src, s.sum_view(part, where), device_of(s.pos, 1 - s.core))

    def load(self, n):
        if n >= len(self.order):
            return
        r, which = self.order[n]
        for j, (part, name) in enumerate(self.stage_names(r)):
            src = self.grads[part[0]].at[span_index(self.where(part, which)) + (self.s.core,) + part_slice(part)]
            dst = self.stages[name].at[n % 2].at[..., pl.ds(0, part[2][1] - part[2][0]), pl.ds(0, part[3][1] - part[3][0])]
            copy = pltpu.make_async_copy(src, dst, self.stage_sem.at[n % 2, j])
            copy.start()
            self.loads[n, part] = copy

    def add(self, n):
        r, which = self.order[n]
        s = self.s
        for part, name in self.stage_names(r):
            self.loads[n, part].wait()
            self.pushed[part, which].wait_recv()
            where = self.where(part, which)
            ref, idx = s.sum_at(part[0], span_index(where))
            here = idx + s.cut(part)
            stage = self.stages[name].at[n % 2]
            ref[here] = ref[here] + stage[..., pl.ds(0, part[2][1] - part[2][0]), pl.ds(0, part[3][1] - part[3][0])]
        self.load(n + 2)


def pack_vectors(plain, qkv, fc, d_pre, d_bias_qkv, d_mid, d_bias_fc):
    out = []
    for h in range(2):
        mine = row_owner(h)
        rows = {}

        def give(table, values, row_ids):
            owner, row, entry = table[0:1], table[1:2], table[2:3]
            pick = entry_picker(entry)
            low = values.astype(BF).astype(F32)
            for r in row_ids:
                hit = (mine == owner) if len(row_ids) == 1 else ((mine == owner) & (row == r))
                part = dot_nt(jnp.where(hit, low, 0.0).astype(BF), pick)
                rows[r] = rows[r] + part if r in rows else part

        for r, values in ((0, d_pre[0]), (1, d_pre[1]), (4, d_mid[0:1]), (5, d_mid[1:2]), (6, d_mid[2:3]), (7, d_mid[3:4])):
            give(plain[...], values, (r,))
        for p in range(8):
            give(qkv[:, 512 * p:512 * p + 512], d_bias_qkv[p:p + 1], (2, 3))
            give(fc[:, 640 * p:640 * p + 640], d_bias_fc[p:p + 1], (8, 9, 10, 11))
        total = jnp.zeros((1024, 128), F32)
        for r in range(12):
            total += dot_tn(row_picker(r), rows[r].astype(BF))
        out.append(total.astype(BF))
    return out


BACK_ROUNDS = {
    1: [(2, "A", (0, 80), (0, 384)), (2, "B", (0, 80), (384, 512)), (2, "C", (0, 80), (512, 640)), (1, "B", (0, 80), (0, 128))],
    2: [(3, "A", (0, 80), (0, 384)), (3, "B", (0, 80), (384, 512)), (3, "C", (0, 80), (512, 640)), (1, "C", (0, 80), (128, 256))],
}
VECTOR_ROUND = [(4, "A", (0, 16), (0, 128))]
BACK_ORDER = [(1, 2), (2, 2), (1, 1), (1, -1), (2, 1), (2, -1), (1, 0), (2, 0)]
STAGES = {"A0": (2, 4, 2, 80, 384), "B0": (2, 4, 2, 80, 128), "B1": (2, 4, 2, 80, 128), "C0": (4, 4, 80, 128),
          "C1": (4, 4, 80, 128)}


def spread_columns(grads, packed):
    for i in range(4):
        chunks = []
        for m in range(3):
            n = 3 * i + m
            kind, group = n // 4, n % 4
            last = (768, 832, 896)[kind]
            pair = [jnp.concatenate([grads[at, :, 256 * kind:256 * kind + 256], grads[at, :, last:last + 64]], axis=1)
                    for at in (group, 4 + group)]
            chunks.append(jnp.concatenate(pair, axis=0))
        wide = jnp.concatenate(chunks, axis=1)
        blank = jnp.zeros((256, 16), BF)
        for m in range(2):
            both = jnp.concatenate([wide[:, 480 * m:480 * m + 240], blank, wide[:, 480 * m + 240:480 * m + 480], blank], axis=1)
            packed[2 * i + m, :, 0:512] = both[0:128]
            packed[2 * i + m, :, 512:1024] = both[128:256]


def rows_of(packed, p):
    return jnp.concatenate([packed[p, :, 0:512], packed[p, :, 512:1024]], axis=0)


def back_kernel(d_out, d_fc, d_pj, mixed_grad, data, tokens, middle_grad, vecs, normed, w_all, plain, qkv_table, fc_table,
                d_mid, d_bias_fc, kept, given, input_grad, flat,
                sum_out, sum_fc, sum_pj, slot_out, slot_fc, slot_pj, *rest):
    stages = dict(zip(sorted(STAGES), rest[:5]))
    (grad, sent, grads, dk, dv, nt, nt_other, packed_other, w, d_bias, d_vec, got_vec, slot_vec, send_sem, recv_sem, stage_sem, heads_send,
     heads_recv, heads_local, w_sem, mg_sem, free_sem, s_out, s_fc, s_pj, s_qkv,
     s_vec) = rest[5:]
    pos, core = coords()
    partner = device_of(pos, 1 - core)
    send = Sender(send_sem, recv_sem)
    s = Scatter(pos, core, {0: (sum_fc, False), 1: (sum_out, False), 2: (sum_fc, False), 3: (sum_pj, False), 4: (d_vec, True)},
                {0: slot_fc, 1: slot_out, 2: slot_fc, 3: slot_pj, 4: slot_vec},
                {0: s_qkv, 1: s_out, 2: s_fc, 3: s_pj, 4: s_vec}, send, {**BACK_ROUNDS, 0: ROUNDS[0], 4: VECTOR_ROUND})
    pairs = Pairs(s, {1: d_out, 2: d_fc, 3: d_pj}, stages, stage_sem, BACK_ORDER)
    pairs.load(0)
    pairs.load(1)
    bring = pltpu.make_async_copy(middle_grad, input_grad, mg_sem.at[0])
    bring.start()

    def fetch(n):
        copy = pltpu.make_async_copy(w_all.at[n // 8, n // 2 % 4, pl.ds(n % 2 * 2, 2)], w.at[n % 2], w_sem.at[n % 2])
        copy.start()
        return copy

    loads = {0: fetch(0), 1: fetch(1)}
    others_here = greet(pos, core, heads=True)
    nt[...] = turned(normed[...]).reshape(8, 2, 80, 256)
    others_here()
    first = Heads(mixed_grad, grad, heads_send.at[0], heads_recv.at[0], heads_local.at[0])
    second = Heads(sent, grads, heads_send.at[1], heads_recv.at[1], heads_local.at[1])
    first.start(range(8))
    pairs.push_all()
    push_nt = send(nt.at[:, 1 - core], nt_other, partner)
    dk[...] = jnp.zeros_like(dk)
    dv[...] = jnp.zeros_like(dv)
    column, row = segment_views(data)

    def attend_step(i):
        attend_back_block(data, grad, sent, dk, dv, column, row, i)
        attend_back_end(sent, dk, dv, i)
        second.start((2 * i, 2 * i + 1))

    pairs.add(0)
    s.step1(2, 1)
    pairs.add(1)
    s.step1(2, 2)
    first.wait_recv()
    attend_step(3)
    pairs.add(2)
    pairs.add(3)
    s.step2(2, 1)
    attend_step(2)
    pairs.add(4)
    pairs.add(5)
    s.step2(2, 2)
    attend_step(1)
    attend_step(0)
    pairs.add(6)
    s.step3(2, 1)
    s.step1(1, 1)
    pairs.add(7)
    second.wait_recv()
    second.wait_send()
    packed = sent
    spread_columns(grads, packed)
    push_packed = send(packed, packed_other, partner)
    s.step2(1, 1)
    total = [jnp.zeros((256, 640), F32), jnp.zeros((256, 640), F32)]

    def back_through(p):
        mine = rows_of(packed, p)
        for half in range(2):
            n = 2 * p + half
            loads[n].wait()
            total[half] += dot_nt(mine, w[half].reshape(640, 512))
            if n + 2 < 16:
                loads[n + 2] = fetch(n + 2)
        d_bias[p:p + 1] = jnp.sum(mine.astype(F32), axis=0, keepdims=True)

    for p in range(3):
        back_through(p)
    s.step3(1, 1)
    s.step1(0, 1)
    for p in range(3, 6):
        back_through(p)
    s.step3(0, 1)
    send.finish(s.copies_of(2, 1))
    for device in ring_devices(pos, core):
        pl.semaphore_signal(free_sem, inc=1, device_id=device, device_id_type=MESH)
    s.step3(2, 2)
    s.step1(1, 2)
    for p in range(6, 8):
        back_through(p)
    push_nt.wait_recv()
    push_packed.wait_recv()

    def weight_grad(p):
        both = dot(nt[:, core].reshape(640, 256), rows_of(packed, p)) + dot(nt_other[...].reshape(640, 256), rows_of(packed_other, p))
        sum_fc[p // 4, p % 4, :, :, :, 0:512] = both.astype(BF).reshape(4, 2, 80, 512)

    for p in range(4):
        weight_grad(p)
    s.step2(1, 2)
    for p in range(4, 8):
        weight_grad(p)
    pl.semaphore_wait(free_sem, 9)
    s.step1(2, 0)
    s.step3(1, 2)
    s.step1(0, 2)
    u, r = norm_parts(tokens[...].astype(F32))
    back, dg, db = norm_back(u, r, vecs[0:1], jnp.concatenate(total, axis=1))
    bring.wait()
    input_grad[...] = input_grad[...] + back
    s.step2(2, 0)
    for h, part in enumerate(pack_vectors(plain, qkv_table, fc_table, (dg, db), d_bias, d_mid, d_bias_fc)):
        d_vec[:, :, :, :, h] = part.reshape(2, 4, 4, 2, 16, 128)
    push = send(d_vec.at[:, :, :, :, 1 - core], got_vec, partner)
    s.step3(0, 2)
    s.step3(2, 0)
    s.step1(1, 0)
    push.wait_recv()
    d_vec[:, :, :, :, core] = d_vec[:, :, :, :, core] + got_vec[...]
    s.step1(2, 4)
    s.step2(1, 0)
    s.step2(2, 4)
    s.step3(2, 4)
    s.step1(1, 4)
    s.step3(1, 0)
    s.step1(0, 0)
    s.step2(1, 4)
    s.step3(1, 4)
    s.step1(0, 4)
    s.step3(0, 0)
    for c in range(2):
        mine = jnp.concatenate([s_fc[:, 320 * c:320 * c + 320], s_pj[:, 320 * c:320 * c + 320],
                                s_qkv[:, 256 * c:256 * c + 240], s_out[:, 80 * c:80 * c + 80]], axis=1)

        @pl.when(core == c)
        def _():
            kept[...] = mine

        @pl.when(core != c)
        def _():
            given[...] = mine

    s.step3(0, 4)
    flat[...] = vector_flat(s_vec[...])
    first.wait_send()
    send.finish()


BACK_SENDS = 3 + sum(15 * len(r) for r in BACK_ROUNDS.values()) + 11 * (len(ROUNDS[0]) + 1)


def back(d_out, d_fc, d_pj, mixed_grad, data, tokens, middle_grad, vecs, normed, w_all, plain, qkv_table, fc_table, d_mid,
         d_bias_fc):
    sds = jax.ShapeDtypeStruct
    whole = pl.BlockSpec(memory_space=pl.ANY)
    near = pl.BlockSpec(memory_space=VMEM)
    dma = pltpu.SemaphoreType.DMA
    big = [VMEM((2, 4, 4, 2, 80, n), BF) for n in LANES[1:]]
    return pl.pallas_call(
        back_kernel,
        out_shape=[sds((80, 960), F32), sds((80, 960), F32), sds((256, 1280), F32), sds((1, 128), F32)],
        in_specs=[whole] * 4 + [near] * 2 + [whole] + [near] * 2 + [whole] + [near] * 5,
        out_specs=[near] * 4,
        scratch_shapes=big + big + [VMEM((2,) + STAGES[n], BF) for n in sorted(STAGES)] + [
            VMEM((8, 128, 384), BF), VMEM((8, 128, 1024), BF), VMEM((8, 128, 1024), BF),
            VMEM((1024, 384), F32), VMEM((1024, 384), F32), VMEM((8, 2, 80, 256), BF), VMEM((8, 80, 256), BF),
            VMEM((8, 128, 1024), BF), VMEM((2, 2, 2, 2, 80, 512), BF), VMEM((8, 512), F32),
            VMEM((2, 4, 4, 2, 2, 16, 128), BF), VMEM((2, 4, 4, 2, 16, 128), BF), VMEM((2, 4, 4, 2, 16, 128), BF),
            dma((BACK_SENDS,)), dma((BACK_SENDS,)), dma((2, 5)), dma((2, 8)), dma((2, 8)), dma((2,)),
            dma((2,)), dma((1,)), pltpu.SemaphoreType.REGULAR,
        ] + [VMEM((80, n), F32) for n in LANES[1:] + LANES[:1]] + [VMEM((16, 128), F32)],
        compiler_params=pltpu.CompilerParams(collective_id=1, has_side_effects=True, vmem_limit_bytes=63 * MIB),
        name="attend_back_and_scatter",
    )(d_out, d_fc, d_pj, mixed_grad, data, tokens, middle_grad, vecs, normed, w_all, plain, qkv_table, fc_table, d_mid, d_bias_fc)


GELU_A = 0.7978845608028654
GELU_B = 0.044715


def joined(mixed, s):
    return jnp.concatenate([mixed[4 * s + g, :, 0:320] for g in range(4)], axis=1)


def feed_kernel(tokens, cotangent, mixed, w_out, vecs, fc, pj, bias_fc,
                block_out, middle_grad, mixed_grad, d_fc, d_pj, d_out, d_bias_fc, d_vec,
                middle, a2, a2_t, bg_t, mixed_t, out_sum, a2_sum):
    p = pl.program_id(0)

    @pl.when(p == 0)
    def _():
        rows = jnp.concatenate([joined(mixed, 0), joined(mixed, 1)], axis=0)
        mixed_t[...] = turned(rows)
        parts = [dot(rows, w_out[n])[:, 0:160] for n in range(8)]
        total = tokens[...].astype(F32) + (jnp.concatenate(parts, axis=1) + vecs[4:5])
        middle[...] = total
        u, _ = norm_parts(total)
        low = (u * vecs[5:6] + vecs[6:7]).astype(BF)
        a2[...] = low
        a2_t[...] = turned(low)
        bg_t[...] = turned(cotangent[...])
        out_sum[...] = jnp.zeros_like(out_sum)
        a2_sum[...] = jnp.zeros_like(a2_sum)

    pre = dot(a2[...], fc[0]) + bias_fc[pl.ds(p, 1)]
    square = pre * pre
    t = jnp.tanh(GELU_A * (pre + GELU_B * pre * square))
    act = (0.5 * pre * (1.0 + t)).astype(BF)
    slope = 0.5 * (1.0 + t) + 0.5 * pre * (1.0 - t * t) * (GELU_A * (1.0 + 3.0 * GELU_B * square))
    out_sum[...] += dot_nt(act, pj[0])
    d_pj[0] = dot(bg_t[...], act).astype(BF)
    pre_grad = (slope * dot(cotangent[...], pj[0])).astype(BF)
    d_bias_fc[pl.ds(p, 1)] = jnp.sum(pre_grad.astype(F32), axis=0, keepdims=True)
    d_fc[0] = dot(a2_t[...], pre_grad).astype(BF)
    a2_sum[...] += dot_nt(pre_grad, fc[0])

    @pl.when(p == 7)
    def _():
        block_out[...] = (middle[...] + (out_sum[...] + vecs[7:8])).astype(BF)
        u, r = norm_parts(middle[...])
        dv, dg, db = norm_back(u, r, vecs[5:6], a2_sum[...])
        c = cotangent[...].astype(F32)
        total = c + dv
        middle_grad[...] = total
        low = total.astype(BF)
        d_vec[0:1] = jnp.sum(low.astype(F32), axis=0, keepdims=True)
        d_vec[1:2] = dg
        d_vec[2:3] = db
        d_vec[3:4] = jnp.sum(c, axis=0, keepdims=True)
        back_sum = jnp.zeros((256, 1280), F32)
        for n in range(8):
            mine = jnp.concatenate([low[:, 160 * n:160 * n + 160], jnp.zeros((256, 96), BF)], axis=1)
            d_out[n] = dot(mixed_t[...], mine).astype(BF)
            back_sum += dot_nt(mine, w_out[n])
        back_low = back_sum.astype(BF)
        for g in range(4):
            rows = jnp.concatenate([back_low[:, 320 * g:320 * g + 320], jnp.zeros((256, 64), BF)], axis=1)
            for s in range(2):
                mixed_grad[s * 4 + g] = rows[s * 128:(s + 1) * 128]


def feed(tokens, cotangent, mixed, w_out, vecs, fc, pj, bias_fc):
    full = lambda *shape: pl.BlockSpec(shape, lambda p: (0,) * len(shape))
    step = lambda *shape: pl.BlockSpec((1,) + shape, lambda p: (p,) + (0,) * len(shape))
    sds = jax.ShapeDtypeStruct
    return pl.pallas_call(
        feed_kernel,
        grid=(8,),
        in_specs=[full(256, 1280), full(256, 1280), full(8, 128, 384), full(8, 1280, 256), full(8, 1280),
                  step(1280, 640), step(1280, 640), full(8, 640)],
        out_specs=[full(256, 1280), full(256, 1280), full(8, 128, 384), step(1280, 640), step(1280, 640),
                   full(8, 1280, 256), full(8, 640), full(4, 1280)],
        out_shape=[sds((256, 1280), BF), sds((256, 1280), F32), sds((8, 128, 384), BF), sds((8, 1280, 640), BF),
                   sds((8, 1280, 640), BF), sds((8, 1280, 256), BF), sds((8, 640), F32), sds((4, 1280), F32)],
        scratch_shapes=[VMEM((256, 1280), F32), VMEM((256, 1280), BF), VMEM((1280, 256), BF), VMEM((1280, 256), BF),
                        VMEM((1280, 256), BF), VMEM((256, 1280), F32), VMEM((256, 1280), F32)],
        compiler_params=pltpu.CompilerParams(vmem_limit_bytes=60 * MIB),
        name="feed_forward_and_back",
    )(tokens, cotangent, mixed, w_out, vecs, fc, pj, bias_fc)


def body(tokens, segments, cotangent, w_qkv, w_out, w_fc, w_proj, *vectors):
    core = lax.rem(lax.axis_index("dp"), 2)
    pairs = [(i, i ^ 1) for i in range(16)]
    flat = jnp.concatenate([vectors[n] for n in (0, 1, 2, 3, 4, 5, 7, 6)] + [jnp.zeros((8,), BF)]).reshape(1, 128)
    mine = jnp.concatenate([w_fc, w_proj.T, w_qkv, jnp.zeros((160, 16), BF), w_out, jnp.zeros((160, 48), BF)], axis=1)
    mine = mine.reshape(2, 80, 1024)
    kept = lax.dynamic_index_in_dim(mine, core, 0, False)
    got = lax.ppermute(lax.dynamic_index_in_dim(mine, 1 - core, 0, False), "dp", pairs)
    select = jnp.asarray(selector(), BF)
    plain, qkv_table, fc_table = (jnp.asarray(t) for t in place_tables())
    tokens = tokens.reshape(256, 1280)
    cotangent = cotangent.reshape(256, 1280)
    seg = jnp.pad(jnp.broadcast_to(segments.reshape(256, 1).astype(BF), (256, 64)), ((0, 0), (64, 0)))
    qkv, out, fc, pj, normed, data, mixed, vecs, bias_fc = front(kept, got, flat, tokens, seg, select, plain, qkv_table, fc_table)
    (block_out, middle_grad, mixed_grad, d_fc, d_pj, d_out, d_bias_fc, d_mid) = feed(
        tokens, cotangent, mixed, out.reshape(8, 1280, 256), vecs, fc.reshape(8, 1280, 640), pj.reshape(8, 1280, 640), bias_fc)
    shape = (2, 4, 4, 2, 2, 80)
    kept, given, input_grad, flat = back(
        d_out.reshape(shape + (256,)), d_fc.reshape(shape + (640,)), d_pj.reshape(shape + (640,)), mixed_grad, data, tokens,
        middle_grad, vecs, normed, qkv, plain, qkv_table, fc_table, d_mid, d_bias_fc)
    got = lax.ppermute(given, "dp", pairs)
    halves = (jnp.where(core == 0, kept, got), jnp.where(core == 0, got, kept))
    rows = jnp.concatenate(halves, axis=0)
    d_proj = jnp.concatenate([half[:, 320:640].T for half in halves], axis=1)
    flat = flat.reshape(128)
    ends = tuple(flat[10 * ids[0]:10 * ids[-1] + 10] for ids in VECTOR_ROWS)
    return (block_out.reshape(2, 128, 1280), input_grad.reshape(2, 128, 1280), rows[:, 640:880], rows[:, 880:960],
            rows[:, 0:320], d_proj) + ends


def solution(mesh):
    weights = (P("ctx", "dp"), P("ctx", "dp"), P("ctx", "dp"), P("dp", "ctx"))
    vectors = (P(("dp", "ctx")),) * 8
    rows = P("dp", "ctx", None)
    return jax.shard_map(
        body,
        mesh=mesh,
        in_specs=(rows, P("dp", "ctx"), rows) + weights + vectors,
        out_specs=(rows, rows) + weights + vectors,
        check_vma=False,
    )
```
